32 devices in a mesh: dp: 4 (over y, x), fsdp: 8 (over z, core).
Axes of the slice: x: 2, y: 2, z: 4, core: 2. Of those that a mesh axis runs over, the one named last changes fastest.
Arguments:
- tokens: bfloat16 [40960, 512], P(('dp', 'fsdp')), may hold values from -6 to 6
- features: bfloat16 [40960, 512], P(('dp', 'fsdp')), may hold values from -6 to 6
- cameras: int32 [32], P(('dp', 'fsdp')), may hold values from 2 to 4
- cotangent: bfloat16 [40960, 512], P(('dp', 'fsdp')), may hold values from -6 to 6
- w_qkv: bfloat16 [512, 1536], P(('dp', 'fsdp')), may hold values from -0.25 to 0.25
- w_out: bfloat16 [512, 512], P(('dp', 'fsdp')), may hold values from -1 to 1
- w_up: bfloat16 [512, 3200], P(('dp', 'fsdp')), may hold values from -0.25 to 0.25
- w_down: bfloat16 [512, 3200], P(('dp', 'fsdp')), may hold values from -0.109375 to 0.109375
- w_feat: bfloat16 [512, 512], P(('dp', 'fsdp')), may hold values from -0.25 to 0.25
- b_query: float32 [512], replicated, may hold values from -3 to 3
- b_value: float32 [512], replicated, may hold values from -3 to 3
- b_out: float32 [512], replicated, may hold values from -3 to 3
- gain_first: float32 [512], replicated, may hold values from 0.5 to 1.5
- shift_first: float32 [512], replicated, may hold values from -2 to 2
- b_up: float32 [3200], replicated, may hold values from -3 to 3
- b_down: float32 [512], replicated, may hold values from -3 to 3
- gain_second: float32 [512], replicated, may hold values from 0.5 to 1.5
- shift_second: float32 [512], replicated, may hold values from -2 to 2
- b_feat: float32 [512], replicated, may hold values from -3 to 3
Outputs:
- output: bfloat16 [40960, 512], P(('dp', 'fsdp'))
- grad_tokens: bfloat16 [40960, 512], P(('dp', 'fsdp'))
- grad_features: bfloat16 [40960, 512], P(('dp', 'fsdp'))
- grad_w_qkv: float32 [512, 1536], P(('dp', 'fsdp'))
- grad_w_out: float32 [512, 512], P(('dp', 'fsdp'))
- grad_w_up: float32 [512, 3200], P(('dp', 'fsdp'))
- grad_w_down: float32 [512, 3200], P(('dp', 'fsdp'))
- grad_w_feat: float32 [512, 512], P(('dp', 'fsdp'))
- grad_b_query: float32 [512], replicated
- grad_b_value: float32 [512], replicated
- grad_b_out: float32 [512], replicated
- grad_gain_first: float32 [512], replicated
- grad_shift_first: float32 [512], replicated
- grad_b_up: float32 [3200], replicated
- grad_b_down: float32 [512], replicated
- grad_gain_second: float32 [512], replicated
- grad_shift_second: float32 [512], replicated
- grad_b_feat: float32 [512], replicated
The draws below stay inside these ranges and needn't reach their ends.
Inputs may be any that keep to these rules, and one draw needn't show every extreme that they name: Each episode's number of cameras.
All inputs are finite; a program needn't handle non-finite values.
Results may differ from the reference program's by a relative error of at most 0.018.
The reference program's roundings to bfloat16 on the way count: a program that leaves them out, or rounds other values in their place, can miss the bound.
Values may be sent and summed in bfloat16 or wider, within the bound.
A program may use at most 320 MiB of HBM per device.

```python
import jax
import jax.numpy as jnp
from jax import lax

D = 512
HEADS = 8
HEAD = 64
FF = 3200
C = 512
SLOTS = 1280
CAM_LEN = 300
EPISODES = 32
TOKENS = 40960


def place_ends(values, stream_key, low, top_value):
    longest = values.shape.index(max(values.shape))
    spots = []
    for shift in (0, 1):
        where = [jax.random.randint(jax.random.fold_in(stream_key, axis), (), 0, length) for axis, length in enumerate(values.shape)]
        where[longest] = (where[longest] + shift) % values.shape[longest]
        spots.append(tuple(where))
    return values.at[spots[0]].set(low).at[spots[1]].set(top_value)


def levels(own_key, shape, pieces, smallest, top_value):
    level, own = 1.0, jax.random.fold_in(own_key, 6)
    for axis_at, shards_of in pieces:
        heights = jnp.exp(jax.random.uniform(jax.random.fold_in(own, axis_at), (shards_of,), jnp.float32, smallest / len(pieces), top_value / len(pieces)))
        level = level * jnp.repeat(heights, shape[axis_at] // shards_of).reshape([-1 if axis == axis_at else 1 for axis in range(len(shape))])
    return level


def noise(own_key, dims, deviation, most, pieces=(), held_as=jnp.bfloat16):
    factor_of = levels(own_key, dims, pieces, -0.22, 0.18) if pieces else 1.0
    entries = jax.random.normal(own_key, dims, jnp.float32) * deviation * factor_of
    return jnp.minimum(jnp.maximum(entries, -most), most).astype(held_as)


def setup_inputs(seed: int = 0) -> dict:
    seeds = jax.random.split(jax.random.key(seed), 20)
    return {
        "tokens": noise(seeds[0], (TOKENS, D), 1.0, 6.0, ((0, 32),)),
        "features": noise(seeds[1], (TOKENS, C), 1.0, 6.0, ((0, 32),)),
        "cameras": place_ends(jax.random.randint(seeds[2], (EPISODES,), 2, 5), jax.random.fold_in(seeds[2], 1), 2, 4).astype(jnp.int32),
        "cotangent": noise(seeds[3], (TOKENS, D), 1.0, 6.0, ((0, 32),)),
        "w_qkv": noise(seeds[4], (D, 3 * D), D ** -0.5, 0.25, ((0, 32),)),
        "w_out": noise(seeds[5], (D, D), (D // 16) ** -0.5, 1.0, ((0, 32),)),
        "w_up": noise(seeds[6], (D, FF), D ** -0.5, 0.25, ((0, 32),)),
        "w_down": noise(seeds[7], (D, FF), FF ** -0.5, 0.109375, ((0, 32),)),
        "w_feat": noise(seeds[8], (C, D), C ** -0.5, 0.25, ((0, 32),)),
        "b_query": noise(seeds[9], (D,), 0.5, 3.0, (), jnp.float32),
        "b_value": noise(seeds[10], (D,), 0.5, 3.0, (), jnp.float32),
        "b_out": noise(seeds[11], (D,), 0.5, 3.0, (), jnp.float32),
        "gain_first": jnp.clip(1.0 + 0.1 * jax.random.normal(seeds[12], (D,), jnp.float32), 0.5, 1.5),
        "shift_first": noise(seeds[13], (D,), 0.3, 2.0, (), jnp.float32),
        "b_up": noise(seeds[14], (FF,), 0.5, 3.0, (), jnp.float32),
        "b_down": noise(seeds[15], (D,), 0.5, 3.0, (), jnp.float32),
        "gain_second": jnp.clip(1.0 + 0.1 * jax.random.normal(seeds[16], (D,), jnp.float32), 0.5, 1.5),
        "shift_second": noise(seeds[17], (D,), 0.3, 2.0, (), jnp.float32),
        "b_feat": noise(seeds[18], (D,), 0.5, 3.0, (), jnp.float32),
    }


HIGH = lax.Precision.HIGHEST
NEG_BIG = -1000000000.0
NORM_EPS = 1e-05

@jax.custom_vjp
def low(v):
    return lax.optimization_barrier(v.astype(jnp.bfloat16)).astype(jnp.float32)

@jax.custom_vjp
def low_back(v):
    return v

def low_keep(v):
    return (low(v), None)

def low_pass(kept, grad):
    return (grad,)

def back_keep(v):
    return (v, None)

def back_low(kept, grad):
    return (low(grad),)
low.defvjp(low_keep, low_pass)
low_back.defvjp(back_keep, back_low)

def both_ways(value):
    return low(low_back(value))

def product(left, right):
    return jnp.dot(left, right, precision=HIGH, preferred_element_type=jnp.float32)

def layer_norm(value, gain, shift):
    average = lax.optimization_barrier(jnp.mean(value, axis=-1, keepdims=True))
    centered = value - average
    variance = lax.optimization_barrier(jnp.mean(centered * centered, axis=-1, keepdims=True))
    return centered * lax.rsqrt(variance + NORM_EPS) * gain + shift

def episode(rows, feats, count, weights):
    w_qkv, w_out, w_up, w_down, w_feat, b_query, b_value, b_out, gain_first, shift_first, b_up, b_down, gain_second, shift_second, b_feat = weights
    slot_ids = jnp.arange(SLOTS, dtype=jnp.int32)
    limits = 2 + CAM_LEN * count
    valid_keys = slot_ids < limits
    camera_rows = jnp.logical_and(slot_ids >= 2, valid_keys).astype(jnp.float32)[:, None]
    memory = low_back(product(feats, w_feat) + b_feat)
    start = rows + camera_rows * memory
    start_low = low(start)
    joined = product(start_low, w_qkv)
    queries = both_ways((joined[:, :D] + b_query) * 0.125).reshape(SLOTS, HEADS, HEAD)
    key_rows = both_ways(joined[:, D:2 * D]).reshape(SLOTS, HEADS, HEAD)
    value_rows = both_ways(joined[:, 2 * D:] + b_value).reshape(SLOTS, HEADS, HEAD)
    scores = jnp.einsum('qhd,khd->hqk', queries, key_rows, precision=HIGH)
    scores = low_back(jnp.where(valid_keys[None, None, :], scores, NEG_BIG))
    row_top = lax.optimization_barrier(jnp.max(scores, axis=-1, keepdims=True))
    exponent = jnp.exp(scores - row_top)
    attn_probs = low(exponent / lax.optimization_barrier(jnp.sum(exponent, axis=-1, keepdims=True)))
    mixed_rows = jnp.einsum('hqk,khd->qhd', attn_probs, value_rows, precision=HIGH).reshape(SLOTS, D)
    attended = low_back(product(both_ways(mixed_rows), w_out) + b_out)
    normed = layer_norm(start + attended, gain_first, shift_first)
    inner = low_back(product(low(normed), w_up) + b_up)
    active = low(jax.nn.gelu(inner))
    branch = low_back(product(active, w_down.T) + b_down)
    final = layer_norm(normed + branch, gain_second, shift_second)
    return valid_keys.astype(jnp.float32)[:, None] * final

def reference(tokens, features, cameras, cotangent, w_qkv, w_out, w_up, w_down, w_feat, b_query, b_value, b_out, gain_first, shift_first, b_up, b_down, gain_second, shift_second, b_feat):
    params = tuple((item.astype(jnp.float32) for item in (w_qkv, w_out, w_up, w_down, w_feat, b_query, b_value, b_out, gain_first, shift_first, b_up, b_down, gain_second, shift_second, b_feat)))

    def forward(rows, feats, weights):

        def one_episode(item_tuple):
            return jax.checkpoint(episode)(item_tuple[0], item_tuple[1], item_tuple[2], weights)
        result = lax.map(one_episode, (rows.reshape(-1, SLOTS, D), feats.reshape(-1, SLOTS, C), cameras))
        return result.reshape(-1, D)
    output, pullback = jax.vjp(forward, tokens.astype(jnp.float32), features.astype(jnp.float32), params)
    grad_rows, grad_feats, grad_params = pullback(cotangent.astype(jnp.float32))
    return (output.astype(jnp.bfloat16), grad_rows.astype(jnp.bfloat16), grad_feats.astype(jnp.bfloat16), grad_params[0], grad_params[1], grad_params[2], grad_params[3], grad_params[4], grad_params[5], grad_params[6], grad_params[7], grad_params[8], grad_params[9], grad_params[10], grad_params[11], grad_params[12], grad_params[13], grad_params[14])
```

```python
import functools

import jax
import jax.numpy as jnp
from jax import lax
from jax.experimental import pallas as pl
from jax.experimental.pallas import tpu as pltpu
from jax.sharding import PartitionSpec as P

HEAD = 64
SLOTS = 1280
CAM_LEN = 300
CAMS_MAX = 4
NORM_EPS = 1e-05
LOG2E = 1.4426950408889634
GELU_C = 0.7978845608028654
GELU_A = 0.044715

ROWS = -(-(2 + CAM_LEN * CAMS_MAX) // 64) * 64
STEP = ROWS // 4
QBLOCKS = [(at, min(256, ROWS - at)) for at in range(0, ROWS, 256)]
MIB = 2**20

bf16 = jnp.bfloat16
f32 = jnp.float32


def dg(left, right, over_left, over_right):
    return lax.dot_general(
        left, right, (((over_left,), (over_right,)), ((), ())), preferred_element_type=f32
    )


def chunks(total, width):
    return [(at, min(width, total - at)) for at in range(0, total, width)]


def norm_parts(value):
    average = jnp.mean(value, axis=-1, keepdims=True)
    centered = value - average
    variance = jnp.mean(centered * centered, axis=-1, keepdims=True)
    scale = lax.rsqrt(variance + NORM_EPS)
    return centered * scale, scale


def norm_back(grad, unit, scale, gain):
    inside = grad * gain
    one = jnp.mean(inside, axis=-1, keepdims=True)
    two = jnp.mean(inside * unit, axis=-1, keepdims=True)
    return scale * (inside - one - unit * two)


def fold(value):
    rows, width = value.shape
    return jnp.sum(value.reshape(rows // 8, 8, width), axis=0)


def split_low(value):
    high = value.astype(bf16)
    return high, (value - high.astype(f32)).astype(bf16)


def forward_kernel(
    cameras,
    tokens,
    features,
    cotangent,
    w_feat,
    w_qkv,
    w_out,
    w_up,
    w_down,
    b_query,
    b_value,
    b_out,
    gain_first,
    shift_first,
    b_up,
    b_down,
    gain_second,
    shift_second,
    b_feat,
    output,
    start_low,
    q_rows,
    k_rows,
    v_rows,
    dmix_high,
    dmix_low,
    dots,
    grad_first,
    probs,
    grad_down,
    grad_up,
    grad_out,
    sums,
    sums_up,
    first,
    act,
    gin,
    work,
    mixed,
    mixed_low,
    inverse,
    normed_low,
    grad_branch,
    grad_att,
    q_cat,
    v_cat,
    k_cat,
    stage,
    prob_sem,
    stage_sem,
    load_sem,
):
    width = tokens.shape[1]
    hidden = w_up.shape[1]
    heads = width // HEAD
    pairs = heads // 2
    limit = 2 + CAM_LEN * cameras[0]

    def rows_of(step):
        return pl.ds(pl.multiple_of(step * STEP, 16), STEP)

    def row_ids(step):
        return step * STEP + lax.broadcasted_iota(jnp.int32, (STEP, 1), 0)

    loads = [
        pltpu.make_async_copy(
            source.at[pl.ds(0, ROWS), :], act.at[:, pl.ds(i * width, width)], load_sem.at[i]
        )
        for i, source in enumerate((features, tokens))
    ]
    for load in loads:
        load.start()
    for load in loads:
        load.wait()

    def project(step, carry):
        rows = rows_of(step)
        ids = row_ids(step)
        valid = ids < limit
        camera = jnp.logical_and(ids >= 2, valid)
        memory = dg(act[rows, :width], w_feat[...], 1, 0) + b_feat[...]
        start = act[rows, width : 2 * width].astype(f32) + jnp.where(camera, memory, 0.0)
        first[rows, :] = start
        low = start.astype(bf16)
        start_low[rows, :] = low
        joined = dg(low, w_qkv[...], 1, 0)
        q_rows[rows, :] = ((joined[:, :width] + b_query[...]) * 0.125).astype(bf16)
        keys = joined[:, width : 2 * width]
        lead = k_rows[0:16, :][0:1].astype(f32)
        k_rows[rows, :] = jnp.where(valid, keys, lead).astype(bf16)
        v_rows[rows, :] = (joined[:, 2 * width :] + b_value[...]).astype(bf16)
        return carry

    lax.fori_loop(0, 4, project, 0)

    lane_valid = lax.broadcasted_iota(jnp.int32, (1, ROWS), 1) < limit

    def prob_copy(pair, side):
        source = act if side == 0 else gin
        at = pl.ds(pl.multiple_of(lax.rem(pair, 2) * 1280, 128), 1280)
        return pltpu.make_async_copy(
            source.at[:, at], probs.at[2 * pair + side], prob_sem.at[2 * lax.rem(pair, 2) + side]
        )

    def attend(pair, carry):
        lanes = pl.ds(pl.multiple_of(pair * 128, 128), 128)

        @pl.when(pair >= 2)
        def _():
            prob_copy(pair - 2, 0).wait()
            prob_copy(pair - 2, 1).wait()

        queries = q_rows[:, lanes].astype(f32).T * LOG2E
        high, low = split_low(queries)
        none = jnp.zeros((HEAD, ROWS), bf16)
        values = jnp.where(lane_valid, v_rows[:, lanes].astype(f32).T, 0.0).astype(bf16)
        ones = jnp.broadcast_to(jnp.where(lane_valid, 1.0, 0.0), (HEAD, ROWS)).astype(bf16)
        for side in range(2):
            own = slice(side * HEAD, side * HEAD + HEAD)
            other = slice((1 - side) * HEAD, (1 - side) * HEAD + HEAD)
            q_cat[side, own, :] = high[own]
            q_cat[side, other, :] = none
            q_cat[side, 128 + side * HEAD : 128 + side * HEAD + HEAD, :] = low[own]
            q_cat[side, 128 + (1 - side) * HEAD : 128 + (1 - side) * HEAD + HEAD, :] = none
            v_cat[side, :HEAD, :] = values[own]
            v_cat[side, HEAD:, :] = ones
        keys = k_rows[:, lanes]
        k_cat[:, :128] = keys
        k_cat[:, 128:] = keys
        base = lax.rem(pair, 2) * 1280
        jobs = [(side, at, size) for side in range(2) for at, size in QBLOCKS]
        peak = {}

        def score(job, at_key, keys_here):
            side, at, size = jobs[job]
            here = slice(at_key, at_key + keys_here)
            scores = dg(k_cat[here, :], q_cat[side, :, at : at + size], 1, 0)
            work[job % 3 * 4 + at_key // STEP, :, :size] = scores
            high_here = jnp.max(scores, axis=0, keepdims=True)
            peak[job] = jnp.maximum(peak[job], high_here) if job in peak else high_here

        def weigh(job, at_key, keys_here):
            side, at, size = jobs[job]
            slot = act if side == 0 else gin
            here = slice(at_key, at_key + keys_here)
            slot[here, pl.ds(pl.multiple_of(base + at, 128), size)] = jnp.exp2(
                work[job % 3 * 4 + at_key // STEP, :, :size] - peak[job]
            ).astype(bf16)

        def mix(job):
            side, at, size = jobs[job]
            slot = act if side == 0 else gin
            weight = slot[:, pl.ds(pl.multiple_of(base + at, 128), size)]
            summed = dg(v_cat[side], weight, 1, 0)
            inv = 1.0 / summed[HEAD : HEAD + 1]
            mixed[pl.ds(pl.multiple_of(pair * 128 + side * HEAD, 8), HEAD), at : at + size] = (
                summed[:HEAD] * inv
            )
            inverse[2 * pair + side, :, at : at + size] = inv

        parts = chunks(ROWS, STEP)
        for job in (0, 1):
            for part in parts:
                score(job, *part)
        for job in range(len(jobs)):
            for part in parts:
                if job + 2 < len(jobs):
                    score(job + 2, *part)
                weigh(job, *part)
            if job >= 2:
                mix(job - 2)
            if job == len(QBLOCKS) - 1:
                prob_copy(pair, 0).start()
        mix(len(jobs) - 2)
        mix(len(jobs) - 1)
        prob_copy(pair, 1).start()
        return carry

    lax.fori_loop(0, pairs, attend, 0)
    for pair in (pairs - 2, pairs - 1):
        for side in range(2):
            prob_copy(pair, side).wait()

    mixed_low[...] = mixed[...].astype(bf16)
    for at, size in chunks(width, 256):
        cols = slice(at, at + size)
        first[:, cols] += dg(mixed_low[...], w_out[:, cols], 0, 0) + b_out[:, cols]
    sums[...] = jnp.zeros_like(sums)
    sums_up[...] = jnp.zeros_like(sums_up)
    cuts = chunks(hidden, 512)

    def feed(step, carry):
        rows = rows_of(step)
        valid = row_ids(step) < limit
        unit_first, scale_first = norm_parts(first[rows, :])
        normed = unit_first * gain_first[...] + shift_first[...]
        low = normed.astype(bf16)
        normed_low[rows, :] = low
        for at, size in cuts:
            cols = slice(at, at + size)
            inner = dg(low, w_up[:, cols], 1, 0) + b_up[:, cols]
            square = inner * inner
            half = 0.5 + 0.5 * jnp.tanh(inner * (GELU_C + (GELU_C * GELU_A) * square))
            value = inner * half
            act[rows, cols] = value.astype(bf16)
            slope = half + value * (1.0 - half) * (2 * GELU_C + (6 * GELU_C * GELU_A) * square)
            for cut, wide in chunks(size, 256):
                work[(at + cut) // 256, :, :wide] = slope[:, cut : cut + wide]
        branch = dg(act[rows, :], w_down[...], 1, 1) + b_down[...]
        unit_second, scale_second = norm_parts(normed + branch)
        final = unit_second * gain_second[...] + shift_second[...]
        output[rows, :] = jnp.where(valid, final, 0.0).astype(bf16)
        grad = jnp.where(valid, cotangent[rows, :].astype(f32), 0.0)
        sums[0] += fold(grad * unit_second)
        sums[1] += fold(grad)
        grad_second = norm_back(grad, unit_second, scale_second, gain_second[...])
        low_branch = grad_second.astype(bf16)
        grad_branch[rows, :] = low_branch
        sums[2] += fold(low_branch.astype(f32))
        for at, size in cuts:
            cols = slice(at, at + size)
            slope = [work[(at + cut) // 256, :, :wide] for cut, wide in chunks(size, 256)]
            low_inner = (
                dg(low_branch, w_down[:, cols], 1, 0) * jnp.concatenate(slope, axis=1)
            ).astype(bf16)
            gin[rows, cols] = low_inner
            sums_up[:, cols] += fold(low_inner.astype(f32))
        grad_normed = grad_second + dg(gin[rows, :], w_up[...], 1, 1)
        sums[3] += fold(grad_normed * unit_first)
        sums[4] += fold(grad_normed)
        back = norm_back(grad_normed, unit_first, scale_first, gain_first[...])
        grad_first[rows, :] = back
        low_att = back.astype(bf16)
        grad_att[rows, :] = low_att
        sums[5] += fold(low_att.astype(f32))
        return carry

    lax.fori_loop(0, 4, feed, 0)
    output[ROWS:, :] = jnp.zeros((SLOTS - ROWS, width), bf16)

    for at, size in QBLOCKS:
        cols = slice(at, at + size)
        grad_mixed = dg(w_out[...], grad_att[cols, :], 1, 1).astype(bf16).astype(f32)
        scaled = grad_mixed.reshape(heads, HEAD, size) * inverse[:, :, cols]
        dots[:, :, cols] = jnp.sum(
            scaled * mixed[:, cols].reshape(heads, HEAD, size), axis=1, keepdims=True
        )
        high, low = split_low(scaled.reshape(width, size))
        dmix_high[:, cols] = high
        dmix_low[:, cols] = low

    def weight_copy(target, at, size, slot):
        return pltpu.make_async_copy(
            stage.at[slot, :, pl.ds(0, size)], target.at[:, pl.ds(at, size)], stage_sem.at[slot]
        )

    pending = {}
    for turn, (left, right, target, (at, size)) in enumerate(
        [(grad_branch, act, grad_down, cut) for cut in cuts]
        + [(normed_low, gin, grad_up, cut) for cut in cuts]
    ):
        slot = turn % 2
        if slot in pending:
            pending[slot].wait()
        stage[slot, :, 0:size] = dg(left[...], right[:, at : at + size], 0, 0).astype(bf16)
        pending[slot] = weight_copy(target, at, size, slot)
        pending[slot].start()
    grad_out[...] = dg(mixed_low[...], grad_att[...], 1, 0).astype(bf16)
    for copy in pending.values():
        copy.wait()


def shaped(shape, dtype):
    return jax.ShapeDtypeStruct(shape, dtype)


def forward_call(cameras, tokens, features, cotangent, weights, biases):
    width = tokens.shape[1]
    hidden = weights[3].shape[1]
    heads = width // HEAD
    outs = (
        shaped((SLOTS, width), bf16),
        shaped((ROWS, width), bf16),
        shaped((ROWS, width), bf16),
        shaped((ROWS, width), bf16),
        shaped((ROWS, width), bf16),
        shaped((width, ROWS), bf16),
        shaped((width, ROWS), bf16),
        shaped((heads, 1, ROWS), f32),
        shaped((ROWS, width), f32),
        shaped((heads, ROWS, 1280), bf16),
        shaped((width, hidden), bf16),
        shaped((width, hidden), bf16),
        shaped((width, width), bf16),
        shaped((6, 8, width), f32),
        shaped((8, hidden), f32),
    )
    vmem = pl.BlockSpec(memory_space=pltpu.VMEM)
    hbm = pl.BlockSpec(memory_space=pl.ANY)
    return pl.pallas_call(
        forward_kernel,
        out_shape=outs,
        in_specs=[pl.BlockSpec(memory_space=pltpu.SMEM)] + [hbm] * 2 + [vmem] * 16,
        out_specs=tuple(hbm if i in (9, 10, 11) else vmem for i in range(15)),
        scratch_shapes=[
            pltpu.VMEM((ROWS, width), f32),
            pltpu.VMEM((ROWS, hidden), bf16),
            pltpu.VMEM((ROWS, hidden), bf16),
            pltpu.VMEM((max(12, -(-hidden // 256)), STEP, 256), f32),
            pltpu.VMEM((width, ROWS), f32),
            pltpu.VMEM((width, ROWS), bf16),
            pltpu.VMEM((heads, 1, ROWS), f32),
            pltpu.VMEM((ROWS, width), bf16),
            pltpu.VMEM((ROWS, width), bf16),
            pltpu.VMEM((ROWS, width), bf16),
            pltpu.VMEM((2, 256, ROWS), bf16),
            pltpu.VMEM((2, 128, ROWS), bf16),
            pltpu.VMEM((ROWS, 256), bf16),
            pltpu.VMEM((2, width, 512), bf16),
            pltpu.SemaphoreType.DMA((4,)),
            pltpu.SemaphoreType.DMA((2,)),
            pltpu.SemaphoreType.DMA((2,)),
        ],
        compiler_params=pltpu.CompilerParams(vmem_limit_bytes=62 * MIB),
        name="layer_forward",
    )(cameras, tokens, features, cotangent, *weights, *biases)


def backward_kernel(
    cameras,
    features,
    q_rows,
    k_rows,
    v_rows,
    dmix_high,
    dmix_low,
    dots,
    start_low,
    grad_first,
    probs,
    w_qkv,
    w_feat,
    grad_tokens,
    grad_features,
    grad_qkv,
    grad_feat,
    sums,
    feats,
    weights,
    grad_scores,
    joined,
    d_cat,
    d_rows,
    v_cat,
    k_turned,
    grad_memory,
    prob_sem,
    load_sem,
):
    width = q_rows.shape[1]
    heads = width // HEAD
    pairs = heads // 2
    limit = 2 + CAM_LEN * cameras[0]

    def prob_copy(pair, side):
        slot = 2 * lax.rem(pair, 2) + side
        return pltpu.make_async_copy(
            probs.at[2 * pair + side], weights.at[slot], prob_sem.at[slot]
        )

    for side in range(2):
        prob_copy(0, side).start()
    load = pltpu.make_async_copy(features.at[pl.ds(0, ROWS), :], feats, load_sem)
    load.start()
    sums[...] = jnp.zeros_like(sums)
    lane_valid = lax.broadcasted_iota(jnp.int32, (1, ROWS), 1) < limit
    row_valid = lax.broadcasted_iota(jnp.int32, (ROWS, 1), 0) < limit

    def attend_back(pair, carry):
        lanes = pl.ds(pl.multiple_of(pair * 128, 128), 128)

        @pl.when(pair + 1 < pairs)
        def _():
            prob_copy(pair + 1, 0).start()
            prob_copy(pair + 1, 1).start()

        both = pl.ds(pl.multiple_of(pair * 128, 128), 128)
        high = dmix_high[both, :]
        low = dmix_low[both, :]
        none = jnp.zeros((HEAD, ROWS), bf16)
        for side in range(2):
            own = slice(side * HEAD, side * HEAD + HEAD)
            mine, its = side * HEAD, (1 - side) * HEAD
            d_cat[side, mine : mine + HEAD, :] = high[own]
            d_cat[side, its : its + HEAD, :] = none
            d_cat[side, 128 + mine : 128 + mine + HEAD, :] = low[own]
            d_cat[side, 128 + its : 128 + its + HEAD, :] = none
        d_rows[:, :128] = high.astype(f32).T.astype(bf16)
        d_rows[:, 128:] = low.astype(f32).T.astype(bf16)
        values = v_rows[:, lanes]
        v_cat[:, :128] = values
        v_cat[:, 128:] = values
        k_turned[...] = jnp.where(lane_valid, k_rows[:, lanes].astype(f32).T, 0.0).astype(bf16)
        base = 2 * lax.rem(pair, 2)
        jobs = [(side, at, size) for side in range(2) for at, size in QBLOCKS]
        parts = chunks(ROWS, STEP)
        turned = {0: [], 1: []}
        wide = {}

        def slope(job):
            side, at, size = jobs[job]
            offset = dots[2 * pair + side, :, at : at + size]
            for at_key, keys_here in parts:
                here = slice(at_key, at_key + keys_here)
                grad = dg(v_cat[here, :], d_cat[side, :, at : at + size], 1, 0) - offset
                weight = weights[base + side, here, at : at + size].astype(f32)
                grad_scores[side, here, at : at + size] = (weight * grad).astype(bf16)

        def queries(job):
            side, at, size = jobs[job]
            turned[side].append(
                dg(k_turned[...], grad_scores[side, :, at : at + size], 1, 0)[
                    side * HEAD : side * HEAD + HEAD
                ]
            )

        def spread(side, part):
            here = slice(part[0], part[0] + part[1])
            value = dg(weights[base + side, here, :ROWS], d_rows[...], 1, 0)
            value = value[:, :128] + value[:, 128:]
            key = dg(grad_scores[side, here, :ROWS], q_rows[:, lanes], 1, 0)
            wide[side, part] = (value, key)

        for side in range(2):
            prob_copy(pair, side).wait()
        for job in range(len(jobs)):
            slope(job)
            if job >= 1:
                queries(job - 1)
            if job > len(QBLOCKS):
                side_job = job - len(QBLOCKS) - 1
                if side_job < len(parts):
                    spread(0, parts[side_job])
        queries(len(jobs) - 1)
        first_lane = lax.broadcasted_iota(jnp.int32, (STEP, 128), 1) < HEAD
        for part in parts:
            spread(1, part)
            here = slice(part[0], part[0] + part[1])
            keep = row_valid[here]
            for which, at in ((0, 2 * width), (1, width)):
                value = jnp.where(first_lane, wide[0, part][which], wide[1, part][which])
                value = jnp.where(keep, value, 0.0).astype(bf16)
                joined[here, pl.ds(pl.multiple_of(at + pair * 128, 128), 128)] = value
        query = jnp.concatenate(
            [jnp.concatenate(turned[0], axis=1), jnp.concatenate(turned[1], axis=1)], axis=0
        )
        joined[:, lanes] = (query.astype(bf16).astype(f32).T * 0.125).astype(bf16)
        return carry

    lax.fori_loop(0, pairs, attend_back, 0)
    load.wait()

    def project_back(step, carry):
        rows = pl.ds(pl.multiple_of(step * STEP, 16), STEP)
        ids = step * STEP + lax.broadcasted_iota(jnp.int32, (STEP, 1), 0)
        camera = jnp.logical_and(ids >= 2, ids < limit)
        part = joined[rows, :]
        sums[0] += fold(part[:, :width].astype(f32))
        sums[1] += fold(part[:, 2 * width :].astype(f32))
        grad_start = grad_first[rows, :] + dg(part, w_qkv[...], 1, 1)
        grad_tokens[rows, :] = grad_start.astype(bf16)
        low = jnp.where(camera, grad_start, 0.0).astype(bf16)
        grad_memory[rows, :] = low
        sums[2] += fold(low.astype(f32))
        grad_features[rows, :] = dg(low, w_feat[...], 1, 1).astype(bf16)
        return carry

    lax.fori_loop(0, 4, project_back, 0)
    grad_tokens[ROWS:, :] = jnp.zeros((SLOTS - ROWS, width), bf16)
    grad_features[ROWS:, :] = jnp.zeros((SLOTS - ROWS, width), bf16)
    for at, size in chunks(3 * width, 512):
        cols = slice(at, at + size)
        grad_qkv[:, cols] = dg(start_low[...], joined[:, cols], 0, 0).astype(bf16)
    grad_feat[...] = dg(feats[...], grad_memory[...], 0, 0).astype(bf16)


def backward_call(cameras, features, saved, w_qkv, w_feat):
    width = features.shape[1]
    heads = width // HEAD
    outs = (
        shaped((SLOTS, width), bf16),
        shaped((SLOTS, width), bf16),
        shaped((width, 3 * width), bf16),
        shaped((width, width), bf16),
        shaped((3, 8, width), f32),
    )
    vmem = pl.BlockSpec(memory_space=pltpu.VMEM)
    hbm = pl.BlockSpec(memory_space=pl.ANY)
    return pl.pallas_call(
        backward_kernel,
        out_shape=outs,
        in_specs=[pl.BlockSpec(memory_space=pltpu.SMEM), hbm] + [vmem] * 8 + [hbm] + [vmem] * 2,
        out_specs=(vmem,) * 5,
        scratch_shapes=[
            pltpu.VMEM((ROWS, width), bf16),
            pltpu.VMEM((4, ROWS, 1280), bf16),
            pltpu.VMEM((2, ROWS, 1280), bf16),
            pltpu.VMEM((ROWS, 3 * width), bf16),
            pltpu.VMEM((2, 256, ROWS), bf16),
            pltpu.VMEM((ROWS, 256), bf16),
            pltpu.VMEM((ROWS, 256), bf16),
            pltpu.VMEM((128, ROWS), bf16),
            pltpu.VMEM((ROWS, width), bf16),
            pltpu.SemaphoreType.DMA((4,)),
            pltpu.SemaphoreType.DMA(()),
        ],
        compiler_params=pltpu.CompilerParams(vmem_limit_bytes=62 * MIB),
        name="layer_backward",
    )(cameras, features, *saved, w_qkv, w_feat)


MESH = pl.DeviceIdType.MESH
GATHER_MSGS = 11


def place():
    dp = lax.axis_index("dp")
    fs = lax.axis_index("fsdp")
    return dp // 2, dp % 2, fs // 2, fs % 2


def device(y, x, z, c):
    return (y * 2 + x, z * 2 + c)


def neighbours():
    y, x, z, c = place()
    around = [device(y, x, (z + k) % 4, c) for k in (1, 2, 3)]
    return around + [device(y, 1 - x, z, c), device(1 - y, x, z, c), device(y, x, z, 1 - c)]


def greet():
    barrier = pltpu.get_barrier_semaphore()
    peers = neighbours()
    for peer in peers:
        pl.semaphore_signal(barrier, inc=1, device_id=peer, device_id_type=MESH)
    pl.semaphore_wait(barrier, len(peers))


class Gather:
    def __init__(self, shard, whole, send, recv, local, group):
        self.shard, self.whole, self.send, self.recv = shard, whole, send, recv
        self.local, self.group = local, group
        self.sent = []

    def copy(self, msg, source, target, peer):
        return pltpu.make_async_remote_copy(
            src_ref=source,
            dst_ref=target,
            send_sem=self.send.at[self.group, msg],
            recv_sem=self.recv.at[self.group, msg],
            device_id=peer,
            device_id_type=MESH,
        )

    def push(self, msg, part, peer):
        copy = self.copy(msg, part, part, peer)
        copy.start()
        self.sent.append(copy)

    def arrived(self, msg, part):
        self.copy(msg, part, part, self.nobody).wait_recv()

    def stage(self, number):
        y, x, z, c = place()
        self.nobody = device(y, x, z, 1 - c)
        whole = self.whole
        dp, dp_x, dp_y, dp_d = y * 2 + x, y * 2 + 1 - x, (1 - y) * 2 + x, (1 - y) * 2 + 1 - x
        to_x, to_y, to_c = device(y, 1 - x, z, c), device(1 - y, x, z, c), device(y, x, z, 1 - c)
        if number == 0:
            own = whole.at[dp, z, c]
            keep = pltpu.make_async_copy(self.shard, own, self.local.at[self.group])
            keep.start()
            for k in (1, 2, 3):
                copy = self.copy(k - 1, self.shard, own, device(y, x, (z + k) % 4, c))
                copy.start()
                self.sent.append(copy)
            keep.wait()
        elif number == 1:
            for k in (1, 2, 3):
                self.arrived(k - 1, whole.at[dp, (z + 4 - k) % 4, c])
            column = whole.at[dp, :, c]
            self.push(3, column, to_x)
            self.push(4, column, to_y)
            self.push(7, column, to_c)
        elif number == 2:
            self.arrived(3, whole.at[dp_x, :, c])
            self.push(5, whole.at[dp_x, pl.ds(0, 2), c], to_y)
            self.arrived(4, whole.at[dp_y, :, c])
            self.push(6, whole.at[dp_y, pl.ds(2, 2), c], to_x)
            self.push(8, whole.at[dp_x, :, c], to_c)
            self.push(9, whole.at[dp_y, :, c], to_c)
        elif number == 3:
            self.arrived(5, whole.at[dp_d, pl.ds(0, 2), c])
            self.arrived(6, whole.at[dp_d, pl.ds(2, 2), c])
            self.push(10, whole.at[dp_d, :, c], to_c)
        elif number == 4:
            for msg, place_dp in ((7, dp), (8, dp_x), (9, dp_y), (10, dp_d)):
                self.arrived(msg, whole.at[place_dp, :, 1 - c])
        elif number == 5:
            for copy in self.sent:
                copy.wait_send()


class Reduce:
    def __init__(self, part, out, bufs, send, recv, group):
        self.part, self.out, self.send, self.recv, self.group = part, out, send, recv, group
        self.half, self.diag, self.side, self.line = bufs
        self.sent = []

    copy = Gather.copy

    def push(self, msg, source, target, peer):
        copy = self.copy(msg, source, target, peer)
        copy.start()
        self.sent.append(copy)

    def arrived(self, msg, target):
        self.copy(msg, target, target, self.nobody).wait_recv()

    def add(self, target, *sources):
        total = sources[0][...].astype(f32)
        for source in sources[1:]:
            total = total + source[...].astype(f32)
        target[...] = total.astype(target.dtype)

    def stage(self, number):
        y, x, z, c = place()
        self.nobody = device(y, x, z, 1 - c)
        dp, dp_x, dp_y, dp_d = y * 2 + x, y * 2 + 1 - x, (1 - y) * 2 + x, (1 - y) * 2 + 1 - x
        to_x, to_y, to_c = device(y, 1 - x, z, c), device(1 - y, x, z, c), device(y, x, z, 1 - c)
        part, half = self.part, self.half
        if number == 0:
            for msg, at in ((0, dp_d), (1, dp_x), (2, dp_y), (3, dp)):
                self.push(msg, part.at[at, :, 1 - c], half.at[at], to_c)
        elif number == 1:
            self.arrived(0, half.at[dp_d])
            self.add(half.at[dp_d], half.at[dp_d], part.at[dp_d, :, c])
            self.push(4, half.at[dp_d, pl.ds(0, 2)], self.diag.at[0], to_x)
            self.push(5, half.at[dp_d, pl.ds(2, 2)], self.diag.at[1], to_y)
            self.arrived(1, half.at[dp_x])
            self.add(half.at[dp_x], half.at[dp_x], part.at[dp_x, :, c])
            self.arrived(2, half.at[dp_y])
            self.add(half.at[dp_y], half.at[dp_y], part.at[dp_y, :, c])
        elif number == 2:
            self.arrived(5, self.diag.at[1])
            late = half.at[dp_x, pl.ds(2, 2)]
            self.add(late, late, self.diag.at[1])
            self.push(6, half.at[dp_x], self.side.at[0], to_x)
            self.arrived(4, self.diag.at[0])
            late = half.at[dp_y, pl.ds(0, 2)]
            self.add(late, late, self.diag.at[0])
            self.push(7, half.at[dp_y], self.side.at[1], to_y)
            self.arrived(3, half.at[dp])
            self.add(half.at[dp], half.at[dp], part.at[dp, :, c])
        elif number == 3:
            self.arrived(6, self.side.at[0])
            self.arrived(7, self.side.at[1])
            self.add(half.at[dp], half.at[dp], self.side.at[0], self.side.at[1])
            for k in (1, 2, 3):
                self.push(
                    7 + k, half.at[dp, (z + k) % 4], self.line.at[k - 1], device(y, x, (z + k) % 4, c)
                )
        elif number == 4:
            for k in (1, 2, 3):
                self.arrived(7 + k, self.line.at[k - 1])
            self.add(self.out, half.at[dp, z], self.line.at[0], self.line.at[1], self.line.at[2])
        elif number == 5:
            for copy in self.sent:
                copy.wait_send()


class Total:
    def __init__(self, value, out, bufs, send, recv, group):
        self.value, self.out, self.send, self.recv, self.group = value, out, send, recv, group
        self.mine, self.theirs = bufs
        self.sent = []

    copy = Gather.copy

    def stage(self, number):
        y, x, z, c = place()
        self.nobody = device(y, x, z, 1 - c)
        peers = [
            device(y, x, z, 1 - c),
            device(y, 1 - x, z, c),
            device(1 - y, x, z, c),
            device(y, x, z + 1 - 2 * (z % 2), c),
            device(y, x, (z + 2) % 4, c),
        ]
        mine, theirs = self.mine, self.theirs
        if number == 0:
            mine[0] = self.value[...]
        elif number <= 5:
            at = number - 1
            self.copy(at, mine.at[at], theirs.at[at], self.nobody).wait_recv()
            if number < 5:
                mine[number] = mine[at] + theirs[at]
            else:
                self.out[...] = mine[at] + theirs[at]
        if number < 5:
            copy = self.copy(number, mine.at[number], theirs.at[number], peers[number])
            copy.start()
            self.sent.append(copy)
        if number == 6:
            for copy in self.sent:
                copy.wait_send()


def in_turn(groups, last):
    for turn in range(len(groups) + last):
        for at, group in enumerate(groups):
            if 0 <= turn - at <= last:
                group.stage(turn - at)


def gather_kernel(*refs):
    shards, wholes, (send, recv, local) = refs[:5], refs[5:10], refs[10:]
    greet()
    groups = [
        Gather(shard, whole, send, recv, local, i)
        for i, (shard, whole) in enumerate(zip(shards, wholes))
    ]
    in_turn(groups, 5)


def gather_call(weights):
    vmem = pl.BlockSpec(memory_space=pltpu.VMEM)
    outs = tuple(shaped((4, 4, 2) + w.shape, bf16) for w in weights)
    wholes = pl.pallas_call(
        gather_kernel,
        out_shape=outs,
        in_specs=[vmem] * 5,
        out_specs=(vmem,) * 5,
        scratch_shapes=[
            pltpu.SemaphoreType.DMA((5, GATHER_MSGS)),
            pltpu.SemaphoreType.DMA((5, GATHER_MSGS)),
            pltpu.SemaphoreType.DMA((5,)),
        ],
        compiler_params=pltpu.CompilerParams(
            collective_id=0, has_side_effects=True, vmem_limit_bytes=62 * MIB
        ),
        name="gather_weights",
    )(*weights)
    return tuple(whole.reshape(-1, whole.shape[-1]) for whole in wholes)


def reduce_bufs(columns, rows):
    return [
        pltpu.VMEM((4, 4, rows, columns), bf16),
        pltpu.VMEM((2, 2, rows, columns), bf16),
        pltpu.VMEM((2, 4, rows, columns), bf16),
        pltpu.VMEM((3, rows, columns), bf16),
    ]


def reduce_kernel(*refs):
    parts, small, outs, small_out, bufs = refs[:5], refs[5], refs[6:11], refs[11], refs[12:-2]
    send, recv = refs[-2:]
    greet()
    groups = [
        Reduce(parts[i], outs[i], bufs[4 * i : 4 * i + 4], send, recv, i) for i in range(5)
    ]
    groups.append(Total(small, small_out, bufs[20:22], send, recv, 5))
    in_turn(groups, 6)


def reduce_call(grads, small):
    vmem = pl.BlockSpec(memory_space=pltpu.VMEM)
    rows = grads[0].shape[0] // 32
    parts = [grad.reshape(4, 4, 2, rows, grad.shape[1]) for grad in grads]
    bufs = [buf for grad in grads for buf in reduce_bufs(grad.shape[1], rows)]
    bufs += [pltpu.VMEM((5,) + small.shape, f32)] * 2
    return pl.pallas_call(
        reduce_kernel,
        out_shape=tuple(shaped((rows, grad.shape[1]), f32) for grad in grads)
        + (shaped(small.shape, f32),),
        in_specs=[vmem] * 6,
        out_specs=(vmem,) * 6,
        scratch_shapes=bufs
        + [pltpu.SemaphoreType.DMA((6, GATHER_MSGS)), pltpu.SemaphoreType.DMA((6, GATHER_MSGS))],
        compiler_params=pltpu.CompilerParams(
            collective_id=1, has_side_effects=True, vmem_limit_bytes=62 * MIB
        ),
        name="reduce_gradients",
    )(*parts, small)


AXES = ("dp", "fsdp")


def on_device(
    fast,
    tokens,
    features,
    cameras,
    cotangent,
    w_qkv,
    w_out,
    w_up,
    w_down,
    w_feat,
    *biases,
):
    width = tokens.shape[1]
    hidden = w_up.shape[1]
    biases = [bias.reshape(1, -1) for bias in biases]
    shards = (w_feat, w_qkv, w_out, w_up, w_down)
    if fast:
        weights = gather_call(shards)
    else:
        weights = tuple(lax.all_gather(w, AXES, axis=0, tiled=True) for w in shards)
    (
        output,
        start_low,
        q_rows,
        k_rows,
        v_rows,
        dmix_high,
        dmix_low,
        dots,
        grad_first,
        probs,
        grad_down,
        grad_up,
        grad_out,
        sums,
        sums_up,
    ) = forward_call(cameras, tokens, features, cotangent, weights, biases)
    saved = (q_rows, k_rows, v_rows, dmix_high, dmix_low, dots, start_low, grad_first, probs)
    grad_tokens, grad_features, grad_qkv, grad_feat, sums_back = backward_call(
        cameras, features, saved, weights[1], weights[0]
    )
    grads = (grad_down, grad_up, grad_out, grad_qkv, grad_feat)
    small = jnp.concatenate(
        [
            jnp.sum(sums, axis=1).reshape(-1),
            jnp.sum(sums_back, axis=1).reshape(-1),
            jnp.sum(sums_up, axis=0),
        ]
    )
    lines = -(-small.shape[0] // 1024) * 8
    small = jnp.pad(small, (0, lines * 128 - small.shape[0])).reshape(lines, 128)
    if fast:
        *grads, small = reduce_call(grads, small)
    else:
        grads = [
            lax.psum_scatter(
                lax.optimization_barrier(grad.astype(f32)), AXES, scatter_dimension=0, tiled=True
            )
            for grad in grads
        ]
        small = lax.psum(small, AXES)
    small = small.reshape(-1)
    rows = small[: 9 * width].reshape(9, width)
    grad_b_up = small[9 * width : 9 * width + hidden]
    grad_down, grad_up, grad_out, grad_qkv, grad_feat = grads
    return (
        output,
        grad_tokens,
        grad_features,
        grad_qkv,
        grad_out,
        grad_up,
        grad_down,
        grad_feat,
        rows[6],
        rows[7],
        rows[5],
        rows[3],
        rows[4],
        grad_b_up,
        rows[2],
        rows[0],
        rows[1],
        rows[8],
    )


def solution(mesh):
    split = P(AXES, None)
    fast = mesh.shape["dp"] == 4 and mesh.shape["fsdp"] == 8
    return jax.shard_map(
        functools.partial(on_device, fast),
        mesh=mesh,
        in_specs=(split, split, P(AXES), split) + (split,) * 5 + (P(),) * 10,
        out_specs=(split,) * 8 + (P(),) * 10,
        check_vma=False,
    )
```

```python
import functools

import jax
import jax.numpy as jnp
from jax import lax
from jax.experimental import pallas as pl
from jax.experimental.pallas import tpu as pltpu
from jax.sharding import PartitionSpec as P

HEAD = 64
SLOTS = 1280
CAM_LEN = 300
CAMS_MAX = 4
NORM_EPS = 1e-05
LOG2E = 1.4426950408889634
GELU_C = 0.7978845608028654
GELU_A = 0.044715

ROWS = -(-(2 + CAM_LEN * CAMS_MAX) // 64) * 64
STEP = ROWS // 4
QBLOCKS = [(at, min(256, ROWS - at)) for at in range(0, ROWS, 256)]
MIB = 2**20

bf16 = jnp.bfloat16
f32 = jnp.float32


def dg(left, right, over_left, over_right):
    return lax.dot_general(
        left, right, (((over_left,), (over_right,)), ((), ())), preferred_element_type=f32
    )


def chunks(total, width):
    return [(at, min(width, total - at)) for at in range(0, total, width)]


def norm_parts(value):
    average = jnp.mean(value, axis=-1, keepdims=True)
    centered = value - average
    variance = jnp.mean(centered * centered, axis=-1, keepdims=True)
    scale = lax.rsqrt(variance + NORM_EPS)
    return centered * scale, scale


def norm_back(grad, unit, scale, gain):
    inside = grad * gain
    one = jnp.mean(inside, axis=-1, keepdims=True)
    two = jnp.mean(inside * unit, axis=-1, keepdims=True)
    return scale * (inside - one - unit * two)


def fold(value):
    rows, width = value.shape
    return jnp.sum(value.reshape(rows // 8, 8, width), axis=0)


def split_low(value):
    high = value.astype(bf16)
    return high, (value - high.astype(f32)).astype(bf16)


MESH = pl.DeviceIdType.MESH
GATHER_MSGS = 11


def place():
    dp = lax.axis_index("dp")
    fs = lax.axis_index("fsdp")
    return dp // 2, dp % 2, fs // 2, fs % 2


def device(y, x, z, c):
    return (y * 2 + x, z * 2 + c)


def neighbours():
    y, x, z, c = place()
    around = [device(y, x, (z + k) % 4, c) for k in (1, 2, 3)]
    return around + [device(y, 1 - x, z, c), device(1 - y, x, z, c), device(y, x, z, 1 - c)]


def greet():
    barrier = pltpu.get_barrier_semaphore()
    peers = neighbours()
    for peer in peers:
        pl.semaphore_signal(barrier, inc=1, device_id=peer, device_id_type=MESH)
    pl.semaphore_wait(barrier, len(peers))


class Gather:
    def __init__(self, shard, whole, cols, send, recv, local, group):
        self.shard, self.whole, self.cols, self.send, self.recv = shard, whole, cols, send, recv
        self.local, self.group = local, group

    def copy(self, msg, source, target, peer):
        return pltpu.make_async_remote_copy(
            src_ref=source,
            dst_ref=target,
            send_sem=self.send.at[self.group, msg],
            recv_sem=self.recv.at[self.group, msg],
            device_id=peer,
            device_id_type=MESH,
        )

    def stage(self, number):
        y, x, z, c = place()
        at_x, at_y, at_d, at = y * 2 + 1 - x, (1 - y) * 2 + x, (1 - y) * 2 + 1 - x, y * 2 + x
        to_x, to_y, to_c = device(y, 1 - x, z, c), device(1 - y, x, z, c), device(y, x, z, 1 - c)
        cols = pl.ds(*self.cols)
        whole = lambda dp, line, core: self.whole.at[dp, line, core, :, cols]
        own = whole(at, z, c)
        shard = self.shard.at[:, cols]
        every, low, high = slice(None), pl.ds(0, 2), pl.ds(2, 2)
        out = [(shard, own, device(y, x, (z + k) % 4, c)) for k in (1, 2, 3)] + [
            (part, part, peer)
            for part, peer in (
                (whole(at, every, c), to_x),
                (whole(at, every, c), to_y),
                (whole(at_x, low, c), to_y),
                (whole(at_y, high, c), to_x),
                (whole(at, every, c), to_c),
                (whole(at_x, every, c), to_c),
                (whole(at_y, every, c), to_c),
                (whole(at_d, every, c), to_c),
            )
        ]
        arrived = lambda msg, part: self.copy(msg, part, part, to_c).wait_recv()
        start = lambda msg: self.copy(msg, *out[msg]).start()
        if number == 0:
            keep = pltpu.make_async_copy(shard, own, self.local.at[self.group])
            keep.start()
            for msg in (0, 1, 2):
                start(msg)
            keep.wait()
        elif number == 1:
            for k in (1, 2, 3):
                arrived(k - 1, whole(at, (z + 4 - k) % 4, c))
            for msg in (3, 4, 7):
                start(msg)
        elif number == 2:
            arrived(3, whole(at_x, every, c))
            start(5)
            arrived(4, whole(at_y, every, c))
            for msg in (6, 8, 9):
                start(msg)
        elif number == 3:
            arrived(5, whole(at_d, low, c))
            arrived(6, whole(at_d, high, c))
            start(10)
        elif number == 4:
            for msg, dp in ((7, at), (8, at_x), (9, at_y), (10, at_d)):
                arrived(msg, whole(dp, every, 1 - c))
        elif number == 5:
            for msg, ends in enumerate(out):
                self.copy(msg, *ends).wait_send()


def turns(groups, *list_of):
    for stage, group in list_of:
        groups[group].stage(stage)


def matrix(ref, cols=slice(None)):
    value = ref[(slice(None),) * (len(ref.shape) - 1) + (cols,)]
    return value.reshape(-1, value.shape[-1])


class Reduce:
    def __init__(self, part, out, bufs, send, recv, group):
        self.part, self.out, self.send, self.recv, self.group = part, out, send, recv, group
        self.half, self.diag, self.side, self.line = bufs
        self.sent = []

    copy = Gather.copy

    def push(self, msg, source, target, peer):
        copy = self.copy(msg, source, target, peer)
        copy.start()
        self.sent.append(copy)

    def arrived(self, msg, target):
        self.copy(msg, target, target, self.nobody).wait_recv()

    def add(self, target, *sources):
        total = sources[0][...].astype(f32)
        for source in sources[1:]:
            total = total + source[...].astype(f32)
        target[...] = total.astype(target.dtype)

    def stage(self, number):
        y, x, z, c = place()
        self.nobody = device(y, x, z, 1 - c)
        dp, dp_x, dp_y, dp_d = y * 2 + x, y * 2 + 1 - x, (1 - y) * 2 + x, (1 - y) * 2 + 1 - x
        to_x, to_y, to_c = device(y, 1 - x, z, c), device(1 - y, x, z, c), device(y, x, z, 1 - c)
        part, half = self.part, self.half
        if number == 0:
            for msg, at in ((0, dp_d), (1, dp_x), (2, dp_y), (3, dp)):
                self.push(msg, part.at[at, :, 1 - c], half.at[at], to_c)
        elif number == 1:
            self.arrived(0, half.at[dp_d])
            self.add(half.at[dp_d], half.at[dp_d], part.at[dp_d, :, c])
            self.push(4, half.at[dp_d, pl.ds(0, 2)], self.diag.at[0], to_x)
            self.push(5, half.at[dp_d, pl.ds(2, 2)], self.diag.at[1], to_y)
            self.arrived(1, half.at[dp_x])
            self.add(half.at[dp_x], half.at[dp_x], part.at[dp_x, :, c])
            self.arrived(2, half.at[dp_y])
            self.add(half.at[dp_y], half.at[dp_y], part.at[dp_y, :, c])
        elif number == 2:
            self.arrived(5, self.diag.at[1])
            late = half.at[dp_x, pl.ds(2, 2)]
            self.add(late, late, self.diag.at[1])
            self.push(6, half.at[dp_x], self.side.at[0], to_x)
            self.arrived(4, self.diag.at[0])
            late = half.at[dp_y, pl.ds(0, 2)]
            self.add(late, late, self.diag.at[0])
            self.push(7, half.at[dp_y], self.side.at[1], to_y)
            self.arrived(3, half.at[dp])
            self.add(half.at[dp], half.at[dp], part.at[dp, :, c])
        elif number == 3:
            self.arrived(6, self.side.at[0])
            self.arrived(7, self.side.at[1])
            self.add(half.at[dp], half.at[dp], self.side.at[0], self.side.at[1])
            for k in (1, 2, 3):
                self.push(
                    7 + k, half.at[dp, (z + k) % 4], self.line.at[k - 1], device(y, x, (z + k) % 4, c)
                )
        elif number == 4:
            for k in (1, 2, 3):
                self.arrived(7 + k, self.line.at[k - 1])
            self.add(self.out, half.at[dp, z], self.line.at[0], self.line.at[1], self.line.at[2])
        elif number == 5:
            for copy in self.sent:
                copy.wait_send()


class Total:
    def __init__(self, value, out, bufs, send, recv, group):
        self.value, self.out, self.send, self.recv, self.group = value, out, send, recv, group
        self.mine, self.theirs = bufs
        self.sent = []

    copy = Gather.copy

    def stage(self, number):
        y, x, z, c = place()
        self.nobody = device(y, x, z, 1 - c)
        peers = [
            device(y, x, z, 1 - c),
            device(y, 1 - x, z, c),
            device(1 - y, x, z, c),
            device(y, x, z + 1 - 2 * (z % 2), c),
            device(y, x, (z + 2) % 4, c),
        ]
        mine, theirs = self.mine, self.theirs
        if number == 0:
            mine[0] = self.value[...]
        elif number <= 5:
            at = number - 1
            self.copy(at, mine.at[at], theirs.at[at], self.nobody).wait_recv()
            if number < 5:
                mine[number] = mine[at] + theirs[at]
            else:
                self.out[...] = mine[at] + theirs[at]
        if number < 5:
            copy = self.copy(number, mine.at[number], theirs.at[number], peers[number])
            copy.start()
            self.sent.append(copy)
        if number == 6:
            for copy in self.sent:
                copy.wait_send()


def in_turn(groups, last):
    for turn in range(len(groups) + last):
        for at, group in enumerate(groups):
            if 0 <= turn - at <= last:
                group.stage(turn - at)


def forward_kernel(fast, *refs):
    refs = list(refs)
    take = lambda count: [refs.pop(0) for _ in range(count)]
    cameras, tokens, features, cotangent = take(4)
    shards = take(5)
    b_query, b_value, b_out, gain_first, shift_first = take(5)
    b_up, b_down, gain_second, shift_second, b_feat = take(5)
    output, start_low, q_rows, k_rows, v_rows, dmix_high, dmix_low, dots = take(8)
    grad_first, probs, grad_down, grad_up, grad_out, sums, sums_up = take(7)
    w_feat, w_qkv = take(2) if fast else shards[:2]
    first, act, gin, work, mixed, mixed_low, inverse = take(7)
    normed_low, grad_branch, grad_att, q_cat, v_cat, k_cat, stage = take(7)
    prob_sem, stage_sem, load_sem = take(3)
    w_out, w_up, w_down = take(3) if fast else shards[2:]
    width = tokens.shape[1]
    hidden = w_up.shape[-1]
    if fast:
        send, recv, local = take(3)
        half = hidden // 256 * 128
        wholes = (w_feat, w_qkv, w_out, w_up, w_up, w_down, w_down)
        pieces = ((0, width), (0, 3 * width), (0, width)) + ((0, half), (half, hidden - half)) * 2
        gather = [
            Gather(shards[which], whole, cols, send, recv, local, i)
            for i, (which, whole, cols) in enumerate(zip((0, 1, 2, 3, 3, 4, 4), wholes, pieces))
        ]
        greet()
        turns(gather, (0, 0), (0, 1))
    heads = width // HEAD
    pairs = heads // 2
    limit = 2 + CAM_LEN * cameras[0]

    def rows_of(step):
        return pl.ds(pl.multiple_of(step * STEP, 16), STEP)

    def row_ids(step):
        return step * STEP + lax.broadcasted_iota(jnp.int32, (STEP, 1), 0)

    loads = [
        pltpu.make_async_copy(
            source.at[pl.ds(0, ROWS), :], act.at[:, pl.ds(i * width, width)], load_sem.at[i]
        )
        for i, source in enumerate((features, tokens))
    ]
    for load in loads:
        load.start()
    if fast:
        turns(gather, (1, 0), (1, 1), (0, 2), (0, 3), (0, 4), (0, 5), (0, 6), (2, 0), (2, 1))
        turns(gather, (3, 0), (3, 1), (4, 0), (4, 1), (1, 2))
    for load in loads:
        load.wait()

    def project(step, carry):
        rows = rows_of(step)
        ids = row_ids(step)
        valid = ids < limit
        camera = jnp.logical_and(ids >= 2, valid)
        memory = dg(act[rows, :width], matrix(w_feat), 1, 0) + b_feat[...]
        start = act[rows, width : 2 * width].astype(f32) + jnp.where(camera, memory, 0.0)
        first[rows, :] = start
        low = start.astype(bf16)
        start_low[rows, :] = low
        joined = dg(low, matrix(w_qkv), 1, 0)
        q_rows[rows, :] = ((joined[:, :width] + b_query[...]) * 0.125).astype(bf16)
        keys = joined[:, width : 2 * width]
        lead = k_rows[0:16, :][0:1].astype(f32)
        k_rows[rows, :] = jnp.where(valid, keys, lead).astype(bf16)
        v_rows[rows, :] = (joined[:, 2 * width :] + b_value[...]).astype(bf16)
        return carry

    lax.fori_loop(0, 4, project, 0)

    lane_valid = lax.broadcasted_iota(jnp.int32, (1, ROWS), 1) < limit

    def prob_copy(pair, side):
        source = act if side == 0 else gin
        at = pl.ds(pl.multiple_of(lax.rem(pair, 2) * 1280, 128), 1280)
        return pltpu.make_async_copy(
            source.at[:, at], probs.at[2 * pair + side], prob_sem.at[2 * lax.rem(pair, 2) + side]
        )

    def attend(pair, carry):
        lanes = pl.ds(pl.multiple_of(pair * 128, 128), 128)
        if fast:
            for at_pair in range(pairs):

                @pl.when(pair == at_pair)
                def _():
                    turns(gather, (1, at_pair + 3), (2, at_pair + 2))
                    if at_pair:
                        turns(gather, (3, at_pair + 1))

        @pl.when(pair >= 2)
        def _():
            prob_copy(pair - 2, 0).wait()
            prob_copy(pair - 2, 1).wait()

        queries = q_rows[:, lanes].astype(f32).T * LOG2E
        high, low = split_low(queries)
        none = jnp.zeros((HEAD, ROWS), bf16)
        values = jnp.where(lane_valid, v_rows[:, lanes].astype(f32).T, 0.0).astype(bf16)
        ones = jnp.broadcast_to(jnp.where(lane_valid, 1.0, 0.0), (HEAD, ROWS)).astype(bf16)
        for side in range(2):
            own = slice(side * HEAD, side * HEAD + HEAD)
            other = slice((1 - side) * HEAD, (1 - side) * HEAD + HEAD)
            q_cat[side, own, :] = high[own]
            q_cat[side, other, :] = none
            q_cat[side, 128 + side * HEAD : 128 + side * HEAD + HEAD, :] = low[own]
            q_cat[side, 128 + (1 - side) * HEAD : 128 + (1 - side) * HEAD + HEAD, :] = none
            v_cat[side, :HEAD, :] = values[own]
            v_cat[side, HEAD:, :] = ones
        keys = k_rows[:, lanes]
        k_cat[:, :128] = keys
        k_cat[:, 128:] = keys
        base = lax.rem(pair, 2) * 1280
        jobs = [(side, at, size) for side in range(2) for at, size in QBLOCKS]
        peak = {}

        def score(job, at_key, keys_here):
            side, at, size = jobs[job]
            here = slice(at_key, at_key + keys_here)
            scores = dg(k_cat[here, :], q_cat[side, :, at : at + size], 1, 0)
            work[job % 3 * 4 + at_key // STEP, :, :size] = scores
            high_here = jnp.max(scores, axis=0, keepdims=True)
            peak[job] = jnp.maximum(peak[job], high_here) if job in peak else high_here

        def weigh(job, at_key, keys_here):
            side, at, size = jobs[job]
            slot = act if side == 0 else gin
            here = slice(at_key, at_key + keys_here)
            slot[here, pl.ds(pl.multiple_of(base + at, 128), size)] = jnp.exp2(
                work[job % 3 * 4 + at_key // STEP, :, :size] - peak[job]
            ).astype(bf16)

        def mix(job):
            side, at, size = jobs[job]
            slot = act if side == 0 else gin
            weight = slot[:, pl.ds(pl.multiple_of(base + at, 128), size)]
            summed = dg(v_cat[side], weight, 1, 0)
            inv = 1.0 / summed[HEAD : HEAD + 1]
            mixed[pl.ds(pl.multiple_of(pair * 128 + side * HEAD, 8), HEAD), at : at + size] = (
                summed[:HEAD] * inv
            )
            inverse[2 * pair + side, :, at : at + size] = inv

        parts = chunks(ROWS, STEP)
        for job in (0, 1):
            for part in parts:
                score(job, *part)
        for job in range(len(jobs)):
            for part in parts:
                if job + 2 < len(jobs):
                    score(job + 2, *part)
                weigh(job, *part)
            if job >= 2:
                mix(job - 2)
            if job == len(QBLOCKS) - 1:
                prob_copy(pair, 0).start()
        mix(len(jobs) - 2)
        mix(len(jobs) - 1)
        prob_copy(pair, 1).start()
        return carry

    lax.fori_loop(0, pairs, attend, 0)
    for pair in (pairs - 2, pairs - 1):
        for side in range(2):
            prob_copy(pair, side).wait()

    if fast:
        turns(gather, (2, 6), (3, 5), (4, 2))
    mixed_low[...] = mixed[...].astype(bf16)
    for at, size in chunks(width, 256):
        cols = slice(at, at + size)
        first[:, cols] += dg(mixed_low[...], matrix(w_out, cols), 0, 0) + b_out[:, cols]
    sums[...] = jnp.zeros_like(sums)
    sums_up[...] = jnp.zeros_like(sums_up)
    cuts = chunks(hidden, 512)
    if fast:
        turns(gather, (3, 6), (4, 3), (4, 4), (4, 5), (4, 6), *[(5, i) for i in range(7)])

    def feed(step, carry):
        rows = rows_of(step)
        valid = row_ids(step) < limit
        unit_first, scale_first = norm_parts(first[rows, :])
        normed = unit_first * gain_first[...] + shift_first[...]
        low = normed.astype(bf16)
        normed_low[rows, :] = low
        for at, size in cuts:
            cols = slice(at, at + size)
            inner = dg(low, matrix(w_up, cols), 1, 0) + b_up[:, cols]
            square = inner * inner
            half = 0.5 + 0.5 * jnp.tanh(inner * (GELU_C + (GELU_C * GELU_A) * square))
            value = inner * half
            act[rows, cols] = value.astype(bf16)
            slope = half + value * (1.0 - half) * (2 * GELU_C + (6 * GELU_C * GELU_A) * square)
            for cut, wide in chunks(size, 256):
                work[(at + cut) // 256, :, :wide] = slope[:, cut : cut + wide]
        branch = dg(act[rows, :], matrix(w_down), 1, 1) + b_down[...]
        unit_second, scale_second = norm_parts(normed + branch)
        final = unit_second * gain_second[...] + shift_second[...]
        output[rows, :] = jnp.where(valid, final, 0.0).astype(bf16)
        grad = jnp.where(valid, cotangent[rows, :].astype(f32), 0.0)
        sums[0] += fold(grad * unit_second)
        sums[1] += fold(grad)
        grad_second = norm_back(grad, unit_second, scale_second, gain_second[...])
        low_branch = grad_second.astype(bf16)
        grad_branch[rows, :] = low_branch
        sums[2] += fold(low_branch.astype(f32))
        for at, size in cuts:
            cols = slice(at, at + size)
            slope = [work[(at + cut) // 256, :, :wide] for cut, wide in chunks(size, 256)]
            low_inner = (
                dg(low_branch, matrix(w_down, cols), 1, 0) * jnp.concatenate(slope, axis=1)
            ).astype(bf16)
            gin[rows, cols] = low_inner
            sums_up[:, cols] += fold(low_inner.astype(f32))
        grad_normed = grad_second + dg(gin[rows, :], matrix(w_up), 1, 1)
        sums[3] += fold(grad_normed * unit_first)
        sums[4] += fold(grad_normed)
        back = norm_back(grad_normed, unit_first, scale_first, gain_first[...])
        grad_first[rows, :] = back
        low_att = back.astype(bf16)
        grad_att[rows, :] = low_att
        sums[5] += fold(low_att.astype(f32))
        return carry

    lax.fori_loop(0, 4, feed, 0)
    output[ROWS:, :] = jnp.zeros((SLOTS - ROWS, width), bf16)

    for at, size in QBLOCKS:
        cols = slice(at, at + size)
        grad_mixed = dg(matrix(w_out), grad_att[cols, :], 1, 1).astype(bf16).astype(f32)
        scaled = grad_mixed.reshape(heads, HEAD, size) * inverse[:, :, cols]
        dots[:, :, cols] = jnp.sum(
            scaled * mixed[:, cols].reshape(heads, HEAD, size), axis=1, keepdims=True
        )
        high, low = split_low(scaled.reshape(width, size))
        dmix_high[:, cols] = high
        dmix_low[:, cols] = low

    def weight_copy(target, at, size, slot):
        return pltpu.make_async_copy(
            stage.at[slot, :, pl.ds(0, size)], target.at[:, pl.ds(at, size)], stage_sem.at[slot]
        )

    pending = {}
    for turn, (left, right, target, (at, size)) in enumerate(
        [(grad_branch, act, grad_down, cut) for cut in cuts]
        + [(normed_low, gin, grad_up, cut) for cut in cuts]
    ):
        slot = turn % 2
        if slot in pending:
            pending[slot].wait()
        stage[slot, :, 0:size] = dg(left[...], right[:, at : at + size], 0, 0).astype(bf16)
        pending[slot] = weight_copy(target, at, size, slot)
        pending[slot].start()
    grad_out[...] = dg(mixed_low[...], grad_att[...], 1, 0).astype(bf16)
    for copy in pending.values():
        copy.wait()


def shaped(shape, dtype):
    return jax.ShapeDtypeStruct(shape, dtype)


def forward_call(fast, cameras, tokens, features, cotangent, weights, biases):
    width = tokens.shape[1]
    hidden = weights[3].shape[1]
    heads = width // HEAD
    outs = (
        shaped((SLOTS, width), bf16),
        shaped((ROWS, width), bf16),
        shaped((ROWS, width), bf16),
        shaped((ROWS, width), bf16),
        shaped((ROWS, width), bf16),
        shaped((width, ROWS), bf16),
        shaped((width, ROWS), bf16),
        shaped((heads, 1, ROWS), f32),
        shaped((ROWS, width), f32),
        shaped((heads, ROWS, 1280), bf16),
        shaped((width, hidden), bf16),
        shaped((width, hidden), bf16),
        shaped((width, width), bf16),
        shaped((6, 8, width), f32),
        shaped((8, hidden), f32),
    )
    wholes = [(4, 4, 2) + w.shape for w in weights]
    if fast:
        outs += tuple(shaped(whole, bf16) for whole in wholes[:2])
    vmem = pl.BlockSpec(memory_space=pltpu.VMEM)
    hbm = pl.BlockSpec(memory_space=pl.ANY)
    return pl.pallas_call(
        functools.partial(forward_kernel, fast),
        out_shape=outs,
        in_specs=[pl.BlockSpec(memory_space=pltpu.SMEM)] + [hbm] * 2 + [vmem] * 16,
        out_specs=tuple(hbm if i in (9, 10, 11) else vmem for i in range(len(outs))),
        scratch_shapes=[
            pltpu.VMEM((ROWS, width), f32),
            pltpu.VMEM((ROWS, hidden), bf16),
            pltpu.VMEM((ROWS, hidden), bf16),
            pltpu.VMEM((max(12, -(-hidden // 256)), STEP, 256), f32),
            pltpu.VMEM((width, ROWS), f32),
            pltpu.VMEM((width, ROWS), bf16),
            pltpu.VMEM((heads, 1, ROWS), f32),
            pltpu.VMEM((ROWS, width), bf16),
            pltpu.VMEM((ROWS, width), bf16),
            pltpu.VMEM((ROWS, width), bf16),
            pltpu.VMEM((2, 256, ROWS), bf16),
            pltpu.VMEM((2, 128, ROWS), bf16),
            pltpu.VMEM((ROWS, 256), bf16),
            pltpu.VMEM((2, width, 512), bf16),
            pltpu.SemaphoreType.DMA((4,)),
            pltpu.SemaphoreType.DMA((2,)),
            pltpu.SemaphoreType.DMA((2,)),
        ]
        + fast
        * (
            [pltpu.VMEM(whole, bf16) for whole in wholes[2:]]
            + [
                pltpu.SemaphoreType.DMA((7, GATHER_MSGS)),
                pltpu.SemaphoreType.DMA((7, GATHER_MSGS)),
                pltpu.SemaphoreType.DMA((7,)),
            ]
        ),
        compiler_params=pltpu.CompilerParams(
            vmem_limit_bytes=62 * MIB,
            collective_id=0 if fast else None,
            has_side_effects=fast,
        ),
        name="layer_forward",
    )(cameras, tokens, features, cotangent, *weights, *biases)


def backward_kernel(
    cameras,
    features,
    q_rows,
    k_rows,
    v_rows,
    dmix_high,
    dmix_low,
    dots,
    start_low,
    grad_first,
    probs,
    w_qkv,
    w_feat,
    grad_tokens,
    grad_features,
    grad_qkv,
    grad_feat,
    sums,
    feats,
    weights,
    grad_scores,
    joined,
    d_cat,
    d_rows,
    v_cat,
    k_turned,
    grad_memory,
    prob_sem,
    load_sem,
):
    width = q_rows.shape[1]
    heads = width // HEAD
    pairs = heads // 2
    limit = 2 + CAM_LEN * cameras[0]

    def prob_copy(pair, side):
        slot = 2 * lax.rem(pair, 2) + side
        return pltpu.make_async_copy(
            probs.at[2 * pair + side], weights.at[slot], prob_sem.at[slot]
        )

    for side in range(2):
        prob_copy(0, side).start()
    load = pltpu.make_async_copy(features.at[pl.ds(0, ROWS), :], feats, load_sem)
    load.start()
    sums[...] = jnp.zeros_like(sums)
    lane_valid = lax.broadcasted_iota(jnp.int32, (1, ROWS), 1) < limit
    row_valid = lax.broadcasted_iota(jnp.int32, (ROWS, 1), 0) < limit

    def attend_back(pair, carry):
        lanes = pl.ds(pl.multiple_of(pair * 128, 128), 128)

        @pl.when(pair + 1 < pairs)
        def _():
            prob_copy(pair + 1, 0).start()
            prob_copy(pair + 1, 1).start()

        both = pl.ds(pl.multiple_of(pair * 128, 128), 128)
        high = dmix_high[both, :]
        low = dmix_low[both, :]
        none = jnp.zeros((HEAD, ROWS), bf16)
        for side in range(2):
            own = slice(side * HEAD, side * HEAD + HEAD)
            mine, its = side * HEAD, (1 - side) * HEAD
            d_cat[side, mine : mine + HEAD, :] = high[own]
            d_cat[side, its : its + HEAD, :] = none
            d_cat[side, 128 + mine : 128 + mine + HEAD, :] = low[own]
            d_cat[side, 128 + its : 128 + its + HEAD, :] = none
        d_rows[:, :128] = high.astype(f32).T.astype(bf16)
        d_rows[:, 128:] = low.astype(f32).T.astype(bf16)
        values = v_rows[:, lanes]
        v_cat[:, :128] = values
        v_cat[:, 128:] = values
        k_turned[...] = jnp.where(lane_valid, k_rows[:, lanes].astype(f32).T, 0.0).astype(bf16)
        base = 2 * lax.rem(pair, 2)
        jobs = [(side, at, size) for side in range(2) for at, size in QBLOCKS]
        parts = chunks(ROWS, STEP)
        turned = {0: [], 1: []}
        wide = {}

        def slope(job):
            side, at, size = jobs[job]
            offset = dots[2 * pair + side, :, at : at + size]
            for at_key, keys_here in parts:
                here = slice(at_key, at_key + keys_here)
                grad = dg(v_cat[here, :], d_cat[side, :, at : at + size], 1, 0) - offset
                weight = weights[base + side, here, at : at + size].astype(f32)
                grad_scores[side, here, at : at + size] = (weight * grad).astype(bf16)

        def queries(job):
            side, at, size = jobs[job]
            turned[side].append(
                dg(k_turned[...], grad_scores[side, :, at : at + size], 1, 0)[
                    side * HEAD : side * HEAD + HEAD
                ]
            )

        def spread(side, part):
            here = slice(part[0], part[0] + part[1])
            value = dg(weights[base + side, here, :ROWS], d_rows[...], 1, 0)
            value = value[:, :128] + value[:, 128:]
            key = dg(grad_scores[side, here, :ROWS], q_rows[:, lanes], 1, 0)
            wide[side, part] = (value, key)

        for side in range(2):
            prob_copy(pair, side).wait()
        for job in range(len(jobs)):
            slope(job)
            if job >= 1:
                queries(job - 1)
            if job > len(QBLOCKS):
                side_job = job - len(QBLOCKS) - 1
                if side_job < len(parts):
                    spread(0, parts[side_job])
        queries(len(jobs) - 1)
        first_lane = lax.broadcasted_iota(jnp.int32, (STEP, 128), 1) < HEAD
        for part in parts:
            spread(1, part)
            here = slice(part[0], part[0] + part[1])
            keep = row_valid[here]
            for which, at in ((0, 2 * width), (1, width)):
                value = jnp.where(first_lane, wide[0, part][which], wide[1, part][which])
                value = jnp.where(keep, value, 0.0).astype(bf16)
                joined[here, pl.ds(pl.multiple_of(at + pair * 128, 128), 128)] = value
        query = jnp.concatenate(
            [jnp.concatenate(turned[0], axis=1), jnp.concatenate(turned[1], axis=1)], axis=0
        )
        joined[:, lanes] = (query.astype(bf16).astype(f32).T * 0.125).astype(bf16)
        return carry

    lax.fori_loop(0, pairs, attend_back, 0)
    load.wait()

    def project_back(step, carry):
        rows = pl.ds(pl.multiple_of(step * STEP, 16), STEP)
        ids = step * STEP + lax.broadcasted_iota(jnp.int32, (STEP, 1), 0)
        camera = jnp.logical_and(ids >= 2, ids < limit)
        part = joined[rows, :]
        sums[0] += fold(part[:, :width].astype(f32))
        sums[1] += fold(part[:, 2 * width :].astype(f32))
        grad_start = grad_first[rows, :] + dg(part, w_qkv[...], 1, 1)
        grad_tokens[rows, :] = grad_start.astype(bf16)
        low = jnp.where(camera, grad_start, 0.0).astype(bf16)
        grad_memory[rows, :] = low
        sums[2] += fold(low.astype(f32))
        grad_features[rows, :] = dg(low, w_feat[...], 1, 1).astype(bf16)
        return carry

    lax.fori_loop(0, 4, project_back, 0)
    grad_tokens[ROWS:, :] = jnp.zeros((SLOTS - ROWS, width), bf16)
    grad_features[ROWS:, :] = jnp.zeros((SLOTS - ROWS, width), bf16)
    for at, size in chunks(3 * width, 512):
        cols = slice(at, at + size)
        grad_qkv[:, cols] = dg(start_low[...], joined[:, cols], 0, 0).astype(bf16)
    grad_feat[...] = dg(feats[...], grad_memory[...], 0, 0).astype(bf16)


def backward_call(cameras, features, saved, w_qkv, w_feat):
    width = features.shape[1]
    heads = width // HEAD
    outs = (
        shaped((SLOTS, width), bf16),
        shaped((SLOTS, width), bf16),
        shaped((width, 3 * width), bf16),
        shaped((width, width), bf16),
        shaped((3, 8, width), f32),
    )
    vmem = pl.BlockSpec(memory_space=pltpu.VMEM)
    hbm = pl.BlockSpec(memory_space=pl.ANY)
    return pl.pallas_call(
        backward_kernel,
        out_shape=outs,
        in_specs=[pl.BlockSpec(memory_space=pltpu.SMEM), hbm] + [vmem] * 8 + [hbm] + [vmem] * 2,
        out_specs=(vmem,) * 5,
        scratch_shapes=[
            pltpu.VMEM((ROWS, width), bf16),
            pltpu.VMEM((4, ROWS, 1280), bf16),
            pltpu.VMEM((2, ROWS, 1280), bf16),
            pltpu.VMEM((ROWS, 3 * width), bf16),
            pltpu.VMEM((2, 256, ROWS), bf16),
            pltpu.VMEM((ROWS, 256), bf16),
            pltpu.VMEM((ROWS, 256), bf16),
            pltpu.VMEM((128, ROWS), bf16),
            pltpu.VMEM((ROWS, width), bf16),
            pltpu.SemaphoreType.DMA((4,)),
            pltpu.SemaphoreType.DMA(()),
        ],
        compiler_params=pltpu.CompilerParams(vmem_limit_bytes=62 * MIB),
        name="layer_backward",
    )(cameras, features, *saved, w_qkv, w_feat)


def reduce_bufs(columns, rows):
    return [
        pltpu.VMEM((4, 4, rows, columns), bf16),
        pltpu.VMEM((2, 2, rows, columns), bf16),
        pltpu.VMEM((2, 4, rows, columns), bf16),
        pltpu.VMEM((3, rows, columns), bf16),
    ]


def reduce_kernel(*refs):
    parts, small, outs, small_out, bufs = refs[:5], refs[5], refs[6:11], refs[11], refs[12:-2]
    send, recv = refs[-2:]
    greet()
    groups = [
        Reduce(parts[i], outs[i], bufs[4 * i : 4 * i + 4], send, recv, i) for i in range(5)
    ]
    groups.append(Total(small, small_out, bufs[20:22], send, recv, 5))
    in_turn(groups, 6)


def reduce_call(grads, small):
    vmem = pl.BlockSpec(memory_space=pltpu.VMEM)
    rows = grads[0].shape[0] // 32
    parts = [grad.reshape(4, 4, 2, rows, grad.shape[1]) for grad in grads]
    bufs = [buf for grad in grads for buf in reduce_bufs(grad.shape[1], rows)]
    bufs += [pltpu.VMEM((5,) + small.shape, f32)] * 2
    return pl.pallas_call(
        reduce_kernel,
        out_shape=tuple(shaped((rows, grad.shape[1]), f32) for grad in grads)
        + (shaped(small.shape, f32),),
        in_specs=[vmem] * 6,
        out_specs=(vmem,) * 6,
        scratch_shapes=bufs
        + [pltpu.SemaphoreType.DMA((6, GATHER_MSGS)), pltpu.SemaphoreType.DMA((6, GATHER_MSGS))],
        compiler_params=pltpu.CompilerParams(
            collective_id=1, has_side_effects=True, vmem_limit_bytes=62 * MIB
        ),
        name="reduce_gradients",
    )(*parts, small)


AXES = ("dp", "fsdp")


def on_device(
    fast,
    tokens,
    features,
    cameras,
    cotangent,
    w_qkv,
    w_out,
    w_up,
    w_down,
    w_feat,
    *biases,
):
    width = tokens.shape[1]
    hidden = w_up.shape[1]
    biases = [bias.reshape(1, -1) for bias in biases]
    shards = (w_feat, w_qkv, w_out, w_up, w_down)
    weights = shards
    if not fast:
        weights = tuple(lax.all_gather(w, AXES, axis=0, tiled=True) for w in shards)
    (
        output,
        start_low,
        q_rows,
        k_rows,
        v_rows,
        dmix_high,
        dmix_low,
        dots,
        grad_first,
        probs,
        grad_down,
        grad_up,
        grad_out,
        sums,
        sums_up,
        *wholes,
    ) = forward_call(fast, cameras, tokens, features, cotangent, weights, biases)
    if fast:
        weights = [whole.reshape(width, -1) for whole in wholes]
    saved = (q_rows, k_rows, v_rows, dmix_high, dmix_low, dots, start_low, grad_first, probs)
    grad_tokens, grad_features, grad_qkv, grad_feat, sums_back = backward_call(
        cameras, features, saved, weights[1], weights[0]
    )
    grads = (grad_down, grad_up, grad_out, grad_qkv, grad_feat)
    small = jnp.concatenate(
        [
            jnp.sum(sums, axis=1).reshape(-1),
            jnp.sum(sums_back, axis=1).reshape(-1),
            jnp.sum(sums_up, axis=0),
        ]
    )
    lines = -(-small.shape[0] // 1024) * 8
    small = jnp.pad(small, (0, lines * 128 - small.shape[0])).reshape(lines, 128)
    if fast:
        *grads, small = reduce_call(grads, small)
    else:
        grads = [
            lax.psum_scatter(
                lax.optimization_barrier(grad.astype(f32)), AXES, scatter_dimension=0, tiled=True
            )
            for grad in grads
        ]
        small = lax.psum(small, AXES)
    small = small.reshape(-1)
    rows = small[: 9 * width].reshape(9, width)
    grad_b_up = small[9 * width : 9 * width + hidden]
    grad_down, grad_up, grad_out, grad_qkv, grad_feat = grads
    return (
        output,
        grad_tokens,
        grad_features,
        grad_qkv,
        grad_out,
        grad_up,
        grad_down,
        grad_feat,
        rows[6],
        rows[7],
        rows[5],
        rows[3],
        rows[4],
        grad_b_up,
        rows[2],
        rows[0],
        rows[1],
        rows[8],
    )


def solution(mesh):
    split = P(AXES, None)
    fast = mesh.shape["dp"] == 4 and mesh.shape["fsdp"] == 8
    return jax.shard_map(
        functools.partial(on_device, fast),
        mesh=mesh,
        in_specs=(split, split, P(AXES), split) + (split,) * 5 + (P(),) * 10,
        out_specs=(split,) * 8 + (P(),) * 10,
        check_vma=False,
    )
```

```python
import functools

import jax
import jax.numpy as jnp
from jax import lax
from jax.experimental import pallas as pl
from jax.experimental.pallas import tpu as pltpu
from jax.sharding import PartitionSpec as P

HEAD = 64
SLOTS = 1280
CAM_LEN = 300
CAMS_MAX = 4
NORM_EPS = 1e-05
LOG2E = 1.4426950408889634
GELU_C = 0.7978845608028654
GELU_A = 0.044715

ROWS = -(-(2 + CAM_LEN * CAMS_MAX) // 64) * 64
STEP = ROWS // 4
QBLOCKS = [(at, min(256, ROWS - at)) for at in range(0, ROWS, 256)]
MIB = 2**20

bf16 = jnp.bfloat16
f32 = jnp.float32


def dg(left, right, over_left, over_right):
    return lax.dot_general(
        left, right, (((over_left,), (over_right,)), ((), ())), preferred_element_type=f32
    )


def chunks(total, width):
    return [(at, min(width, total - at)) for at in range(0, total, width)]


def norm_parts(value):
    average = jnp.mean(value, axis=-1, keepdims=True)
    centered = value - average
    variance = jnp.mean(centered * centered, axis=-1, keepdims=True)
    scale = lax.rsqrt(variance + NORM_EPS)
    return centered * scale, scale


def norm_back(grad, unit, scale, gain):
    inside = grad * gain
    one = jnp.mean(inside, axis=-1, keepdims=True)
    two = jnp.mean(inside * unit, axis=-1, keepdims=True)
    return scale * (inside - one - unit * two)


def line_of(ref, cols=slice(None)):
    return ref[cols].reshape(1, -1)


def fold(value):
    rows, width = value.shape
    return jnp.sum(value.reshape(rows // 8, 8, width), axis=0)


def split_low(value):
    high = value.astype(bf16)
    return high, (value - high.astype(f32)).astype(bf16)


MESH = pl.DeviceIdType.MESH
MESSAGES = 11


def place():
    dp = lax.axis_index("dp")
    fs = lax.axis_index("fsdp")
    return dp // 2, dp % 2, fs // 2, fs % 2


def device(y, x, z, c):
    return (y * 2 + x, z * 2 + c)


def neighbours():
    y, x, z, c = place()
    around = [device(y, x, (z + k) % 4, c) for k in (1, 2, 3)]
    return around + [
        device(y, 1 - x, z, c),
        device(1 - y, x, z, c),
        device(1 - y, 1 - x, z, c),
        device(y, x, z, 1 - c),
    ]


def greet():
    barrier = pltpu.get_barrier_semaphore()
    peers = neighbours()
    for peer in peers:
        pl.semaphore_signal(barrier, inc=1, device_id=peer, device_id_type=MESH)
    pl.semaphore_wait(barrier, len(peers))


class Gather:
    def __init__(self, shard, whole, cols, send, recv, local, group):
        self.shard, self.whole, self.cols, self.send, self.recv = shard, whole, cols, send, recv
        self.local, self.group = local, group

    def copy(self, msg, source, target, peer):
        return pltpu.make_async_remote_copy(
            src_ref=source,
            dst_ref=target,
            send_sem=self.send.at[self.group, msg],
            recv_sem=self.recv.at[self.group, msg],
            device_id=peer,
            device_id_type=MESH,
        )

    def stage(self, number):
        y, x, z, c = place()
        at_x, at_y, at_d, at = y * 2 + 1 - x, (1 - y) * 2 + x, (1 - y) * 2 + 1 - x, y * 2 + x
        to_x, to_y, to_c = device(y, 1 - x, z, c), device(1 - y, x, z, c), device(y, x, z, 1 - c)
        cols = pl.ds(*self.cols)
        whole = lambda dp, line, core: self.whole.at[dp, line, core, :, cols]
        own = whole(at, z, c)
        shard = self.shard.at[:, cols]
        every, low, high = slice(None), pl.ds(0, 2), pl.ds(2, 2)
        out = [(shard, own, device(y, x, (z + k) % 4, c)) for k in (1, 2, 3)] + [
            (part, part, peer)
            for part, peer in (
                (whole(at, every, c), to_x),
                (whole(at, every, c), to_y),
                (whole(at_x, low, c), to_y),
                (whole(at_y, high, c), to_x),
                (whole(at, every, c), to_c),
                (whole(at_x, every, c), to_c),
                (whole(at_y, every, c), to_c),
                (whole(at_d, every, c), to_c),
            )
        ]
        arrived = lambda msg, part: self.copy(msg, part, part, to_c).wait_recv()
        start = lambda msg: self.copy(msg, *out[msg]).start()
        if number == 0:
            keep = pltpu.make_async_copy(shard, own, self.local.at[self.group])
            keep.start()
            for msg in (0, 1, 2):
                start(msg)
            keep.wait()
        elif number == 1:
            for k in (1, 2, 3):
                arrived(k - 1, whole(at, (z + 4 - k) % 4, c))
            for msg in (3, 4, 7):
                start(msg)
        elif number == 2:
            arrived(3, whole(at_x, every, c))
            start(5)
            arrived(4, whole(at_y, every, c))
            for msg in (6, 8, 9):
                start(msg)
        elif number == 3:
            arrived(5, whole(at_d, low, c))
            arrived(6, whole(at_d, high, c))
            start(10)
        elif number == 4:
            for msg, dp in ((7, at), (8, at_x), (9, at_y), (10, at_d)):
                arrived(msg, whole(dp, every, 1 - c))
        elif number == 5:
            for msg, ends in enumerate(out):
                self.copy(msg, *ends).wait_send()


def turns(groups, *list_of):
    for stage, group in list_of:
        groups[group].stage(stage)


def matrix(ref, cols=slice(None)):
    value = ref[(slice(None),) * (len(ref.shape) - 1) + (cols,)]
    return value.reshape(-1, value.shape[-1])


class Reduce:
    def __init__(self, part, cols, write, bufs, mine, direct, send, recv, local, group):
        self.part, self.cols, self.write, self.mine, self.direct = part, cols, write, mine, direct
        self.send, self.recv, self.local, self.group = send, recv, local, group
        self.half, self.diag, self.side, self.line = bufs

    copy = Gather.copy

    def add(self, target, *sources):
        if len(sources) == 2:
            target[...] = sources[0][...] + sources[1][...]
            return
        total = sources[0][...].astype(f32)
        for source in sources[1:]:
            total = total + source[...].astype(f32)
        target[...] = total.astype(target.dtype)

    def stage(self, number):
        y, x, z, c = place()
        at_x, at_y, at_d, at = y * 2 + 1 - x, (1 - y) * 2 + x, (1 - y) * 2 + 1 - x, y * 2 + x
        to_x, to_y, to_c = device(y, 1 - x, z, c), device(1 - y, x, z, c), device(y, x, z, 1 - c)
        to_d = device(1 - y, 1 - x, z, c)
        cols = pl.ds(*self.cols)
        half, diag, side, line = self.half, self.diag, self.side, self.line
        if self.mine is None:
            mine = lambda dp: self.part.at[dp, :, c, :, cols]
        else:
            mine = lambda dp: self.mine.at[dp]
            fetch = lambda: pltpu.make_async_copy(
                self.part.at[:, :, c, :, cols], self.mine, self.local.at[self.group]
            )
        low, high = pl.ds(0, 2), pl.ds(2, 2)
        blocks = (at_d, at_x, at_y, at)
        out = [(self.part.at[dp, :, 1 - c, :, cols], half.at[dp], to_c) for dp in blocks]
        if self.direct:
            out += [
                (half.at[at_d], diag, to_d),
                None,
                (half.at[at_x], side.at[0], to_x),
                (half.at[at_y], side.at[1], to_y),
            ]
        else:
            out += [
                (half.at[at_d, low], diag.at[0], to_x),
                (half.at[at_d, high], diag.at[1], to_y),
                (half.at[at_x], side.at[0], to_x),
                (half.at[at_y], side.at[1], to_y),
            ]
        out += [
            (half.at[at, (z + k) % 4], line.at[k - 1], device(y, x, (z + k) % 4, c))
            for k in (1, 2, 3)
        ]
        arrived = lambda msg: self.copy(msg, *out[msg][1:2] * 2, to_c).wait_recv()
        start = lambda msg: self.copy(msg, *out[msg]).start()

        def halve(msg):
            self.copy(msg, half.at[blocks[msg]], half.at[blocks[msg]], to_c).wait_recv()
            self.add(half.at[blocks[msg]], half.at[blocks[msg]], mine(blocks[msg]))

        if number == 0:
            for msg in range(4):
                start(msg)
            if self.mine is not None:
                fetch().start()
        elif number == 1:
            if self.mine is not None:
                fetch().wait()
            halve(0)
            start(4)
            if not self.direct:
                start(5)
            halve(1)
            if self.direct:
                start(6)
            halve(2)
            if self.direct:
                start(7)
            halve(3)
        elif number == 2 and not self.direct:
            arrived(5)
            late = half.at[at_x, high]
            self.add(late, late, diag.at[1])
            start(6)
            arrived(4)
            late = half.at[at_y, low]
            self.add(late, late, diag.at[0])
            start(7)
        elif number == 3:
            own = half.at[at]
            if self.direct:
                arrived(4)
            arrived(6)
            arrived(7)
            self.add(own, own, side.at[0], side.at[1], *((diag,) if self.direct else ()))
            for k in (1, 2, 3):
                start(7 + k)
        elif number == 4:
            for k in (1, 2, 3):
                arrived(7 + k)
            total = half[at, z].astype(f32) + line[0].astype(f32)
            self.write(total + line[1].astype(f32) + line[2].astype(f32))
        elif number == 5:
            for msg, ends in enumerate(out):
                if ends is not None:
                    self.copy(msg, *ends).wait_send()


class Total:
    def __init__(self, value, out, bufs, send, recv, group):
        self.value, self.out, self.send, self.recv, self.group = value, out, send, recv, group
        self.line, self.plane, self.pair = bufs

    copy = Gather.copy

    def stage(self, number):
        y, x, z, c = place()
        at_x, at_y, at_d, at = y * 2 + 1 - x, (1 - y) * 2 + x, (1 - y) * 2 + 1 - x, y * 2 + x
        to_c = device(y, x, z, 1 - c)
        line, plane, pair = self.line, self.plane, self.pair
        out = [(line.at[z], device(y, x, (z + k) % 4, c)) for k in (1, 2, 3)] + [
            (plane.at[at], device(y, 1 - x, z, c)),
            (plane.at[at], device(1 - y, x, z, c)),
            (plane.at[at], device(1 - y, 1 - x, z, c)),
            (pair.at[c], to_c),
        ]
        came = [line.at[(z + 4 - k) % 4] for k in (1, 2, 3)]
        came += [plane.at[dp] for dp in (at_x, at_y, at_d)] + [pair.at[1 - c]]

        def start(msg):
            self.copy(msg, out[msg][0], out[msg][0], out[msg][1]).start()

        def arrived(msg):
            self.copy(msg, came[msg], came[msg], to_c).wait_recv()

        if number == 0:
            line[z] = self.value[...]
            for msg in (0, 1, 2):
                start(msg)
        elif number == 1:
            for msg in (0, 1, 2):
                arrived(msg)
            plane[at] = line[0] + line[1] + line[2] + line[3]
            for msg in (3, 4, 5):
                start(msg)
        elif number == 2:
            for msg in (3, 4, 5):
                arrived(msg)
            pair[c] = plane[0] + plane[1] + plane[2] + plane[3]
            start(6)
        elif number == 3:
            arrived(6)
            self.out[...] = pair[0] + pair[1]
        elif number == 5:
            for msg in range(7):
                self.copy(msg, out[msg][0], out[msg][0], out[msg][1]).wait_send()


def forward_kernel(fast, *refs):
    refs = list(refs)
    take = lambda count: [refs.pop(0) for _ in range(count)]
    cameras, tokens, features, cotangent = take(4)
    shards = take(5)
    b_query, b_value, b_out, gain_first, shift_first = take(5)
    b_up, b_down, gain_second, shift_second, b_feat = take(5)
    output, start_low, q_rows, k_rows, v_rows, dmix_high, dmix_low, dots = take(8)
    grad_first, probs, grad_down, grad_up, grad_out, small = take(6)
    w_feat, w_qkv = take(2) if fast else shards[:2]
    first, act, gin, work, mixed, mixed_low, inverse = take(7)
    normed_low, grad_branch, grad_att, q_cat, v_cat, k_cat, stage, sums, sums_up = take(9)
    prob_sem, stage_sem, load_sem = take(3)
    w_out, w_up, w_down = take(3) if fast else shards[2:]
    width = tokens.shape[1]
    hidden = w_up.shape[-1]
    if fast:
        send, recv, local = take(3)
        half = hidden // 256 * 128
        wholes = (w_feat, w_qkv, w_out, w_up, w_up, w_down, w_down)
        pieces = ((0, width), (0, 3 * width), (0, width)) + ((0, half), (half, hidden - half)) * 2
        gather = [
            Gather(shards[which], whole, cols, send, recv, local, i)
            for i, (which, whole, cols) in enumerate(zip((0, 1, 2, 3, 3, 4, 4), wholes, pieces))
        ]
        greet()
        turns(gather, (0, 0), (0, 1))
    heads = width // HEAD
    pairs = heads // 2
    limit = 2 + CAM_LEN * cameras[0]

    def rows_of(step):
        return pl.ds(pl.multiple_of(step * STEP, 16), STEP)

    def row_ids(step):
        return step * STEP + lax.broadcasted_iota(jnp.int32, (STEP, 1), 0)

    loads = [
        pltpu.make_async_copy(
            source.at[pl.ds(0, ROWS), :], act.at[:, pl.ds(i * width, width)], load_sem.at[i]
        )
        for i, source in enumerate((features, tokens))
    ]
    for load in loads:
        load.start()
    if fast:
        turns(gather, (1, 0), (1, 1), (0, 2), (0, 3), (0, 4), (0, 5), (0, 6), (2, 0), (2, 1))
        turns(gather, (3, 0), (3, 1), (4, 0), (4, 1), (1, 2))
    for load in loads:
        load.wait()

    def project(step, carry):
        rows = rows_of(step)
        ids = row_ids(step)
        valid = ids < limit
        camera = jnp.logical_and(ids >= 2, valid)
        memory = dg(act[rows, :width], matrix(w_feat), 1, 0) + line_of(b_feat)
        start = act[rows, width : 2 * width].astype(f32) + jnp.where(camera, memory, 0.0)
        first[rows, :] = start
        low = start.astype(bf16)
        start_low[rows, :] = low
        joined = dg(low, matrix(w_qkv), 1, 0)
        q_rows[rows, :] = ((joined[:, :width] + line_of(b_query)) * 0.125).astype(bf16)
        keys = joined[:, width : 2 * width]
        lead = k_rows[0:16, :][0:1].astype(f32)
        k_rows[rows, :] = jnp.where(valid, keys, lead).astype(bf16)
        v_rows[rows, :] = (joined[:, 2 * width :] + line_of(b_value)).astype(bf16)
        return carry

    lax.fori_loop(0, 4, project, 0)

    lane_valid = lax.broadcasted_iota(jnp.int32, (1, ROWS), 1) < limit

    def prob_copy(pair, side):
        source = act if side == 0 else gin
        at = pl.ds(pl.multiple_of(lax.rem(pair, 2) * 1280, 128), 1280)
        return pltpu.make_async_copy(
            source.at[:, at], probs.at[2 * pair + side], prob_sem.at[2 * lax.rem(pair, 2) + side]
        )

    def attend(pair, carry):
        lanes = pl.ds(pl.multiple_of(pair * 128, 128), 128)
        if fast:
            for at_pair in range(pairs):

                @pl.when(pair == at_pair)
                def _():
                    turns(gather, (1, at_pair + 3), (2, at_pair + 2))
                    if at_pair:
                        turns(gather, (3, at_pair + 1))

        @pl.when(pair >= 2)
        def _():
            prob_copy(pair - 2, 0).wait()
            prob_copy(pair - 2, 1).wait()

        queries = q_rows[:, lanes].astype(f32).T * LOG2E
        high, low = split_low(queries)
        none = jnp.zeros((HEAD, ROWS), bf16)
        values = jnp.where(lane_valid, v_rows[:, lanes].astype(f32).T, 0.0).astype(bf16)
        ones = jnp.broadcast_to(jnp.where(lane_valid, 1.0, 0.0), (HEAD, ROWS)).astype(bf16)
        for side in range(2):
            own = slice(side * HEAD, side * HEAD + HEAD)
            other = slice((1 - side) * HEAD, (1 - side) * HEAD + HEAD)
            q_cat[side, own, :] = high[own]
            q_cat[side, other, :] = none
            q_cat[side, 128 + side * HEAD : 128 + side * HEAD + HEAD, :] = low[own]
            q_cat[side, 128 + (1 - side) * HEAD : 128 + (1 - side) * HEAD + HEAD, :] = none
            v_cat[side, :HEAD, :] = values[own]
            v_cat[side, HEAD:, :] = ones
        keys = k_rows[:, lanes]
        k_cat[:, :128] = keys
        k_cat[:, 128:] = keys
        base = lax.rem(pair, 2) * 1280
        jobs = [(side, at, size) for side in range(2) for at, size in QBLOCKS]
        peak = {}

        def score(job, at_key, keys_here):
            side, at, size = jobs[job]
            here = slice(at_key, at_key + keys_here)
            scores = dg(k_cat[here, :], q_cat[side, :, at : at + size], 1, 0)
            work[job % 3 * 4 + at_key // STEP, :, :size] = scores
            high_here = jnp.max(scores, axis=0, keepdims=True)
            peak[job] = jnp.maximum(peak[job], high_here) if job in peak else high_here

        def weigh(job, at_key, keys_here):
            side, at, size = jobs[job]
            slot = act if side == 0 else gin
            here = slice(at_key, at_key + keys_here)
            slot[here, pl.ds(pl.multiple_of(base + at, 128), size)] = jnp.exp2(
                work[job % 3 * 4 + at_key // STEP, :, :size] - peak[job]
            ).astype(bf16)

        def mix(job):
            side, at, size = jobs[job]
            slot = act if side == 0 else gin
            weight = slot[:, pl.ds(pl.multiple_of(base + at, 128), size)]
            summed = dg(v_cat[side], weight, 1, 0)
            inv = 1.0 / summed[HEAD : HEAD + 1]
            mixed[pl.ds(pl.multiple_of(pair * 128 + side * HEAD, 8), HEAD), at : at + size] = (
                summed[:HEAD] * inv
            )
            inverse[2 * pair + side, :, at : at + size] = inv

        parts = chunks(ROWS, STEP)
        for job in (0, 1):
            for part in parts:
                score(job, *part)
        for job in range(len(jobs)):
            for part in parts:
                if job + 2 < len(jobs):
                    score(job + 2, *part)
                weigh(job, *part)
            if job >= 2:
                mix(job - 2)
            if job == len(QBLOCKS) - 1:
                prob_copy(pair, 0).start()
        mix(len(jobs) - 2)
        mix(len(jobs) - 1)
        prob_copy(pair, 1).start()
        return carry

    lax.fori_loop(0, pairs, attend, 0)
    for pair in (pairs - 2, pairs - 1):
        for side in range(2):
            prob_copy(pair, side).wait()

    if fast:
        turns(gather, (2, 6), (3, 5), (4, 2))
    mixed_low[...] = mixed[...].astype(bf16)
    for at, size in chunks(width, 256):
        cols = slice(at, at + size)
        first[:, cols] += dg(mixed_low[...], matrix(w_out, cols), 0, 0) + line_of(b_out, cols)
    sums[...] = jnp.zeros_like(sums)
    sums_up[...] = jnp.zeros_like(sums_up)
    cuts = chunks(hidden, 512)
    if fast:
        turns(gather, (3, 6), (4, 3), (4, 4), (4, 5), (4, 6), *[(5, i) for i in range(7)])

    def feed(step, carry):
        rows = rows_of(step)
        valid = row_ids(step) < limit
        unit_first, scale_first = norm_parts(first[rows, :])
        normed = unit_first * line_of(gain_first) + line_of(shift_first)
        low = normed.astype(bf16)
        normed_low[rows, :] = low
        for at, size in cuts:
            cols = slice(at, at + size)
            inner = dg(low, matrix(w_up, cols), 1, 0) + line_of(b_up, cols)
            square = inner * inner
            half = 0.5 + 0.5 * jnp.tanh(inner * (GELU_C + (GELU_C * GELU_A) * square))
            value = inner * half
            act[rows, cols] = value.astype(bf16)
            slope = half + value * (1.0 - half) * (2 * GELU_C + (6 * GELU_C * GELU_A) * square)
            for cut, wide in chunks(size, 256):
                work[(at + cut) // 256, :, :wide] = slope[:, cut : cut + wide]
        branch = dg(act[rows, :], matrix(w_down), 1, 1) + line_of(b_down)
        unit_second, scale_second = norm_parts(normed + branch)
        final = unit_second * line_of(gain_second) + line_of(shift_second)
        output[rows, :] = jnp.where(valid, final, 0.0).astype(bf16)
        grad = jnp.where(valid, cotangent[rows, :].astype(f32), 0.0)
        sums[0] += fold(grad * unit_second)
        sums[1] += fold(grad)
        grad_second = norm_back(grad, unit_second, scale_second, line_of(gain_second))
        low_branch = grad_second.astype(bf16)
        grad_branch[rows, :] = low_branch
        sums[2] += fold(low_branch.astype(f32))
        for at, size in cuts:
            cols = slice(at, at + size)
            slope = [work[(at + cut) // 256, :, :wide] for cut, wide in chunks(size, 256)]
            low_inner = (
                dg(low_branch, matrix(w_down, cols), 1, 0) * jnp.concatenate(slope, axis=1)
            ).astype(bf16)
            gin[rows, cols] = low_inner
            sums_up[:, cols] += fold(low_inner.astype(f32))
        grad_normed = grad_second + dg(gin[rows, :], matrix(w_up), 1, 1)
        sums[3] += fold(grad_normed * unit_first)
        sums[4] += fold(grad_normed)
        back = norm_back(grad_normed, unit_first, scale_first, line_of(gain_first))
        grad_first[rows, :] = back
        low_att = back.astype(bf16)
        grad_att[rows, :] = low_att
        sums[5] += fold(low_att.astype(f32))
        return carry

    lax.fori_loop(0, 4, feed, 0)
    small[...] = jnp.zeros_like(small)
    for i in range(6):
        small[i : i + 1, :] = jnp.sum(sums[i], axis=0, keepdims=True)
    for i, (at, size) in enumerate(chunks(hidden, width)):
        small[6 + i : 7 + i, :size] = jnp.sum(sums_up[:, at : at + size], axis=0, keepdims=True)
    output[ROWS:, :] = jnp.zeros((SLOTS - ROWS, width), bf16)

    for at, size in QBLOCKS:
        cols = slice(at, at + size)
        grad_mixed = dg(matrix(w_out), grad_att[cols, :], 1, 1).astype(bf16).astype(f32)
        scaled = grad_mixed.reshape(heads, HEAD, size) * inverse[:, :, cols]
        dots[:, :, cols] = jnp.sum(
            scaled * mixed[:, cols].reshape(heads, HEAD, size), axis=1, keepdims=True
        )
        high, low = split_low(scaled.reshape(width, size))
        dmix_high[:, cols] = high
        dmix_low[:, cols] = low

    def weight_copy(target, at, size, slot):
        return pltpu.make_async_copy(
            stage.at[slot, :, pl.ds(0, size)], target.at[:, pl.ds(at, size)], stage_sem.at[slot]
        )

    pending = {}
    for turn, (left, over, right, target, (at, size)) in enumerate(
        [(grad_branch, 0, act, grad_down, cut) for cut in cuts]
        + [(normed_low, 0, gin, grad_up, cut) for cut in cuts]
        + [(mixed_low, 1, grad_att, grad_out, (0, width))]
    ):
        slot = turn % 2
        if slot in pending:
            pending[slot].wait()
        stage[slot, :, 0:size] = dg(left[...], right[:, at : at + size], over, 0).astype(bf16)
        pending[slot] = weight_copy(target, at, size, slot)
        pending[slot].start()
    for copy in pending.values():
        copy.wait()


def shaped(shape, dtype):
    return jax.ShapeDtypeStruct(shape, dtype)


def forward_call(fast, cameras, tokens, features, cotangent, weights, biases):
    width = tokens.shape[1]
    hidden = weights[3].shape[1]
    heads = width // HEAD
    outs = (
        shaped((SLOTS, width), bf16),
        shaped((ROWS, width), bf16),
        shaped((ROWS, width), bf16),
        shaped((ROWS, width), bf16),
        shaped((ROWS, width), bf16),
        shaped((width, ROWS), bf16),
        shaped((width, ROWS), bf16),
        shaped((heads, 1, ROWS), f32),
        shaped((ROWS, width), f32),
        shaped((heads, ROWS, 1280), bf16),
        shaped((width, hidden), bf16),
        shaped((width, hidden), bf16),
        shaped((width, width), bf16),
        shaped((-(-(6 + -(-hidden // width)) // 8) * 8, width), f32),
    )
    wholes = [(4, 4, 2) + w.shape for w in weights]
    if fast:
        outs += tuple(shaped(whole, bf16) for whole in wholes[:2])
    vmem = pl.BlockSpec(memory_space=pltpu.VMEM)
    hbm = pl.BlockSpec(memory_space=pl.ANY)
    return pl.pallas_call(
        functools.partial(forward_kernel, fast),
        out_shape=outs,
        in_specs=[pl.BlockSpec(memory_space=pltpu.SMEM)] + [hbm] * 2 + [vmem] * 16,
        out_specs=tuple(hbm if i in (9, 10, 11, 12) else vmem for i in range(len(outs))),
        scratch_shapes=[
            pltpu.VMEM((ROWS, width), f32),
            pltpu.VMEM((ROWS, hidden), bf16),
            pltpu.VMEM((ROWS, hidden), bf16),
            pltpu.VMEM((max(12, -(-hidden // 256)), STEP, 256), f32),
            pltpu.VMEM((width, ROWS), f32),
            pltpu.VMEM((width, ROWS), bf16),
            pltpu.VMEM((heads, 1, ROWS), f32),
            pltpu.VMEM((ROWS, width), bf16),
            pltpu.VMEM((ROWS, width), bf16),
            pltpu.VMEM((ROWS, width), bf16),
            pltpu.VMEM((2, 256, ROWS), bf16),
            pltpu.VMEM((2, 128, ROWS), bf16),
            pltpu.VMEM((ROWS, 256), bf16),
            pltpu.VMEM((2, width, 512), bf16),
            pltpu.VMEM((6, 8, width), f32),
            pltpu.VMEM((8, hidden), f32),
            pltpu.SemaphoreType.DMA((4,)),
            pltpu.SemaphoreType.DMA((2,)),
            pltpu.SemaphoreType.DMA((2,)),
        ]
        + fast
        * (
            [pltpu.VMEM(whole, bf16) for whole in wholes[2:]]
            + [
                pltpu.SemaphoreType.DMA((7, MESSAGES)),
                pltpu.SemaphoreType.DMA((7, MESSAGES)),
                pltpu.SemaphoreType.DMA((7,)),
            ]
        ),
        compiler_params=pltpu.CompilerParams(
            vmem_limit_bytes=62 * MIB,
            collective_id=0 if fast else None,
            has_side_effects=fast,
        ),
        name="layer_forward",
    )(cameras, tokens, features, cotangent, *weights, *biases)


def reduce_plan(width, hidden):
    half = hidden // 256 * 128
    plan = [(which, cols, False) for which in (0, 1) for cols in ((0, half), (half, hidden - half))]
    plan += [(2, (0, width), False)]
    plan += [(3, (pair * 384, 384), False) for pair in range(width // 128)]
    return plan + [(4, (0, width), True)]


HOOKS = {
    (0, 0): ((1, 0), (1, 10)),
    (0, 1): ((1, 1),),
    (0, 2): ((2, 0), (2, 10)),
    (1, 0): ((1, 2), (0, 5), (3, 10)),
    (1, 1): ((2, 1), (1, 5)),
    (1, 2): ((3, 0), (1, 3)),
    (2, 0): ((2, 2), (0, 6), (2, 5)),
    (2, 1): ((3, 1), (1, 4), (1, 6)),
    (2, 2): ((2, 3), (4, 0), (3, 5)),
    (3, 0): ((3, 2), (0, 7), (2, 6)),
    (3, 1): ((2, 4), (1, 7), (4, 1), (4, 5)),
    (3, 2): ((3, 3), (3, 6)),
    "pairs": ((0, 8), (2, 7), (4, 2)),
    "rows0": ((1, 8), (3, 4), (4, 3)),
    "rows1": ((3, 7), (4, 6)),
    "rows2": ((2, 8),),
    "feat": ((0, 9), (4, 4), (0, 11)),
    "half": ((3, 8), (1, 9), (1, 11), (4, 7)),
    "end": ((4, 8), (2, 11), (3, 9), (3, 11), (4, 9)),
}


def backward_kernel(fast, *refs):
    refs = list(refs)
    take = lambda count: [refs.pop(0) for _ in range(count)]
    cameras, features, q_rows, k_rows, v_rows, dmix_high, dmix_low, dots = take(8)
    start_low, grad_first, probs, w_qkv, w_feat = take(5)
    if fast:
        grad_down, grad_up, grad_out, small = take(4)
        grad_tokens, grad_features, *summed = take(7)
        total, total_late = take(2)
    else:
        grad_tokens, grad_features, grad_qkv, grad_feat, small_late = take(5)
    feats, weights, grad_scores, joined, d_cat, d_rows, v_cat = take(7)
    k_turned, grad_memory, pair_rows, sums, prob_sem, load_sem = take(6)
    width = q_rows.shape[1]
    heads = width // HEAD
    pairs = heads // 2
    limit = 2 + CAM_LEN * cameras[0]
    if fast:
        small_late, part_qkv, part_feat = take(3)
        send, recv, local = refs[-3:]
        plan = reduce_plan(width, grad_up.shape[-1])
        parts_of = (grad_down, grad_up, grad_out, part_qkv, part_feat)

        def writer(which, cols):
            def write(value):
                if which == 3:
                    pair = cols[0] // 384
                    for i in range(3):
                        at = i * width + pair * 128
                        summed[3][:, at : at + 128] = value[:, i * 128 : i * 128 + 128]
                else:
                    summed[which][:, cols[0] : cols[0] + cols[1]] = value

            return write

        groups = []
        for i, (which, cols, direct) in enumerate(plan):
            bufs = take(4)
            mine = take(1)[0] if which < 3 else None
            groups.append(
                Reduce(
                    parts_of[which], cols, writer(which, cols), bufs, mine, direct, send, recv, local, i
                )
            )
        groups.append(Total(small, total, take(3), send, recv, len(plan)))
        groups.append(Total(small_late, total_late, take(3), send, recv, len(plan) + 1))
        greet()
        turns(groups, *[(0, i) for i in range(5)], (0, 10))

    def hook(where):
        if fast:
            turns(groups, *HOOKS[where])

    def pair_hook(pair, spot):
        if fast:
            for at_pair in range(pairs):

                @pl.when(pair == at_pair)
                def _():
                    hook((at_pair, spot))

    def prob_copy(pair, side):
        slot = 2 * lax.rem(pair, 2) + side
        return pltpu.make_async_copy(
            probs.at[2 * pair + side], weights.at[slot], prob_sem.at[slot]
        )

    for side in range(2):
        prob_copy(0, side).start()
    load = pltpu.make_async_copy(features.at[pl.ds(0, ROWS), :], feats, load_sem)
    load.start()
    sums[...] = jnp.zeros_like(sums)
    lane_valid = lax.broadcasted_iota(jnp.int32, (1, ROWS), 1) < limit
    row_valid = lax.broadcasted_iota(jnp.int32, (ROWS, 1), 0) < limit
    none = jnp.zeros((HEAD, ROWS), bf16)

    def attend_back(pair, carry):
        lanes = pl.ds(pl.multiple_of(pair * 128, 128), 128)

        @pl.when(pair + 1 < pairs)
        def _():
            prob_copy(pair + 1, 0).start()
            prob_copy(pair + 1, 1).start()

        pair_hook(pair, 0)
        high = dmix_high[lanes, :]
        low = dmix_low[lanes, :]
        for side in range(2):
            own = slice(side * HEAD, side * HEAD + HEAD)
            mine, its = side * HEAD, (1 - side) * HEAD
            d_cat[side, mine : mine + HEAD, :] = high[own]
            d_cat[side, its : its + HEAD, :] = none
            d_cat[side, 128 + mine : 128 + mine + HEAD, :] = low[own]
            d_cat[side, 128 + its : 128 + its + HEAD, :] = none
        d_rows[:, :128] = high.astype(f32).T.astype(bf16)
        d_rows[:, 128:] = low.astype(f32).T.astype(bf16)
        values = v_rows[:, lanes]
        v_cat[:, :128] = values
        v_cat[:, 128:] = values
        k_turned[...] = jnp.where(lane_valid, k_rows[:, lanes].astype(f32).T, 0.0).astype(bf16)
        base = 2 * lax.rem(pair, 2)
        jobs = [(side, at, size) for side in range(2) for at, size in QBLOCKS]
        parts = chunks(ROWS, STEP)
        turned = {0: [], 1: []}
        wide = {}

        def slope(job):
            side, at, size = jobs[job]
            offset = dots[2 * pair + side, :, at : at + size]
            for at_key, keys_here in parts:
                here = slice(at_key, at_key + keys_here)
                grad = dg(v_cat[here, :], d_cat[side, :, at : at + size], 1, 0) - offset
                weight = weights[base + side, here, at : at + size].astype(f32)
                grad_scores[side, here, at : at + size] = (weight * grad).astype(bf16)

        def queries(job):
            side, at, size = jobs[job]
            turned[side].append(
                dg(k_turned[...], grad_scores[side, :, at : at + size], 1, 0)[
                    side * HEAD : side * HEAD + HEAD
                ]
            )

        def spread(side, part):
            here = slice(part[0], part[0] + part[1])
            value = dg(weights[base + side, here, :ROWS], d_rows[...], 1, 0)
            value = value[:, :128] + value[:, 128:]
            key = dg(grad_scores[side, here, :ROWS], q_rows[:, lanes], 1, 0)
            wide[side, part] = (value, key)

        for side in range(2):
            prob_copy(pair, side).wait()
        for job in range(len(jobs)):
            if job == len(QBLOCKS):
                pair_hook(pair, 1)
            slope(job)
            if job >= 1:
                queries(job - 1)
            if job > len(QBLOCKS):
                side_job = job - len(QBLOCKS) - 1
                if side_job < len(parts):
                    spread(0, parts[side_job])
        queries(len(jobs) - 1)
        pair_hook(pair, 2)
        first_lane = lax.broadcasted_iota(jnp.int32, (STEP, 128), 1) < HEAD
        for part in parts:
            spread(1, part)
            here = slice(part[0], part[0] + part[1])
            keep = row_valid[here]
            for which, at in ((0, 2), (1, 1)):
                value = jnp.where(first_lane, wide[0, part][which], wide[1, part][which])
                value = jnp.where(keep, value, 0.0).astype(bf16)
                joined[here, pl.ds(pl.multiple_of(at * width + pair * 128, 128), 128)] = value
                pair_rows[here, at * 128 : at * 128 + 128] = value
        query = jnp.concatenate(
            [jnp.concatenate(turned[0], axis=1), jnp.concatenate(turned[1], axis=1)], axis=0
        )
        query = (query.astype(bf16).astype(f32).T * 0.125).astype(bf16)
        joined[:, lanes] = query
        pair_rows[:, :128] = query
        grad = dg(start_low[...], pair_rows[...], 0, 0).astype(bf16)
        if fast:
            at = pl.ds(pl.multiple_of(pair * 384, 128), 384)
            part_qkv[:, :, :, :, at] = grad.reshape(part_qkv.shape[:4] + (384,))
        else:
            for i in range(3):
                at = pl.ds(pl.multiple_of(i * width + pair * 128, 128), 128)
                grad_qkv[:, at] = grad[:, i * 128 : i * 128 + 128]
        return carry

    lax.fori_loop(0, pairs, attend_back, 0)
    load.wait()
    hook("pairs")

    for step in range(4):
        rows = slice(step * STEP, step * STEP + STEP)
        ids = step * STEP + lax.broadcasted_iota(jnp.int32, (STEP, 1), 0)
        camera = jnp.logical_and(ids >= 2, ids < limit)
        part = joined[rows, :]
        sums[0] += fold(part[:, :width].astype(f32))
        sums[1] += fold(part[:, 2 * width :].astype(f32))
        grad_start = grad_first[rows, :] + dg(part, w_qkv[...], 1, 1)
        grad_tokens[rows, :] = grad_start.astype(bf16)
        low = jnp.where(camera, grad_start, 0.0).astype(bf16)
        grad_memory[rows, :] = low
        sums[2] += fold(low.astype(f32))
        if step < 3:
            hook(f"rows{step}")
    grad = dg(feats[...], grad_memory[...], 0, 0).astype(bf16)
    small_late[...] = jnp.zeros_like(small_late)
    for i in range(3):
        small_late[i : i + 1, :] = jnp.sum(sums[i], axis=0, keepdims=True)
    if fast:
        part_feat[...] = grad.reshape(part_feat.shape)
    else:
        grad_feat[...] = grad
    hook("feat")
    for step in range(4):
        rows = slice(step * STEP, step * STEP + STEP)
        grad_features[rows, :] = dg(grad_memory[rows, :], w_feat[...], 1, 1).astype(bf16)
        if step == 1:
            hook("half")
    grad_tokens[ROWS:, :] = jnp.zeros((SLOTS - ROWS, width), bf16)
    grad_features[ROWS:, :] = jnp.zeros((SLOTS - ROWS, width), bf16)
    hook("end")
    if fast:
        turns(groups, *[(5, i) for i in range(len(groups))])


def backward_call(fast, cameras, features, saved, w_qkv, w_feat, grads, small):
    width = features.shape[1]
    heads = width // HEAD
    vmem = pl.BlockSpec(memory_space=pltpu.VMEM)
    hbm = pl.BlockSpec(memory_space=pl.ANY)
    scratch = [
        pltpu.VMEM((ROWS, width), bf16),
        pltpu.VMEM((4, ROWS, 1280), bf16),
        pltpu.VMEM((2, ROWS, 1280), bf16),
        pltpu.VMEM((ROWS, 3 * width), bf16),
        pltpu.VMEM((2, 256, ROWS), bf16),
        pltpu.VMEM((ROWS, 256), bf16),
        pltpu.VMEM((ROWS, 256), bf16),
        pltpu.VMEM((128, ROWS), bf16),
        pltpu.VMEM((ROWS, width), bf16),
        pltpu.VMEM((ROWS, 384), bf16),
        pltpu.VMEM((3, 8, width), f32),
        pltpu.SemaphoreType.DMA((4,)),
        pltpu.SemaphoreType.DMA(()),
    ]
    outs = (shaped((SLOTS, width), bf16),) * 2
    inputs = [cameras, features, *saved, w_qkv, w_feat]
    specs = [pl.BlockSpec(memory_space=pltpu.SMEM), hbm] + [vmem] * 8 + [hbm] + [vmem] * 2
    if fast:
        hidden = grads[0].shape[1]
        rows = width // 32
        late = (8, width)
        outs += tuple(shaped((rows, n), f32) for n in (hidden, hidden, width, 3 * width, width))
        outs += (shaped(small.shape, f32), shaped(late, f32))
        inputs += [grad.reshape(4, 4, 2, rows, -1) for grad in grads] + [small]
        specs += [hbm] * 3 + [vmem]
        scratch += [
            pltpu.VMEM(late, f32),
            pltpu.VMEM((4, 4, 2, rows, 3 * width), bf16),
            pltpu.VMEM((4, 4, 2, rows, width), bf16),
        ]
        plan = reduce_plan(width, hidden)
        for which, (_, size), direct in plan:
            scratch += [
                pltpu.VMEM((4, 4, rows, size), bf16),
                pltpu.VMEM((4, rows, size) if direct else (2, 2, rows, size), bf16),
                pltpu.VMEM((2, 4, rows, size), bf16),
                pltpu.VMEM((3, rows, size), bf16),
            ]
            if which < 3:
                scratch += [pltpu.VMEM((4, 4, rows, size), bf16)]
        for shape in (small.shape, late):
            scratch += [pltpu.VMEM((count,) + shape, f32) for count in (4, 4, 2)]
        scratch += [
            pltpu.SemaphoreType.DMA((len(plan) + 2, MESSAGES)),
            pltpu.SemaphoreType.DMA((len(plan) + 2, MESSAGES)),
            pltpu.SemaphoreType.DMA((len(plan),)),
        ]
    else:
        outs += (
            shaped((width, 3 * width), bf16),
            shaped((width, width), bf16),
            shaped((8, width), f32),
        )
    return pl.pallas_call(
        functools.partial(backward_kernel, fast),
        out_shape=outs,
        in_specs=specs,
        out_specs=(vmem,) * len(outs),
        scratch_shapes=scratch,
        compiler_params=pltpu.CompilerParams(
            vmem_limit_bytes=62 * MIB,
            collective_id=1 if fast else None,
            has_side_effects=fast,
        ),
        name="layer_backward",
    )(*inputs)


def finish_kernel(*refs):
    refs = list(refs)
    take = lambda count: [refs.pop(0) for _ in range(count)]
    sources, (small, late), targets = take(8), take(2), take(8)
    vectors, sem = take(10), refs[0]
    copies = [
        pltpu.make_async_copy(source, target, sem.at[i])
        for i, (source, target) in enumerate(zip(sources, targets))
    ]
    for copy in copies:
        copy.start()
    places = ((late, 0), (late, 1), (small, 5), (small, 3), (small, 4), None)
    places += ((small, 2), (small, 0), (small, 1), (late, 2))
    for vector, spot in zip(vectors, places):
        if spot is None:
            for i, (at, size) in enumerate(chunks(vector.shape[0], small.shape[1])):
                vector[at : at + size] = small[6 + i, :size]
        else:
            vector[...] = spot[0][spot[1]]
    for copy in copies:
        copy.wait()


def finish_call(large, small, late, hidden):
    width = small.shape[1]
    vmem = pl.BlockSpec(memory_space=pltpu.VMEM)
    hbm = pl.BlockSpec(memory_space=pl.ANY)
    return pl.pallas_call(
        finish_kernel,
        out_shape=tuple(shaped(a.shape, a.dtype) for a in large)
        + tuple(shaped((hidden if i == 5 else width,), f32) for i in range(10)),
        in_specs=[vmem] * 10,
        out_specs=(hbm,) * 8 + (vmem,) * 10,
        scratch_shapes=[pltpu.SemaphoreType.DMA((8,))],
        name="place_outputs",
    )(*large, small, late)


AXES = ("dp", "fsdp")


def on_device(
    fast,
    tokens,
    features,
    cameras,
    cotangent,
    w_qkv,
    w_out,
    w_up,
    w_down,
    w_feat,
    *biases,
):
    width = tokens.shape[1]
    hidden = w_up.shape[1]
    weights = (w_feat, w_qkv, w_out, w_up, w_down)
    if not fast:
        weights = tuple(lax.all_gather(w, AXES, axis=0, tiled=True) for w in weights)
    output, start_low, *rest = forward_call(fast, cameras, tokens, features, cotangent, weights, biases)
    q_rows, k_rows, v_rows, dmix_high, dmix_low, dots, grad_first, probs, *rest = rest
    grad_down, grad_up, grad_out, small, *wholes = rest
    if fast:
        weights = [whole.reshape(width, -1) for whole in wholes]
    saved = (q_rows, k_rows, v_rows, dmix_high, dmix_low, dots, start_low, grad_first, probs)
    grads = (grad_down, grad_up, grad_out)
    grad_tokens, grad_features, *rest = backward_call(
        fast, cameras, features, saved, weights[1], weights[0], grads, small
    )
    if fast:
        *grads, small, late = rest
    else:
        grads += tuple(rest[:2])
        grads = [
            lax.psum_scatter(
                lax.optimization_barrier(grad.astype(f32)), AXES, scatter_dimension=0, tiled=True
            )
            for grad in grads
        ]
        small, late = lax.psum((small, rest[2]), AXES)
    grad_down, grad_up, grad_out, grad_qkv, grad_feat = grads
    large = (output, grad_tokens, grad_features, grad_qkv, grad_out, grad_up, grad_down, grad_feat)
    return finish_call(large, small, late, hidden)


def solution(mesh):
    split = P(AXES, None)
    fast = mesh.shape["dp"] == 4 and mesh.shape["fsdp"] == 8
    return jax.shard_map(
        functools.partial(on_device, fast),
        mesh=mesh,
        in_specs=(split, split, P(AXES), split) + (split,) * 5 + (P(),) * 10,
        out_specs=(split,) * 8 + (P(),) * 10,
        check_vma=False,
    )
```

```python
import functools

import jax
import jax.numpy as jnp
from jax import lax
from jax.experimental import pallas as pl
from jax.experimental.pallas import tpu as pltpu
from jax.sharding import PartitionSpec as P

HEAD = 64
SLOTS = 1280
CAM_LEN = 300
CAMS_MAX = 4
NORM_EPS = 1e-05
LOG2E = 1.4426950408889634
GELU_C = 0.7978845608028654
GELU_A = 0.044715

ROWS = -(-(2 + CAM_LEN * CAMS_MAX) // 64) * 64
STEP = ROWS // 4
QBLOCKS = [(at, min(256, ROWS - at)) for at in range(0, ROWS, 256)]
MIB = 2**20

bf16 = jnp.bfloat16
f32 = jnp.float32


def dg(left, right, over_left, over_right):
    return lax.dot_general(
        left, right, (((over_left,), (over_right,)), ((), ())), preferred_element_type=f32
    )


def chunks(total, width):
    return [(at, min(width, total - at)) for at in range(0, total, width)]


def norm_parts(value):
    average = jnp.mean(value, axis=-1, keepdims=True)
    centered = value - average
    variance = jnp.mean(centered * centered, axis=-1, keepdims=True)
    scale = lax.rsqrt(variance + NORM_EPS)
    return centered * scale, scale


def norm_back(grad, unit, scale, gain):
    inside = grad * gain
    one = jnp.mean(inside, axis=-1, keepdims=True)
    two = jnp.mean(inside * unit, axis=-1, keepdims=True)
    return scale * (inside - one - unit * two)


def line_of(ref, cols=slice(None)):
    return ref[cols].reshape(1, -1)


def fold(value):
    rows, width = value.shape
    return jnp.sum(value.reshape(rows // 8, 8, width), axis=0)


def split_low(value):
    high = value.astype(bf16)
    return high, (value - high.astype(f32)).astype(bf16)


MESH = pl.DeviceIdType.MESH
MESSAGES = 11


def place():
    dp = lax.axis_index("dp")
    fs = lax.axis_index("fsdp")
    return dp // 2, dp % 2, fs // 2, fs % 2


def device(y, x, z, c):
    return (y * 2 + x, z * 2 + c)


def neighbours():
    y, x, z, c = place()
    around = [device(y, x, (z + k) % 4, c) for k in (1, 2, 3)]
    return around + [
        device(y, 1 - x, z, c),
        device(1 - y, x, z, c),
        device(1 - y, 1 - x, z, c),
        device(y, x, z, 1 - c),
    ]


def greet():
    barrier = pltpu.get_barrier_semaphore()
    peers = neighbours()
    for peer in peers:
        pl.semaphore_signal(barrier, inc=1, device_id=peer, device_id_type=MESH)
    pl.semaphore_wait(barrier, len(peers))


class Gather:
    def __init__(self, shard, whole, cols, send, recv, local, group):
        self.shard, self.whole, self.cols, self.send, self.recv = shard, whole, cols, send, recv
        self.local, self.group = local, group

    def copy(self, msg, source, target, peer):
        return pltpu.make_async_remote_copy(
            src_ref=source,
            dst_ref=target,
            send_sem=self.send.at[self.group, msg],
            recv_sem=self.recv.at[self.group, msg],
            device_id=peer,
            device_id_type=MESH,
        )

    def stage(self, number):
        y, x, z, c = place()
        at_x, at_y, at_d, at = y * 2 + 1 - x, (1 - y) * 2 + x, (1 - y) * 2 + 1 - x, y * 2 + x
        to_x, to_y, to_c = device(y, 1 - x, z, c), device(1 - y, x, z, c), device(y, x, z, 1 - c)
        cols = pl.ds(*self.cols)
        whole = lambda dp, line, core: self.whole.at[dp, line, core, :, cols]
        own = whole(at, z, c)
        shard = self.shard.at[:, cols]
        every, low, high = slice(None), pl.ds(0, 2), pl.ds(2, 2)
        out = [(shard, own, device(y, x, (z + k) % 4, c)) for k in (1, 2, 3)] + [
            (part, part, peer)
            for part, peer in (
                (whole(at, every, c), to_x),
                (whole(at, every, c), to_y),
                (whole(at_x, low, c), to_y),
                (whole(at_y, high, c), to_x),
                (whole(at, every, c), to_c),
                (whole(at_x, every, c), to_c),
                (whole(at_y, every, c), to_c),
                (whole(at_d, every, c), to_c),
            )
        ]
        arrived = lambda msg, part: self.copy(msg, part, part, to_c).wait_recv()
        start = lambda msg: self.copy(msg, *out[msg]).start()
        if number == 0:
            keep = pltpu.make_async_copy(shard, own, self.local.at[self.group])
            keep.start()
            for msg in (0, 1, 2):
                start(msg)
            keep.wait()
        elif number == 1:
            for k in (1, 2, 3):
                arrived(k - 1, whole(at, (z + 4 - k) % 4, c))
            for msg in (3, 4, 7):
                start(msg)
        elif number == 2:
            arrived(3, whole(at_x, every, c))
            start(5)
            arrived(4, whole(at_y, every, c))
            for msg in (6, 8, 9):
                start(msg)
        elif number == 3:
            arrived(5, whole(at_d, low, c))
            arrived(6, whole(at_d, high, c))
            start(10)
        elif number == 4:
            for msg, dp in ((7, at), (8, at_x), (9, at_y), (10, at_d)):
                arrived(msg, whole(dp, every, 1 - c))
        elif number == 5:
            for msg, ends in enumerate(out):
                self.copy(msg, *ends).wait_send()


def turns(groups, *list_of):
    for stage, group in list_of:
        groups[group].stage(stage)


def matrix(ref, cols=slice(None)):
    value = ref[(slice(None),) * (len(ref.shape) - 1) + (cols,)]
    return value.reshape(-1, value.shape[-1])


class Reduce:
    def __init__(self, part, cols, write, bufs, direct, send, recv, group):
        self.part, self.cols, self.write, self.direct = part, cols, write, direct
        self.send, self.recv, self.group = send, recv, group
        self.half, self.diag, self.side, self.line = bufs

    copy = Gather.copy

    def add(self, target, *sources):
        if len(sources) == 2:
            target[...] = sources[0][...] + sources[1][...]
            return
        total = sources[0][...].astype(f32)
        for source in sources[1:]:
            total = total + source[...].astype(f32)
        target[...] = total.astype(target.dtype)

    def stage(self, number):
        y, x, z, c = place()
        at_x, at_y, at_d, at = y * 2 + 1 - x, (1 - y) * 2 + x, (1 - y) * 2 + 1 - x, y * 2 + x
        to_x, to_y, to_c = device(y, 1 - x, z, c), device(1 - y, x, z, c), device(y, x, z, 1 - c)
        to_d = device(1 - y, 1 - x, z, c)
        cols = pl.ds(*self.cols)
        half, diag, side, line = self.half, self.diag, self.side, self.line
        mine = lambda dp: self.part.at[dp, :, c, :, cols]
        low, high = pl.ds(0, 2), pl.ds(2, 2)
        blocks = (at_d, at_x, at_y, at)
        out = [(self.part.at[dp, :, 1 - c, :, cols], half.at[dp], to_c) for dp in blocks]
        if self.direct:
            out += [
                (half.at[at_d], diag, to_d),
                None,
                (half.at[at_x], side.at[0], to_x),
                (half.at[at_y], side.at[1], to_y),
            ]
        else:
            out += [
                (half.at[at_d, low], diag.at[0], to_x),
                (half.at[at_d, high], diag.at[1], to_y),
                (half.at[at_x], side.at[0], to_x),
                (half.at[at_y], side.at[1], to_y),
            ]
        out += [
            (half.at[at, (z + k) % 4], line.at[k - 1], device(y, x, (z + k) % 4, c))
            for k in (1, 2, 3)
        ]
        arrived = lambda msg: self.copy(msg, *out[msg][1:2] * 2, to_c).wait_recv()
        start = lambda msg: self.copy(msg, *out[msg]).start()

        def halve(msg):
            self.copy(msg, half.at[blocks[msg]], half.at[blocks[msg]], to_c).wait_recv()
            self.add(half.at[blocks[msg]], half.at[blocks[msg]], mine(blocks[msg]))

        if number == 0:
            for msg in range(4):
                start(msg)
        elif number == 1:
            halve(0)
            start(4)
            if not self.direct:
                start(5)
            halve(1)
            if self.direct:
                start(6)
            halve(2)
            if self.direct:
                start(7)
            halve(3)
        elif number == 2 and not self.direct:
            arrived(5)
            late = half.at[at_x, high]
            self.add(late, late, diag.at[1])
            start(6)
            arrived(4)
            late = half.at[at_y, low]
            self.add(late, late, diag.at[0])
            start(7)
        elif number == 3:
            own = half.at[at]
            if self.direct:
                arrived(4)
            arrived(6)
            arrived(7)
            self.add(own, own, side.at[0], side.at[1], *((diag,) if self.direct else ()))
            for k in (1, 2, 3):
                start(7 + k)
        elif number == 4:
            for k in (1, 2, 3):
                arrived(7 + k)
            total = half[at, z].astype(f32) + line[0].astype(f32)
            self.write(total + line[1].astype(f32) + line[2].astype(f32))
        elif number == 5:
            for msg, ends in enumerate(out):
                if ends is not None:
                    self.copy(msg, *ends).wait_send()


class Total:
    def __init__(self, value, out, bufs, send, recv, group):
        self.value, self.out, self.send, self.recv, self.group = value, out, send, recv, group
        self.line, self.plane, self.pair = bufs

    copy = Gather.copy

    def stage(self, number):
        y, x, z, c = place()
        at_x, at_y, at_d, at = y * 2 + 1 - x, (1 - y) * 2 + x, (1 - y) * 2 + 1 - x, y * 2 + x
        to_c = device(y, x, z, 1 - c)
        line, plane, pair = self.line, self.plane, self.pair
        out = [(line.at[z], device(y, x, (z + k) % 4, c)) for k in (1, 2, 3)] + [
            (plane.at[at], device(y, 1 - x, z, c)),
            (plane.at[at], device(1 - y, x, z, c)),
            (plane.at[at], device(1 - y, 1 - x, z, c)),
            (pair.at[c], to_c),
        ]
        came = [line.at[(z + 4 - k) % 4] for k in (1, 2, 3)]
        came += [plane.at[dp] for dp in (at_x, at_y, at_d)] + [pair.at[1 - c]]

        def start(msg):
            self.copy(msg, out[msg][0], out[msg][0], out[msg][1]).start()

        def arrived(msg):
            self.copy(msg, came[msg], came[msg], to_c).wait_recv()

        if number == 0:
            line[z] = self.value[...]
            for msg in (0, 1, 2):
                start(msg)
        elif number == 1:
            for msg in (0, 1, 2):
                arrived(msg)
            plane[at] = line[0] + line[1] + line[2] + line[3]
            for msg in (3, 4, 5):
                start(msg)
        elif number == 2:
            for msg in (3, 4, 5):
                arrived(msg)
            pair[c] = plane[0] + plane[1] + plane[2] + plane[3]
            start(6)
        elif number == 3:
            arrived(6)
            self.out[...] = pair[0] + pair[1]
        elif number == 5:
            for msg in range(7):
                self.copy(msg, out[msg][0], out[msg][0], out[msg][1]).wait_send()


GATHER_HOOKS = {
    "start": ((0, 0), (0, 1)) + tuple((0, i) for i in range(2, 10)),
    "first": ((1, 0), (1, 1), (1, 2), (2, 0), (2, 1), (1, 3), (3, 0), (3, 1), (4, 0)),
    0: ((1, 4), (2, 2), (1, 5), (4, 1)),
    1: ((3, 2), (2, 3), (1, 6), (4, 2)),
    2: ((3, 3), (2, 4), (2, 5), (1, 7), (4, 3)),
    3: ((3, 4), (3, 5), (2, 6), (1, 8), (4, 4)),
    "out": ((2, 7), (3, 6), (1, 9), (4, 5)),
    "up": ((3, 7), (4, 6), (4, 7)),
    "up1": ((2, 8),),
    "up2": ((3, 8), (2, 9)),
    "down": ((3, 9), (4, 8), (4, 9)) + tuple((5, i) for i in range(10)),
}


def gather_plan(width, hidden):
    half = hidden // 256 * 128
    plan = [(0, (0, width))] + [(1, (pair * 384, 384)) for pair in range(width // 128)]
    plan += [(2, (0, width))]
    return plan + [(which, cols) for which in (3, 4) for cols in ((0, half), (half, hidden - half))]


def forward_kernel(fast, *refs):
    refs = list(refs)
    take = lambda count: [refs.pop(0) for _ in range(count)]
    cameras, tokens, features, cotangent_in = take(4)
    shards = take(5)
    b_query, b_value, b_out, gain_first, shift_first = take(5)
    b_up, b_down, gain_second, shift_second, b_feat = take(5)
    stored = take(14)
    probs, dots, small = take(3)
    wholes_out = take(2) if fast else []
    kept = take(14)
    output, start_low, q_rows, k_rows, v_rows, dmix_high, dmix_low = kept[:7]
    grad_first, act, gin, normed_low, grad_branch, grad_att, mixed_low = kept[7:]
    first, work, mixed, inverse, q_cat, v_cat, k_cat, cotangent, sums, sums_up = take(10)
    prob_sem, load_sem, store_sem, step_sem = take(4)
    w_feat, w_qkv, w_out, w_up, w_down = take(5) if fast else shards
    width = tokens.shape[1]
    hidden = w_up.shape[-1]
    heads = width // HEAD
    pairs = heads // 2
    limit = 2 + CAM_LEN * cameras[0]
    if fast:
        turned_shard, send, recv, local = take(4)
        for pair in range(pairs):
            for i in range(3):
                at = i * width + pair * 128
                turned_shard[:, pair * 384 + i * 128 : pair * 384 + i * 128 + 128] = shards[1][
                    :, at : at + 128
                ]
        shards[1] = turned_shard
        wholes = (w_feat, w_qkv, w_out, w_up, w_down)
        gather = [
            Gather(shards[which], wholes[which], cols, send, recv, local, i)
            for i, (which, cols) in enumerate(gather_plan(width, hidden))
        ]
        greet()

    def hook(where):
        if fast:
            turns(gather, *GATHER_HOOKS[where])

    def hooks(step, where):
        if fast:
            for at_step, name in where:

                @pl.when(step == at_step)
                def _():
                    hook(name)

    def rows_of(step):
        return pl.ds(pl.multiple_of(step * STEP, 16), STEP)

    def row_ids(step):
        return step * STEP + lax.broadcasted_iota(jnp.int32, (STEP, 1), 0)

    def store(i, source=None, target=None):
        return pltpu.make_async_copy(
            kept[i] if source is None else source,
            stored[i] if target is None else target,
            store_sem.at[i],
        )

    def store_step(i, step):
        which = 0 if i == 8 else 1
        rows = rows_of(step)
        return pltpu.make_async_copy(
            kept[i].at[rows, :], stored[i].at[rows, :], step_sem.at[4 * which + step]
        )

    hook("start")
    loads = [
        pltpu.make_async_copy(
            source.at[pl.ds(0, ROWS), :], act.at[:, pl.ds(i * width, width)], load_sem.at[i]
        )
        for i, source in enumerate((features, tokens))
    ]
    loads.append(
        pltpu.make_async_copy(cotangent_in.at[pl.ds(0, ROWS), :], cotangent, load_sem.at[2])
    )
    for load in loads:
        load.start()
    hook("first")
    for load in loads:
        load.wait()

    def project(step, carry):
        rows = rows_of(step)
        ids = row_ids(step)
        camera = jnp.logical_and(ids >= 2, ids < limit)
        memory = dg(act[rows, :width], matrix(w_feat), 1, 0) + line_of(b_feat)
        start = act[rows, width : 2 * width].astype(f32) + jnp.where(camera, memory, 0.0)
        first[rows, :] = start
        start_low[rows, :] = start.astype(bf16)
        return carry

    lax.fori_loop(0, 4, project, 0)
    store(1).start()

    lane_valid = lax.broadcasted_iota(jnp.int32, (1, ROWS), 1) < limit

    def prob_copy(pair, side):
        source = act if side == 0 else gin
        at = pl.ds(pl.multiple_of(lax.rem(pair, 2) * 1280, 128), 1280)
        return pltpu.make_async_copy(
            source.at[:, at], probs.at[2 * pair + side], prob_sem.at[2 * lax.rem(pair, 2) + side]
        )

    def attend(pair, carry):
        lanes = pl.ds(pl.multiple_of(pair * 128, 128), 128)
        hooks(pair, [(i, i) for i in range(pairs)])

        @pl.when(pair >= 2)
        def _():
            prob_copy(pair - 2, 0).wait()
            prob_copy(pair - 2, 1).wait()

        w_pair = matrix(w_qkv, pl.ds(pl.multiple_of(pair * 384, 128), 384))
        for step in range(4):
            rows = slice(step * STEP, step * STEP + STEP)
            part = dg(start_low[rows, :], w_pair, 1, 0)
            q_rows[rows, lanes] = ((part[:, :128] + line_of(b_query, lanes)) * 0.125).astype(bf16)
            keys = part[:, 128:256]
            if step == 0:
                lead = keys[0:1]
            keys = jnp.where(row_ids(step) < limit, keys, lead).astype(bf16)
            k_rows[rows, lanes] = keys
            k_cat[rows, :128] = keys
            k_cat[rows, 128:] = keys
            v_rows[rows, lanes] = (part[:, 256:] + line_of(b_value, lanes)).astype(bf16)
        queries = q_rows[:, lanes].astype(f32).T * LOG2E
        high, low = split_low(queries)
        none = jnp.zeros((HEAD, ROWS), bf16)
        values = jnp.where(lane_valid, v_rows[:, lanes].astype(f32).T, 0.0).astype(bf16)
        ones = jnp.broadcast_to(jnp.where(lane_valid, 1.0, 0.0), (HEAD, ROWS)).astype(bf16)
        for side in range(2):
            own = slice(side * HEAD, side * HEAD + HEAD)
            other = slice((1 - side) * HEAD, (1 - side) * HEAD + HEAD)
            q_cat[side, own, :] = high[own]
            q_cat[side, other, :] = none
            q_cat[side, 128 + side * HEAD : 128 + side * HEAD + HEAD, :] = low[own]
            q_cat[side, 128 + (1 - side) * HEAD : 128 + (1 - side) * HEAD + HEAD, :] = none
            v_cat[side, :HEAD, :] = values[own]
            v_cat[side, HEAD:, :] = ones
        base = lax.rem(pair, 2) * 1280
        jobs = [(side, at, size) for side in range(2) for at, size in QBLOCKS]
        peak = {}

        def score(job, at_key, keys_here):
            side, at, size = jobs[job]
            here = slice(at_key, at_key + keys_here)
            scores = dg(k_cat[here, :], q_cat[side, :, at : at + size], 1, 0)
            work[job % 3 * 4 + at_key // STEP, :, :size] = scores
            high_here = jnp.max(scores, axis=0, keepdims=True)
            peak[job] = jnp.maximum(peak[job], high_here) if job in peak else high_here

        def weigh(job, at_key, keys_here):
            side, at, size = jobs[job]
            slot = act if side == 0 else gin
            here = slice(at_key, at_key + keys_here)
            slot[here, pl.ds(pl.multiple_of(base + at, 128), size)] = jnp.exp2(
                work[job % 3 * 4 + at_key // STEP, :, :size] - peak[job]
            ).astype(bf16)

        def mix(job):
            side, at, size = jobs[job]
            slot = act if side == 0 else gin
            weight = slot[:, pl.ds(pl.multiple_of(base + at, 128), size)]
            summed = dg(v_cat[side], weight, 1, 0)
            inv = 1.0 / summed[HEAD : HEAD + 1]
            mixed[pl.ds(pl.multiple_of(pair * 128 + side * HEAD, 8), HEAD), at : at + size] = (
                summed[:HEAD] * inv
            )
            inverse[2 * pair + side, :, at : at + size] = inv

        parts = chunks(ROWS, STEP)
        for job in (0, 1):
            for part in parts:
                score(job, *part)
        for job in range(len(jobs)):
            for part in parts:
                if job + 2 < len(jobs):
                    score(job + 2, *part)
                weigh(job, *part)
            if job >= 2:
                mix(job - 2)
            if job == len(QBLOCKS) - 1:
                prob_copy(pair, 0).start()
        mix(len(jobs) - 2)
        mix(len(jobs) - 1)
        prob_copy(pair, 1).start()
        return carry

    lax.fori_loop(0, pairs, attend, 0)
    for pair in (pairs - 2, pairs - 1):
        for side in range(2):
            prob_copy(pair, side).wait()

    for i in (2, 3, 4):
        store(i).start()
    hook("out")
    mixed_low[...] = mixed[...].astype(bf16)
    store(13).start()
    for at, size in chunks(width, 256):
        cols = slice(at, at + size)
        first[:, cols] += dg(mixed_low[...], matrix(w_out, cols), 0, 0) + line_of(b_out, cols)
    sums[...] = jnp.zeros_like(sums)
    sums_up[...] = jnp.zeros_like(sums_up)
    cuts = chunks(hidden, 512)
    hook("up")

    def widen(step, carry):
        hooks(step, [(1, "up1"), (2, "up2")])
        rows = rows_of(step)
        unit_first, scale_first = norm_parts(first[rows, :])
        low = (unit_first * line_of(gain_first) + line_of(shift_first)).astype(bf16)
        normed_low[rows, :] = low
        for at, size in cuts:
            cols = slice(at, at + size)
            inner = dg(low, matrix(w_up, cols), 1, 0) + line_of(b_up, cols)
            square = inner * inner
            half = 0.5 + 0.5 * jnp.tanh(inner * (GELU_C + (GELU_C * GELU_A) * square))
            value = inner * half
            act[rows, cols] = value.astype(bf16)
            slope = half + value * (1.0 - half) * (2 * GELU_C + (6 * GELU_C * GELU_A) * square)
            gin[rows, cols] = slope.astype(bf16)
        store_step(8, step).start()
        return carry

    lax.fori_loop(0, 4, widen, 0)
    store(10).start()
    hook("down")

    def feed(step, carry):
        rows = rows_of(step)
        valid = row_ids(step) < limit
        unit_first, scale_first = norm_parts(first[rows, :])
        normed = unit_first * line_of(gain_first) + line_of(shift_first)
        branch = dg(act[rows, :], matrix(w_down), 1, 1) + line_of(b_down)
        unit_second, scale_second = norm_parts(normed + branch)
        final = unit_second * line_of(gain_second) + line_of(shift_second)
        output[rows, :] = jnp.where(valid, final, 0.0).astype(bf16)
        grad = jnp.where(valid, cotangent[rows, :].astype(f32), 0.0)
        sums[0] += fold(grad * unit_second)
        sums[1] += fold(grad)
        grad_second = norm_back(grad, unit_second, scale_second, line_of(gain_second))
        low_branch = grad_second.astype(bf16)
        grad_branch[rows, :] = low_branch
        sums[2] += fold(low_branch.astype(f32))
        for at, size in cuts:
            cols = slice(at, at + size)
            low_inner = (
                dg(low_branch, matrix(w_down, cols), 1, 0) * gin[rows, cols].astype(f32)
            ).astype(bf16)
            gin[rows, cols] = low_inner
            sums_up[:, cols] += fold(low_inner.astype(f32))
        store_step(9, step).start()
        grad_normed = grad_second + dg(gin[rows, :], matrix(w_up), 1, 1)
        sums[3] += fold(grad_normed * unit_first)
        sums[4] += fold(grad_normed)
        back = norm_back(grad_normed, unit_first, scale_first, line_of(gain_first))
        grad_first[rows, :] = back
        low_att = back.astype(bf16)
        grad_att[rows, :] = low_att
        sums[5] += fold(low_att.astype(f32))
        return carry

    lax.fori_loop(0, 4, feed, 0)
    output[ROWS:, :] = jnp.zeros((SLOTS - ROWS, width), bf16)
    for i in (0, 7, 11, 12):
        store(i).start()
    small[...] = jnp.zeros_like(small)
    for i in range(6):
        small[i : i + 1, :] = jnp.sum(sums[i], axis=0, keepdims=True)
    for i, (at, size) in enumerate(chunks(hidden, width)):
        small[6 + i : 7 + i, :size] = jnp.sum(sums_up[:, at : at + size], axis=0, keepdims=True)
    if fast:
        whole_copies = [
            store(14 + i, source, target)
            for i, (source, target) in enumerate(zip((w_feat, w_qkv), wholes_out))
        ]
        for copy in whole_copies:
            copy.start()

    for at, size in QBLOCKS:
        cols = slice(at, at + size)
        grad_mixed = dg(matrix(w_out), grad_att[cols, :], 1, 1).astype(bf16).astype(f32)
        scaled = grad_mixed.reshape(heads, HEAD, size) * inverse[:, :, cols]
        dots[:, :, cols] = jnp.sum(
            scaled * mixed[:, cols].reshape(heads, HEAD, size), axis=1, keepdims=True
        )
        high, low = split_low(scaled.reshape(width, size))
        dmix_high[:, cols] = high
        dmix_low[:, cols] = low
    for i in (5, 6):
        store(i).start()
    for step in range(4):
        store_step(8, step).wait()
        store_step(9, step).wait()
    for i in (0, 1, 2, 3, 4, 5, 6, 7, 10, 11, 12, 13):
        store(i).wait()
    if fast:
        for copy in whole_copies:
            copy.wait()


def shaped(shape, dtype):
    return jax.ShapeDtypeStruct(shape, dtype)


def forward_call(fast, cameras, tokens, features, cotangent, weights, biases):
    width = tokens.shape[1]
    hidden = weights[3].shape[1]
    heads = width // HEAD
    token_rows = shaped((ROWS, width), bf16)
    kept = (shaped((SLOTS, width), bf16),) + (token_rows,) * 4 + (shaped((width, ROWS), bf16),) * 2
    kept += (shaped((ROWS, width), f32),) + (shaped((ROWS, hidden), bf16),) * 2
    kept += (token_rows,) * 3 + (shaped((width, ROWS), bf16),)
    wholes = [(4, 4, 2) + w.shape for w in weights]
    outs = kept + (
        shaped((heads, ROWS, 1280), bf16),
        shaped((heads, 1, ROWS), f32),
        shaped((-(-(6 + -(-hidden // width)) // 8) * 8, width), f32),
    )
    if fast:
        outs += tuple(shaped(whole, bf16) for whole in wholes[:2])
    vmem = pl.BlockSpec(memory_space=pltpu.VMEM)
    hbm = pl.BlockSpec(memory_space=pl.ANY)
    groups = len(gather_plan(width, hidden))
    return pl.pallas_call(
        functools.partial(forward_kernel, fast),
        out_shape=outs,
        in_specs=[pl.BlockSpec(memory_space=pltpu.SMEM)] + [hbm] * 3 + [vmem] * 15,
        out_specs=tuple(vmem if i in (15, 16) else hbm for i in range(len(outs))),
        scratch_shapes=[pltpu.VMEM(k.shape, k.dtype) for k in kept]
        + [
            pltpu.VMEM((ROWS, width), f32),
            pltpu.VMEM((12, STEP, 256), f32),
            pltpu.VMEM((width, ROWS), f32),
            pltpu.VMEM((heads, 1, ROWS), f32),
            pltpu.VMEM((2, 256, ROWS), bf16),
            pltpu.VMEM((2, 128, ROWS), bf16),
            pltpu.VMEM((ROWS, 256), bf16),
            pltpu.VMEM((ROWS, width), bf16),
            pltpu.VMEM((6, 8, width), f32),
            pltpu.VMEM((8, hidden), f32),
            pltpu.SemaphoreType.DMA((4,)),
            pltpu.SemaphoreType.DMA((3,)),
            pltpu.SemaphoreType.DMA((16,)),
            pltpu.SemaphoreType.DMA((8,)),
        ]
        + fast
        * (
            [pltpu.VMEM(whole, bf16) for whole in wholes]
            + [
                pltpu.VMEM(weights[1].shape, bf16),
                pltpu.SemaphoreType.DMA((groups, MESSAGES)),
                pltpu.SemaphoreType.DMA((groups, MESSAGES)),
                pltpu.SemaphoreType.DMA((groups,)),
            ]
        ),
        compiler_params=pltpu.CompilerParams(
            vmem_limit_bytes=62 * MIB,
            collective_id=0 if fast else None,
            has_side_effects=fast,
        ),
        name="layer_forward",
    )(cameras, tokens, features, cotangent, *weights, *biases)


TAIL = 1280


def reduce_plan(width, hidden):
    cuts = ((0, TAIL), (TAIL, TAIL), (2 * TAIL, hidden - 2 * TAIL))
    plan = [(which, cols, False) for which in (0, 1) for cols in cuts]
    plan += [(2, (0, width), False)]
    pairs = width // 128
    plan += [(3, (pair * 384, 384), pair == pairs - 1) for pair in range(pairs)]
    return plan + [(4, (0, width), True)]


REDUCE_HOOKS = {
    "start": ((0, 12),),
    "out": ((0, 6),),
    "tails": ((0, 5), (0, 2), (1, 6)),
    "up0": ((0, 3), (1, 5), (1, 12)),
    "up1": ((0, 4), (1, 2)),
    "down0": ((0, 0), (1, 3), (2, 6)),
    "down1": ((0, 1), (1, 4), (2, 5)),
    (0, 0): ((2, 2), (2, 12)),
    (0, 1): ((1, 0),),
    (0, 2): ((2, 3), (1, 1), (3, 12)),
    (1, 0): ((2, 4), (0, 7), (3, 6)),
    (1, 1): ((1, 7), (3, 5)),
    (1, 2): ((2, 0), (3, 2)),
    (2, 0): ((0, 8), (2, 1)),
    (2, 1): ((1, 8), (2, 7), (3, 3)),
    (2, 2): ((3, 4),),
    (3, 0): ((0, 9), (2, 8)),
    (3, 1): ((1, 9), (3, 0)),
    (3, 2): ((3, 1),),
    "pairs": ((0, 10), (2, 9), (3, 7)),
    "rows0": ((1, 10),),
    "rows1": ((3, 8),),
    "rows2": ((4, 6), (4, 5), (4, 2), (3, 9)),
    "feat": ((0, 11), (0, 13), (4, 3)),
    "half": ((1, 11), (1, 13), (3, 10), (4, 4)),
    "end": ((4, 0), (4, 1), (4, 7), (4, 8), (2, 13), (4, 9), (3, 11), (4, 10), (3, 13), (4, 11))
    + tuple((5, i) for i in range(14)),
}


def put(target, cols, value):
    if len(target.shape) == 2:
        target[:, cols] = value
    else:
        target[:, :, :, :, cols] = value.reshape(target.shape[:4] + value.shape[1:])


def backward_kernel(fast, *refs):
    refs = list(refs)
    take = lambda count: [refs.pop(0) for _ in range(count)]
    cameras, features, probs, dots, act, gin, *wgrad_in = take(10)
    inputs = take(9)
    small = take(1)[0] if fast else None
    grad_tokens, grad_features = take(2)
    if fast:
        summed, (total, total_late) = take(5), take(2)
        parts_of = take(5)
        small_late = take(1)[0]
    else:
        parts_of = take(5)
        small_late = take(1)[0]
    loaded = take(9)
    q_rows, k_rows, v_rows, dmix_high, dmix_low, start_low, grad_first, w_qkv, w_feat = loaded
    weights, grad_scores, joined, d_cat, d_rows, v_cat, k_turned, blank, sums = take(9)
    prob_sem, load_sem, wgrad_sem, out_sem = take(4)
    width = q_rows.shape[1]
    hidden = act.shape[1]
    heads = width // HEAD
    pairs = heads // 2
    limit = 2 + CAM_LEN * cameras[0]
    if fast:
        send, recv, local = refs[-3:]
        plan = reduce_plan(width, hidden)

        def writer(which, cols):
            def write(value):
                if which == 3:
                    pair = cols[0] // 384
                    for i in range(3):
                        at = i * width + pair * 128
                        summed[3][:, at : at + 128] = value[:, i * 128 : i * 128 + 128]
                else:
                    summed[which][:, cols[0] : cols[0] + cols[1]] = value

            return write

        groups = [
            Reduce(parts_of[which], cols, writer(which, cols), take(4), direct, send, recv, i)
            for i, (which, cols, direct) in enumerate(plan)
        ]
        groups.append(Total(small, total, take(3), send, recv, len(plan)))
        groups.append(Total(small_late, total_late, take(3), send, recv, len(plan) + 1))

    def hook(where):
        if fast:
            turns(groups, *REDUCE_HOOKS[where])

    def pair_hook(pair, spot):
        if fast:
            for at_pair in range(pairs):

                @pl.when(pair == at_pair)
                def _():
                    hook((at_pair, spot))

    mixed_low, normed_low = d_cat, joined.at[:, pl.ds(0, width)]
    grad_branch, grad_att = joined.at[:, pl.ds(width, width)], joined.at[:, pl.ds(2 * width, width)]
    tail = pl.ds(2 * TAIL, hidden - 2 * TAIL)
    act_tail = weights.at[2, :, pl.ds(0, hidden - 2 * TAIL)]
    gin_tail = weights.at[2, :, pl.ds(hidden - 2 * TAIL, hidden - 2 * TAIL)]
    ends = [
        (wgrad_in[3], mixed_low),
        (wgrad_in[2], grad_att),
        (wgrad_in[0], normed_low),
        (gin.at[:, tail], gin_tail),
        (wgrad_in[1], grad_branch),
        (act.at[:, tail], act_tail),
        (gin.at[:, pl.ds(0, TAIL)], weights.at[3]),
        (gin.at[:, pl.ds(TAIL, TAIL)], grad_scores.at[0]),
        (act.at[:, pl.ds(0, TAIL)], weights.at[0]),
        (act.at[:, pl.ds(TAIL, TAIL)], weights.at[1]),
    ]
    fetch = [
        pltpu.make_async_copy(source, target, wgrad_sem.at[i])
        for i, (source, target) in enumerate(ends)
    ]
    loads = [
        pltpu.make_async_copy(source, target, load_sem.at[i])
        for i, (source, target) in enumerate(zip(inputs, loaded))
    ]
    for copy in fetch + loads:
        copy.start()
    if fast:
        greet()
    hook("start")

    def prob_copy(pair, side):
        slot = 2 * lax.rem(pair + 1, 2) + side
        return pltpu.make_async_copy(
            probs.at[2 * pair + side], weights.at[slot], prob_sem.at[slot]
        )

    def weight_grad(which, left, right, at, size):
        for cut, wide in chunks(size, 512):
            grad = dg(left[...], right[:, cut : cut + wide], 0, 0).astype(bf16)
            put(parts_of[which], pl.ds(at + cut, wide), grad)

    fetch[0].wait()
    fetch[1].wait()
    grad = dg(mixed_low[...].reshape(width, ROWS), grad_att[...], 1, 0).astype(bf16)
    put(parts_of[2], pl.ds(0, width), grad)
    hook("out")
    fetch[2].wait()
    fetch[3].wait()
    weight_grad(1, normed_low, gin_tail, 2 * TAIL, hidden - 2 * TAIL)
    fetch[4].wait()
    fetch[5].wait()
    weight_grad(0, grad_branch, act_tail, 2 * TAIL, hidden - 2 * TAIL)
    hook("tails")
    fetch[6].wait()
    weight_grad(1, normed_low, weights.at[3], 0, TAIL)
    hook("up0")
    for side in range(2):
        prob_copy(0, side).start()
    fetch[7].wait()
    weight_grad(1, normed_low, grad_scores.at[0], TAIL, TAIL)
    hook("up1")
    fetch[8].wait()
    weight_grad(0, grad_branch, weights.at[0], 0, TAIL)
    hook("down0")
    fetch[9].wait()
    weight_grad(0, grad_branch, weights.at[1], TAIL, TAIL)
    hook("down1")
    for load in loads:
        load.wait()

    sums[...] = jnp.zeros_like(sums)
    lane_valid = lax.broadcasted_iota(jnp.int32, (1, ROWS), 1) < limit
    row_valid = lax.broadcasted_iota(jnp.int32, (ROWS, 1), 0) < limit
    none = jnp.zeros((HEAD, ROWS), bf16)

    def attend_back(pair, carry):
        lanes = pl.ds(pl.multiple_of(pair * 128, 128), 128)

        @pl.when(pair + 1 < pairs)
        def _():
            prob_copy(pair + 1, 0).start()
            prob_copy(pair + 1, 1).start()

        pair_hook(pair, 0)
        high = dmix_high[lanes, :]
        low = dmix_low[lanes, :]
        for side in range(2):
            own = slice(side * HEAD, side * HEAD + HEAD)
            mine, its = side * HEAD, (1 - side) * HEAD
            d_cat[side, mine : mine + HEAD, :] = high[own]
            d_cat[side, its : its + HEAD, :] = none
            d_cat[side, 128 + mine : 128 + mine + HEAD, :] = low[own]
            d_cat[side, 128 + its : 128 + its + HEAD, :] = none
        d_rows[:, :128] = high.astype(f32).T.astype(bf16)
        d_rows[:, 128:] = low.astype(f32).T.astype(bf16)
        values = v_rows[:, lanes]
        v_cat[:, :128] = values
        v_cat[:, 128:] = values
        k_turned[...] = jnp.where(lane_valid, k_rows[:, lanes].astype(f32).T, 0.0).astype(bf16)
        base = 2 * lax.rem(pair + 1, 2)
        jobs = [(side, at, size) for side in range(2) for at, size in QBLOCKS]
        parts = chunks(ROWS, STEP)
        turned = {0: [], 1: []}
        wide = {}

        def slope(job):
            side, at, size = jobs[job]
            offset = dots[2 * pair + side, :, at : at + size]
            for at_key, keys_here in parts:
                here = slice(at_key, at_key + keys_here)
                grad = dg(v_cat[here, :], d_cat[side, :, at : at + size], 1, 0) - offset
                weight = weights[base + side, here, at : at + size].astype(f32)
                grad_scores[side, here, at : at + size] = (weight * grad).astype(bf16)

        def queries(job):
            side, at, size = jobs[job]
            turned[side].append(
                dg(k_turned[...], grad_scores[side, :, at : at + size], 1, 0)[
                    side * HEAD : side * HEAD + HEAD
                ]
            )

        def spread(side, part):
            here = slice(part[0], part[0] + part[1])
            value = dg(weights[base + side, here, :ROWS], d_rows[...], 1, 0)
            value = value[:, :128] + value[:, 128:]
            key = dg(grad_scores[side, here, :ROWS], q_rows[:, lanes], 1, 0)
            wide[side, part] = (value, key)

        for side in range(2):
            prob_copy(pair, side).wait()
        for job in range(len(jobs)):
            if job == len(QBLOCKS):
                pair_hook(pair, 1)
            slope(job)
            if job >= 1:
                queries(job - 1)
            if job > len(QBLOCKS):
                side_job = job - len(QBLOCKS) - 1
                if side_job < len(parts):
                    spread(0, parts[side_job])
        queries(len(jobs) - 1)
        pair_hook(pair, 2)
        first_lane = lax.broadcasted_iota(jnp.int32, (STEP, 128), 1) < HEAD
        spot = lambda i: pl.ds(pl.multiple_of(pair * 384 + i * 128, 128), 128)
        for part in parts:
            spread(1, part)
            here = slice(part[0], part[0] + part[1])
            keep = row_valid[here]
            for which, i in ((0, 2), (1, 1)):
                value = jnp.where(first_lane, wide[0, part][which], wide[1, part][which])
                joined[here, spot(i)] = jnp.where(keep, value, 0.0).astype(bf16)
        query = jnp.concatenate(
            [jnp.concatenate(turned[0], axis=1), jnp.concatenate(turned[1], axis=1)], axis=0
        )
        joined[:, spot(0)] = (query.astype(bf16).astype(f32).T * 0.125).astype(bf16)
        at = pl.ds(pl.multiple_of(pair * 384, 128), 384)
        put(parts_of[3], at, dg(start_low[...], joined[:, at], 0, 0).astype(bf16))
        return carry

    lax.fori_loop(0, pairs, attend_back, 0)
    feats = weights.at[2, :, pl.ds(0, width)]
    tokens_out = weights.at[2, :, pl.ds(width, width)]
    features_out = weights.at[3, :, pl.ds(0, width)]
    grad_memory = grad_scores.at[0, :, pl.ds(0, width)]
    load = pltpu.make_async_copy(features.at[pl.ds(0, ROWS), :], feats, out_sem.at[0])
    load.start()
    blank[...] = jnp.zeros_like(blank)
    body, rest = pl.ds(0, ROWS), pl.ds(ROWS, SLOTS - ROWS)
    stores = [
        pltpu.make_async_copy(source, target, out_sem.at[1 + i])
        for i, (source, target) in enumerate(
            (
                (blank, grad_tokens.at[rest, :]),
                (blank, grad_features.at[rest, :]),
                (tokens_out, grad_tokens.at[body, :]),
                (features_out, grad_features.at[body, :]),
            )
        )
    ]
    stores[0].start()
    stores[1].start()
    hook("pairs")

    for step in range(4):
        rows = slice(step * STEP, step * STEP + STEP)
        ids = step * STEP + lax.broadcasted_iota(jnp.int32, (STEP, 1), 0)
        camera = jnp.logical_and(ids >= 2, ids < limit)
        part = joined[rows, :]
        for pair in range(pairs):
            lanes = slice(pair * 128, pair * 128 + 128)
            sums[0, :, lanes] += fold(part[:, pair * 384 : pair * 384 + 128].astype(f32))
            sums[1, :, lanes] += fold(part[:, pair * 384 + 256 : pair * 384 + 384].astype(f32))
        grad_start = grad_first[rows, :] + dg(part, w_qkv[...], 1, 1)
        tokens_out[rows, :] = grad_start.astype(bf16)
        low = jnp.where(camera, grad_start, 0.0).astype(bf16)
        grad_memory[rows, :] = low
        sums[2] += fold(low.astype(f32))
        if step < 3:
            hook(f"rows{step}")
    stores[2].start()
    load.wait()
    put(parts_of[4], pl.ds(0, width), dg(feats[...], grad_memory[...], 0, 0).astype(bf16))
    small_late[...] = jnp.zeros_like(small_late)
    for i in range(3):
        small_late[i : i + 1, :] = jnp.sum(sums[i], axis=0, keepdims=True)
    hook("feat")
    for step in range(4):
        rows = slice(step * STEP, step * STEP + STEP)
        features_out[rows, :] = dg(grad_memory[rows, :], w_feat[...], 1, 1).astype(bf16)
        if step == 1:
            hook("half")
    stores[3].start()
    hook("end")
    for copy in stores:
        copy.wait()


def backward_call(fast, cameras, features, saved, small):
    probs, dots, act, gin, normed_low, grad_branch, grad_att, mixed_low, *inputs = saved
    width, hidden = features.shape[1], act.shape[1]
    vmem = pl.BlockSpec(memory_space=pltpu.VMEM)
    hbm = pl.BlockSpec(memory_space=pl.ANY)
    rows = width // 32
    columns = (hidden, hidden, width, 3 * width, width)
    late = (8, width)
    outs = (shaped((SLOTS, width), bf16),) * 2
    scratch = []
    reduce_scratch = []
    args = [cameras, features, probs, dots, act, gin, normed_low, grad_branch, grad_att]
    args += [mixed_low.reshape(2, width // 2, ROWS), *inputs]
    specs = [pl.BlockSpec(memory_space=pltpu.SMEM), hbm, hbm, vmem] + [hbm] * 15
    if fast:
        outs += tuple(shaped((rows, n), f32) for n in columns)
        outs += (shaped(small.shape, f32), shaped(late, f32))
        args += [small]
        specs += [vmem]
        scratch += [pltpu.VMEM((4, 4, 2, rows, n), bf16) for n in columns] + [pltpu.VMEM(late, f32)]
        plan = reduce_plan(width, hidden)
        for which, (_, size), direct in plan:
            reduce_scratch += [
                pltpu.VMEM((4, 4, rows, size), bf16),
                pltpu.VMEM((4, rows, size) if direct else (2, 2, rows, size), bf16),
                pltpu.VMEM((2, 4, rows, size), bf16),
                pltpu.VMEM((3, rows, size), bf16),
            ]
        for shape in (small.shape, late):
            reduce_scratch += [pltpu.VMEM((count,) + shape, f32) for count in (4, 4, 2)]
        reduce_scratch += [
            pltpu.SemaphoreType.DMA((len(plan) + 2, MESSAGES)),
            pltpu.SemaphoreType.DMA((len(plan) + 2, MESSAGES)),
            pltpu.SemaphoreType.DMA((len(plan),)),
        ]
    else:
        outs += tuple(shaped((width, n), bf16) for n in columns) + (shaped(late, f32),)
    scratch += [pltpu.VMEM(a.shape, a.dtype) for a in inputs]
    scratch += [
        pltpu.VMEM((4, ROWS, 1280), bf16),
        pltpu.VMEM((2, ROWS, 1280), bf16),
        pltpu.VMEM((ROWS, 3 * width), bf16),
        pltpu.VMEM((2, 256, ROWS), bf16),
        pltpu.VMEM((ROWS, 256), bf16),
        pltpu.VMEM((ROWS, 256), bf16),
        pltpu.VMEM((128, ROWS), bf16),
        pltpu.VMEM((SLOTS - ROWS, width), bf16),
        pltpu.VMEM((3, 8, width), f32),
        pltpu.SemaphoreType.DMA((4,)),
        pltpu.SemaphoreType.DMA((9,)),
        pltpu.SemaphoreType.DMA((10,)),
        pltpu.SemaphoreType.DMA((5,)),
    ]
    return pl.pallas_call(
        functools.partial(backward_kernel, fast),
        out_shape=outs,
        in_specs=specs,
        out_specs=(hbm,) * 2 + (vmem,) * (len(outs) - 2),
        scratch_shapes=scratch + reduce_scratch,
        compiler_params=pltpu.CompilerParams(
            vmem_limit_bytes=62 * MIB,
            collective_id=1 if fast else None,
            has_side_effects=fast,
        ),
        name="layer_backward",
    )(*args)


def finish_kernel(*refs):
    refs = list(refs)
    take = lambda count: [refs.pop(0) for _ in range(count)]
    sources, (small, late), targets = take(8), take(2), take(8)
    vectors, sem = take(10), refs[0]
    copies = [
        pltpu.make_async_copy(source, target, sem.at[i])
        for i, (source, target) in enumerate(zip(sources, targets))
    ]
    for copy in copies:
        copy.start()
    places = ((late, 0), (late, 1), (small, 5), (small, 3), (small, 4), None)
    places += ((small, 2), (small, 0), (small, 1), (late, 2))
    for vector, spot in zip(vectors, places):
        if spot is None:
            for i, (at, size) in enumerate(chunks(vector.shape[0], small.shape[1])):
                vector[at : at + size] = small[6 + i, :size]
        else:
            vector[...] = spot[0][spot[1]]
    for copy in copies:
        copy.wait()


def finish_call(large, small, late, hidden):
    width = small.shape[1]
    vmem = pl.BlockSpec(memory_space=pltpu.VMEM)
    hbm = pl.BlockSpec(memory_space=pl.ANY)
    return pl.pallas_call(
        finish_kernel,
        out_shape=tuple(shaped(a.shape, a.dtype) for a in large)
        + tuple(shaped((hidden if i == 5 else width,), f32) for i in range(10)),
        in_specs=[vmem] * 10,
        out_specs=(hbm,) * 8 + (vmem,) * 10,
        scratch_shapes=[pltpu.SemaphoreType.DMA((8,))],
        name="place_outputs",
    )(*large, small, late)


AXES = ("dp", "fsdp")


def on_device(
    fast,
    tokens,
    features,
    cameras,
    cotangent,
    w_qkv,
    w_out,
    w_up,
    w_down,
    w_feat,
    *biases,
):
    width = tokens.shape[1]
    hidden = w_up.shape[1]
    pairs = width // 128
    weights = (w_feat, w_qkv, w_out, w_up, w_down)
    if not fast:
        weights = [lax.all_gather(w, AXES, axis=0, tiled=True) for w in weights]
        by_pair = weights[1].reshape(width, 3, pairs, 128).transpose(0, 2, 1, 3)
        weights[1] = by_pair.reshape(width, 3 * width)
    output, *kept = forward_call(fast, cameras, tokens, features, cotangent, weights, biases)
    start_low, q_rows, k_rows, v_rows, dmix_high, dmix_low, grad_first, *kept = kept
    act, gin, normed_low, grad_branch, grad_att, mixed_low, probs, dots, small, *wholes = kept
    if fast:
        weights = [whole.reshape(width, -1) for whole in wholes]
    saved = (probs, dots, act, gin, normed_low, grad_branch, grad_att, mixed_low)
    saved += (q_rows, k_rows, v_rows, dmix_high, dmix_low, start_low, grad_first)
    saved += (weights[1], weights[0])
    grad_tokens, grad_features, *grads = backward_call(fast, cameras, features, saved, small)
    if fast:
        *grads, small, late = grads
    else:
        *grads, late = grads
        by_pair = grads[3].reshape(width, pairs, 3, 128).transpose(0, 2, 1, 3)
        grads[3] = by_pair.reshape(width, 3 * width)
        grads = [
            lax.psum_scatter(
                lax.optimization_barrier(grad.astype(f32)), AXES, scatter_dimension=0, tiled=True
            )
            for grad in grads
        ]
        small, late = lax.psum((small, late), AXES)
    grad_down, grad_up, grad_out, grad_qkv, grad_feat = grads
    large = (output, grad_tokens, grad_features, grad_qkv, grad_out, grad_up, grad_down, grad_feat)
    return finish_call(large, small, late, hidden)


def solution(mesh):
    split = P(AXES, None)
    fast = mesh.shape["dp"] == 4 and mesh.shape["fsdp"] == 8
    return jax.shard_map(
        functools.partial(on_device, fast),
        mesh=mesh,
        in_specs=(split, split, P(AXES), split) + (split,) * 5 + (P(),) * 10,
        out_specs=(split,) * 8 + (P(),) * 10,
        check_vma=False,
    )
```

```python
import functools

import jax
import jax.numpy as jnp
from jax import lax
from jax.experimental import pallas as pl
from jax.experimental.pallas import tpu as pltpu
from jax.sharding import PartitionSpec as P

HEAD = 64
SLOTS = 1280
CAM_LEN = 300
CAMS_MAX = 4
NORM_EPS = 1e-05
LOG2E = 1.4426950408889634
GELU_C = 0.7978845608028654
GELU_A = 0.044715

ROWS = -(-(2 + CAM_LEN * CAMS_MAX) // 64) * 64
STEP = ROWS // 4
QBLOCKS = [(at, min(256, ROWS - at)) for at in range(0, ROWS, 256)]
MIB = 2**20

bf16 = jnp.bfloat16
f32 = jnp.float32


def dg(left, right, over_left, over_right):
    return lax.dot_general(
        left, right, (((over_left,), (over_right,)), ((), ())), preferred_element_type=f32
    )


def chunks(total, width):
    return [(at, min(width, total - at)) for at in range(0, total, width)]


def norm_parts(value):
    average = jnp.mean(value, axis=-1, keepdims=True)
    centered = value - average
    variance = jnp.mean(centered * centered, axis=-1, keepdims=True)
    scale = lax.rsqrt(variance + NORM_EPS)
    return centered * scale, scale


def norm_back(grad, unit, scale, gain):
    inside = grad * gain
    one = jnp.mean(inside, axis=-1, keepdims=True)
    two = jnp.mean(inside * unit, axis=-1, keepdims=True)
    return scale * (inside - one - unit * two)


def line_of(ref, cols=slice(None)):
    return ref[cols].reshape(1, -1)


def fold(value):
    rows, width = value.shape
    return jnp.sum(value.reshape(rows // 8, 8, width), axis=0)


def split_low(value):
    high = value.astype(bf16)
    return high, (value - high.astype(f32)).astype(bf16)


MESH = pl.DeviceIdType.MESH
MESSAGES = 11


def place():
    dp = lax.axis_index("dp")
    fs = lax.axis_index("fsdp")
    return dp // 2, dp % 2, fs // 2, fs % 2


def device(y, x, z, c):
    return (y * 2 + x, z * 2 + c)


def neighbours():
    y, x, z, c = place()
    around = [device(y, x, (z + k) % 4, c) for k in (1, 2, 3)]
    return around + [
        device(y, 1 - x, z, c),
        device(1 - y, x, z, c),
        device(1 - y, 1 - x, z, c),
        device(y, x, z, 1 - c),
    ]


def greet():
    barrier = pltpu.get_barrier_semaphore()
    peers = neighbours()
    for peer in peers:
        pl.semaphore_signal(barrier, inc=1, device_id=peer, device_id_type=MESH)
    pl.semaphore_wait(barrier, len(peers))


class Gather:
    def __init__(self, shard, whole, cols, send, recv, local, group):
        self.shard, self.whole, self.cols, self.send, self.recv = shard, whole, cols, send, recv
        self.local, self.group = local, group

    def copy(self, msg, source, target, peer):
        return pltpu.make_async_remote_copy(
            src_ref=source,
            dst_ref=target,
            send_sem=self.send.at[self.group, msg],
            recv_sem=self.recv.at[self.group, msg],
            device_id=peer,
            device_id_type=MESH,
        )

    def stage(self, number):
        y, x, z, c = place()
        at_x, at_y, at_d, at = y * 2 + 1 - x, (1 - y) * 2 + x, (1 - y) * 2 + 1 - x, y * 2 + x
        to_x, to_y, to_c = device(y, 1 - x, z, c), device(1 - y, x, z, c), device(y, x, z, 1 - c)
        cols = pl.ds(*self.cols)
        whole = lambda dp, line, core: self.whole.at[dp, line, core, :, cols]
        own = whole(at, z, c)
        shard = self.shard.at[:, cols]
        every, low, high = slice(None), pl.ds(0, 2), pl.ds(2, 2)
        out = [(shard, own, device(y, x, (z + k) % 4, c)) for k in (1, 2, 3)] + [
            (part, part, peer)
            for part, peer in (
                (whole(at, every, c), to_x),
                (whole(at, every, c), to_y),
                (whole(at_x, low, c), to_y),
                (whole(at_y, high, c), to_x),
                (whole(at, every, c), to_c),
                (whole(at_x, every, c), to_c),
                (whole(at_y, every, c), to_c),
                (whole(at_d, every, c), to_c),
            )
        ]
        arrived = lambda msg, part: self.copy(msg, part, part, to_c).wait_recv()
        start = lambda msg: self.copy(msg, *out[msg]).start()
        if number == 0:
            keep = pltpu.make_async_copy(shard, own, self.local.at[self.group])
            keep.start()
            for msg in (0, 1, 2):
                start(msg)
            keep.wait()
        elif number == 1:
            for k in (1, 2, 3):
                arrived(k - 1, whole(at, (z + 4 - k) % 4, c))
            for msg in (3, 4, 7):
                start(msg)
        elif number == 2:
            arrived(3, whole(at_x, every, c))
            start(5)
            arrived(4, whole(at_y, every, c))
            for msg in (6, 8, 9):
                start(msg)
        elif number == 3:
            arrived(5, whole(at_d, low, c))
            arrived(6, whole(at_d, high, c))
            start(10)
        elif number == 4:
            for msg, dp in ((7, at), (8, at_x), (9, at_y), (10, at_d)):
                arrived(msg, whole(dp, every, 1 - c))
        elif number == 5:
            for msg, ends in enumerate(out):
                self.copy(msg, *ends).wait_send()


def turns(groups, *list_of):
    for stage, group in list_of:
        groups[group].stage(stage)


def matrix(ref, cols=slice(None)):
    value = ref[(slice(None),) * (len(ref.shape) - 1) + (cols,)]
    return value.reshape(-1, value.shape[-1])


class Reduce:
    def __init__(self, part, cols, write, bufs, direct, send, recv, group):
        self.part, self.cols, self.write, self.direct = part, cols, write, direct
        self.send, self.recv, self.group = send, recv, group
        self.half, self.diag, self.side, self.line = bufs

    copy = Gather.copy

    def add(self, target, *sources):
        if len(sources) == 2:
            target[...] = sources[0][...] + sources[1][...]
            return
        total = sources[0][...].astype(f32)
        for source in sources[1:]:
            total = total + source[...].astype(f32)
        target[...] = total.astype(target.dtype)

    def stage(self, number):
        y, x, z, c = place()
        at_x, at_y, at_d, at = y * 2 + 1 - x, (1 - y) * 2 + x, (1 - y) * 2 + 1 - x, y * 2 + x
        to_x, to_y, to_c = device(y, 1 - x, z, c), device(1 - y, x, z, c), device(y, x, z, 1 - c)
        to_d = device(1 - y, 1 - x, z, c)
        cols = pl.ds(*self.cols)
        half, diag, side, line = self.half, self.diag, self.side, self.line
        mine = lambda dp: self.part.at[dp, :, c, :, cols]
        low, high = pl.ds(0, 2), pl.ds(2, 2)
        blocks = (at_d, at_x, at_y, at)
        out = [(self.part.at[dp, :, 1 - c, :, cols], half.at[dp], to_c) for dp in blocks]
        if self.direct:
            out += [
                (half.at[at_d], diag, to_d),
                None,
                (half.at[at_x], side.at[0], to_x),
                (half.at[at_y], side.at[1], to_y),
            ]
        else:
            out += [
                (half.at[at_d, low], diag.at[0], to_x),
                (half.at[at_d, high], diag.at[1], to_y),
                (half.at[at_x], side.at[0], to_x),
                (half.at[at_y], side.at[1], to_y),
            ]
        out += [
            (half.at[at, (z + k) % 4], line.at[k - 1], device(y, x, (z + k) % 4, c))
            for k in (1, 2, 3)
        ]
        arrived = lambda msg: self.copy(msg, *out[msg][1:2] * 2, to_c).wait_recv()
        start = lambda msg: self.copy(msg, *out[msg]).start()

        def halve(msg):
            self.copy(msg, half.at[blocks[msg]], half.at[blocks[msg]], to_c).wait_recv()
            self.add(half.at[blocks[msg]], half.at[blocks[msg]], mine(blocks[msg]))

        if number == 0:
            for msg in range(4):
                start(msg)
        elif number == 1:
            halve(0)
            start(4)
            if not self.direct:
                start(5)
            halve(1)
            if self.direct:
                start(6)
            halve(2)
            if self.direct:
                start(7)
            halve(3)
        elif number == 2 and not self.direct:
            arrived(5)
            late = half.at[at_x, high]
            self.add(late, late, diag.at[1])
            start(6)
            arrived(4)
            late = half.at[at_y, low]
            self.add(late, late, diag.at[0])
            start(7)
        elif number == 3:
            own = half.at[at]
            if self.direct:
                arrived(4)
            arrived(6)
            arrived(7)
            self.add(own, own, side.at[0], side.at[1], *((diag,) if self.direct else ()))
            for k in (1, 2, 3):
                start(7 + k)
        elif number == 4:
            for k in (1, 2, 3):
                arrived(7 + k)
            total = half[at, z].astype(f32) + line[0].astype(f32)
            self.write(total + line[1].astype(f32) + line[2].astype(f32))
        elif number == 5:
            for msg, ends in enumerate(out):
                if ends is not None:
                    self.copy(msg, *ends).wait_send()


class Total:
    def __init__(self, value, out, bufs, send, recv, group):
        self.value, self.out, self.send, self.recv, self.group = value, out, send, recv, group
        self.line, self.plane, self.pair = bufs

    copy = Gather.copy

    def stage(self, number):
        y, x, z, c = place()
        at_x, at_y, at_d, at = y * 2 + 1 - x, (1 - y) * 2 + x, (1 - y) * 2 + 1 - x, y * 2 + x
        to_c = device(y, x, z, 1 - c)
        line, plane, pair = self.line, self.plane, self.pair
        out = [(line.at[z], device(y, x, (z + k) % 4, c)) for k in (1, 2, 3)] + [
            (plane.at[at], device(y, 1 - x, z, c)),
            (plane.at[at], device(1 - y, x, z, c)),
            (plane.at[at], device(1 - y, 1 - x, z, c)),
            (pair.at[c], to_c),
        ]
        came = [line.at[(z + 4 - k) % 4] for k in (1, 2, 3)]
        came += [plane.at[dp] for dp in (at_x, at_y, at_d)] + [pair.at[1 - c]]

        def start(msg):
            self.copy(msg, out[msg][0], out[msg][0], out[msg][1]).start()

        def arrived(msg):
            self.copy(msg, came[msg], came[msg], to_c).wait_recv()

        if number == 0:
            line[z] = self.value[...]
            for msg in (0, 1, 2):
                start(msg)
        elif number == 1:
            for msg in (0, 1, 2):
                arrived(msg)
            plane[at] = line[0] + line[1] + line[2] + line[3]
            for msg in (3, 4, 5):
                start(msg)
        elif number == 2:
            for msg in (3, 4, 5):
                arrived(msg)
            pair[c] = plane[0] + plane[1] + plane[2] + plane[3]
            start(6)
        elif number == 3:
            arrived(6)
            self.out[...] = pair[0] + pair[1]
        elif number == 5:
            for msg in range(7):
                self.copy(msg, out[msg][0], out[msg][0], out[msg][1]).wait_send()


GATHER_HOOKS = {
    "start": ((0, 0), (0, 1)) + tuple((0, i) for i in range(2, 10)),
    "first": ((1, 0), (1, 1), (1, 2), (2, 0), (2, 1), (1, 3), (3, 0), (3, 1), (4, 0)),
    0: ((1, 4), (2, 2), (1, 5), (4, 1)),
    1: ((3, 2), (2, 3), (1, 6), (4, 2)),
    2: ((3, 3), (2, 4), (2, 5), (1, 7), (4, 3)),
    3: ((3, 4), (3, 5), (2, 6), (1, 8), (4, 4)),
    "out": ((2, 7), (3, 6), (1, 9), (4, 5)),
    "up": ((3, 7), (4, 6), (4, 7)),
    "up1": ((2, 8),),
    "up2": ((3, 8), (2, 9)),
    "down": ((3, 9), (4, 8), (4, 9)) + tuple((5, i) for i in range(10)),
}


def gather_plan(width, hidden):
    half = hidden // 256 * 128
    plan = [(0, (0, width))] + [(1, (pair * 384, 384)) for pair in range(width // 128)]
    plan += [(2, (0, width))]
    return plan + [(which, cols) for which in (3, 4) for cols in ((0, half), (half, hidden - half))]


def forward_kernel(fast, *refs):
    refs = list(refs)
    take = lambda count: [refs.pop(0) for _ in range(count)]
    cameras, tokens, features, cotangent_in = take(4)
    shards = take(5)
    b_query, b_value, b_out, gain_first, shift_first = take(5)
    b_up, b_down, gain_second, shift_second, b_feat = take(5)
    stored = take(14)
    probs, dots, small = take(3)
    wholes_out = take(2) if fast else []
    kept = take(14)
    output, start_low, q_rows, k_rows, v_rows, dmix_high, dmix_low = kept[:7]
    grad_first, act, gin, normed_low, grad_branch, grad_att, mixed_low = kept[7:]
    first, work, mixed, inverse, q_cat, v_cat, k_cat, cotangent, sums, sums_up = take(10)
    prob_sem, load_sem, store_sem, step_sem = take(4)
    w_feat, w_qkv, w_out, w_up, w_down = take(5) if fast else shards
    width = tokens.shape[1]
    hidden = w_up.shape[-1]
    heads = width // HEAD
    pairs = heads // 2
    limit = 2 + CAM_LEN * cameras[0]
    if fast:
        turned_shard, send, recv, local = take(4)
        for pair in range(pairs):
            for i in range(3):
                at = i * width + pair * 128
                turned_shard[:, pair * 384 + i * 128 : pair * 384 + i * 128 + 128] = shards[1][
                    :, at : at + 128
                ]
        shards[1] = turned_shard
        wholes = (w_feat, w_qkv, w_out, w_up, w_down)
        gather = [
            Gather(shards[which], wholes[which], cols, send, recv, local, i)
            for i, (which, cols) in enumerate(gather_plan(width, hidden))
        ]
        greet()

    def hook(where):
        if fast:
            turns(gather, *GATHER_HOOKS[where])

    def hooks(step, where):
        if fast:
            for at_step, name in where:

                @pl.when(step == at_step)
                def _():
                    hook(name)

    def rows_of(step):
        return pl.ds(pl.multiple_of(step * STEP, 16), STEP)

    def row_ids(step):
        return step * STEP + lax.broadcasted_iota(jnp.int32, (STEP, 1), 0)

    def store(i, source=None, target=None):
        return pltpu.make_async_copy(
            kept[i] if source is None else source,
            stored[i] if target is None else target,
            store_sem.at[i],
        )

    def store_step(i, step):
        which = 0 if i == 8 else 1
        rows = rows_of(step)
        return pltpu.make_async_copy(
            kept[i].at[rows, :], stored[i].at[rows, :], step_sem.at[4 * which + step]
        )

    hook("start")
    loads = [
        pltpu.make_async_copy(
            source.at[pl.ds(0, ROWS), :], act.at[:, pl.ds(i * width, width)], load_sem.at[i]
        )
        for i, source in enumerate((features, tokens))
    ]
    loads.append(
        pltpu.make_async_copy(cotangent_in.at[pl.ds(0, ROWS), :], cotangent, load_sem.at[2])
    )
    for load in loads:
        load.start()
    hook("first")
    for load in loads:
        load.wait()

    def project(step, carry):
        rows = rows_of(step)
        ids = row_ids(step)
        camera = jnp.logical_and(ids >= 2, ids < limit)
        memory = dg(act[rows, :width], matrix(w_feat), 1, 0) + line_of(b_feat)
        start = act[rows, width : 2 * width].astype(f32) + jnp.where(camera, memory, 0.0)
        first[rows, :] = start
        start_low[rows, :] = start.astype(bf16)
        return carry

    lax.fori_loop(0, 4, project, 0)
    store(1).start()

    lane_valid = lax.broadcasted_iota(jnp.int32, (1, ROWS), 1) < limit

    def prob_copy(pair, side):
        source = act if side == 0 else gin
        at = pl.ds(pl.multiple_of(lax.rem(pair, 2) * 1280, 128), 1280)
        return pltpu.make_async_copy(
            source.at[:, at], probs.at[2 * pair + side], prob_sem.at[2 * lax.rem(pair, 2) + side]
        )

    def attend(pair, carry):
        lanes = pl.ds(pl.multiple_of(pair * 128, 128), 128)
        hooks(pair, [(i, i) for i in range(pairs)])

        @pl.when(pair >= 2)
        def _():
            prob_copy(pair - 2, 0).wait()
            prob_copy(pair - 2, 1).wait()

        w_pair = matrix(w_qkv, pl.ds(pl.multiple_of(pair * 384, 128), 384))
        for step in range(4):
            rows = slice(step * STEP, step * STEP + STEP)
            part = dg(start_low[rows, :], w_pair, 1, 0)
            q_rows[rows, lanes] = ((part[:, :128] + line_of(b_query, lanes)) * 0.125).astype(bf16)
            keys = part[:, 128:256]
            if step == 0:
                lead = keys[0:1]
            keys = jnp.where(row_ids(step) < limit, keys, lead).astype(bf16)
            k_rows[rows, lanes] = keys
            k_cat[rows, :128] = keys
            k_cat[rows, 128:] = keys
            v_rows[rows, lanes] = (part[:, 256:] + line_of(b_value, lanes)).astype(bf16)
        queries = q_rows[:, lanes].astype(f32).T * LOG2E
        high, low = split_low(queries)
        none = jnp.zeros((HEAD, ROWS), bf16)
        values = jnp.where(lane_valid, v_rows[:, lanes].astype(f32).T, 0.0).astype(bf16)
        ones = jnp.broadcast_to(jnp.where(lane_valid, 1.0, 0.0), (HEAD, ROWS)).astype(bf16)
        for side in range(2):
            own = slice(side * HEAD, side * HEAD + HEAD)
            other = slice((1 - side) * HEAD, (1 - side) * HEAD + HEAD)
            q_cat[side, own, :] = high[own]
            q_cat[side, other, :] = none
            q_cat[side, 128 + side * HEAD : 128 + side * HEAD + HEAD, :] = low[own]
            q_cat[side, 128 + (1 - side) * HEAD : 128 + (1 - side) * HEAD + HEAD, :] = none
            v_cat[side, :HEAD, :] = values[own]
            v_cat[side, HEAD:, :] = ones
        base = lax.rem(pair, 2) * 1280
        jobs = [(side, at, size) for side in range(2) for at, size in QBLOCKS]
        peak = {}

        def score(job, at_key, keys_here):
            side, at, size = jobs[job]
            here = slice(at_key, at_key + keys_here)
            scores = dg(k_cat[here, :], q_cat[side, :, at : at + size], 1, 0)
            work[job % 3 * 4 + at_key // STEP, :, :size] = scores
            high_here = jnp.max(scores, axis=0, keepdims=True)
            peak[job] = jnp.maximum(peak[job], high_here) if job in peak else high_here

        def weigh(job, at_key, keys_here):
            side, at, size = jobs[job]
            slot = act if side == 0 else gin
            here = slice(at_key, at_key + keys_here)
            slot[here, pl.ds(pl.multiple_of(base + at, 128), size)] = jnp.exp2(
                work[job % 3 * 4 + at_key // STEP, :, :size] - peak[job]
            ).astype(bf16)

        def mix(job):
            side, at, size = jobs[job]
            slot = act if side == 0 else gin
            weight = slot[:, pl.ds(pl.multiple_of(base + at, 128), size)]
            summed = dg(v_cat[side], weight, 1, 0)
            inv = 1.0 / summed[HEAD : HEAD + 1]
            mixed[pl.ds(pl.multiple_of(pair * 128 + side * HEAD, 8), HEAD), at : at + size] = (
                summed[:HEAD] * inv
            )
            inverse[2 * pair + side, :, at : at + size] = inv

        parts = chunks(ROWS, STEP)
        for job in (0, 1):
            for part in parts:
                score(job, *part)
        for job in range(len(jobs)):
            for part in parts:
                if job + 2 < len(jobs):
                    score(job + 2, *part)
                weigh(job, *part)
            if job >= 2:
                mix(job - 2)
            if job == len(QBLOCKS) - 1:
                prob_copy(pair, 0).start()
        mix(len(jobs) - 2)
        mix(len(jobs) - 1)
        prob_copy(pair, 1).start()
        return carry

    lax.fori_loop(0, pairs, attend, 0)
    for pair in (pairs - 2, pairs - 1):
        for side in range(2):
            prob_copy(pair, side).wait()

    for i in (2, 3, 4):
        store(i).start()
    hook("out")
    mixed_low[...] = mixed[...].astype(bf16)
    store(13).start()
    for at, size in chunks(width, 256):
        cols = slice(at, at + size)
        first[:, cols] += dg(mixed_low[...], matrix(w_out, cols), 0, 0) + line_of(b_out, cols)
    sums[...] = jnp.zeros_like(sums)
    sums_up[...] = jnp.zeros_like(sums_up)
    cuts = chunks(hidden, 512)
    hook("up")

    def widen(step, carry):
        hooks(step, [(1, "up1"), (2, "up2")])
        rows = rows_of(step)
        unit_first, scale_first = norm_parts(first[rows, :])
        low = (unit_first * line_of(gain_first) + line_of(shift_first)).astype(bf16)
        normed_low[rows, :] = low
        for at, size in cuts:
            cols = slice(at, at + size)
            inner = dg(low, matrix(w_up, cols), 1, 0) + line_of(b_up, cols)
            square = inner * inner
            half = 0.5 + 0.5 * jnp.tanh(inner * (GELU_C + (GELU_C * GELU_A) * square))
            value = inner * half
            act[rows, cols] = value.astype(bf16)
            slope = half + value * (1.0 - half) * (2 * GELU_C + (6 * GELU_C * GELU_A) * square)
            gin[rows, cols] = slope.astype(bf16)
        store_step(8, step).start()
        return carry

    lax.fori_loop(0, 4, widen, 0)
    store(10).start()
    hook("down")

    def feed(step, carry):
        rows = rows_of(step)
        valid = row_ids(step) < limit
        unit_first, scale_first = norm_parts(first[rows, :])
        normed = unit_first * line_of(gain_first) + line_of(shift_first)
        branch = dg(act[rows, :], matrix(w_down), 1, 1) + line_of(b_down)
        unit_second, scale_second = norm_parts(normed + branch)
        final = unit_second * line_of(gain_second) + line_of(shift_second)
        output[rows, :] = jnp.where(valid, final, 0.0).astype(bf16)
        grad = jnp.where(valid, cotangent[rows, :].astype(f32), 0.0)
        sums[0] += fold(grad * unit_second)
        sums[1] += fold(grad)
        grad_second = norm_back(grad, unit_second, scale_second, line_of(gain_second))
        low_branch = grad_second.astype(bf16)
        grad_branch[rows, :] = low_branch
        sums[2] += fold(low_branch.astype(f32))
        for at, size in cuts:
            cols = slice(at, at + size)
            low_inner = (
                dg(low_branch, matrix(w_down, cols), 1, 0) * gin[rows, cols].astype(f32)
            ).astype(bf16)
            gin[rows, cols] = low_inner
            sums_up[:, cols] += fold(low_inner.astype(f32))
        store_step(9, step).start()
        grad_normed = grad_second + dg(gin[rows, :], matrix(w_up), 1, 1)
        sums[3] += fold(grad_normed * unit_first)
        sums[4] += fold(grad_normed)
        back = norm_back(grad_normed, unit_first, scale_first, line_of(gain_first))
        grad_first[rows, :] = back
        low_att = back.astype(bf16)
        grad_att[rows, :] = low_att
        sums[5] += fold(low_att.astype(f32))
        return carry

    lax.fori_loop(0, 4, feed, 0)
    output[ROWS:, :] = jnp.zeros((SLOTS - ROWS, width), bf16)
    for i in (0, 7, 11, 12):
        store(i).start()
    small[...] = jnp.zeros_like(small)
    for i in range(6):
        small[i : i + 1, :] = jnp.sum(sums[i], axis=0, keepdims=True)
    for i, (at, size) in enumerate(chunks(hidden, width)):
        small[6 + i : 7 + i, :size] = jnp.sum(sums_up[:, at : at + size], axis=0, keepdims=True)
    if fast:
        whole_copies = [
            store(14 + i, source, target)
            for i, (source, target) in enumerate(zip((w_feat, w_qkv), wholes_out))
        ]
        for copy in whole_copies:
            copy.start()

    for at, size in QBLOCKS:
        cols = slice(at, at + size)
        grad_mixed = dg(matrix(w_out), grad_att[cols, :], 1, 1).astype(bf16).astype(f32)
        scaled = grad_mixed.reshape(heads, HEAD, size) * inverse[:, :, cols]
        dots[:, :, cols] = jnp.sum(
            scaled * mixed[:, cols].reshape(heads, HEAD, size), axis=1, keepdims=True
        )
        high, low = split_low(scaled.reshape(width, size))
        dmix_high[:, cols] = high
        dmix_low[:, cols] = low
    for i in (5, 6):
        store(i).start()
    for step in range(4):
        store_step(8, step).wait()
        store_step(9, step).wait()
    for i in (0, 1, 2, 3, 4, 5, 6, 7, 10, 11, 12, 13):
        store(i).wait()
    if fast:
        for copy in whole_copies:
            copy.wait()


def shaped(shape, dtype):
    return jax.ShapeDtypeStruct(shape, dtype)


def forward_call(fast, cameras, tokens, features, cotangent, weights, biases):
    width = tokens.shape[1]
    hidden = weights[3].shape[1]
    heads = width // HEAD
    token_rows = shaped((ROWS, width), bf16)
    kept = (shaped((SLOTS, width), bf16),) + (token_rows,) * 4 + (shaped((width, ROWS), bf16),) * 2
    kept += (shaped((ROWS, width), f32),) + (shaped((ROWS, hidden), bf16),) * 2
    kept += (token_rows,) * 3 + (shaped((width, ROWS), bf16),)
    wholes = [(4, 4, 2) + w.shape for w in weights]
    outs = kept + (
        shaped((heads, ROWS, 1280), bf16),
        shaped((heads, 1, ROWS), f32),
        shaped((-(-(6 + -(-hidden // width)) // 8) * 8, width), f32),
    )
    if fast:
        outs += tuple(shaped(whole, bf16) for whole in wholes[:2])
    vmem = pl.BlockSpec(memory_space=pltpu.VMEM)
    hbm = pl.BlockSpec(memory_space=pl.ANY)
    groups = len(gather_plan(width, hidden))
    return pl.pallas_call(
        functools.partial(forward_kernel, fast),
        out_shape=outs,
        in_specs=[pl.BlockSpec(memory_space=pltpu.SMEM)] + [hbm] * 3 + [vmem] * 15,
        out_specs=tuple(vmem if i in (15, 16) else hbm for i in range(len(outs))),
        scratch_shapes=[pltpu.VMEM(k.shape, k.dtype) for k in kept]
        + [
            pltpu.VMEM((ROWS, width), f32),
            pltpu.VMEM((12, STEP, 256), f32),
            pltpu.VMEM((width, ROWS), f32),
            pltpu.VMEM((heads, 1, ROWS), f32),
            pltpu.VMEM((2, 256, ROWS), bf16),
            pltpu.VMEM((2, 128, ROWS), bf16),
            pltpu.VMEM((ROWS, 256), bf16),
            pltpu.VMEM((ROWS, width), bf16),
            pltpu.VMEM((6, 8, width), f32),
            pltpu.VMEM((8, hidden), f32),
            pltpu.SemaphoreType.DMA((4,)),
            pltpu.SemaphoreType.DMA((3,)),
            pltpu.SemaphoreType.DMA((16,)),
            pltpu.SemaphoreType.DMA((8,)),
        ]
        + fast
        * (
            [pltpu.VMEM(whole, bf16) for whole in wholes]
            + [
                pltpu.VMEM(weights[1].shape, bf16),
                pltpu.SemaphoreType.DMA((groups, MESSAGES)),
                pltpu.SemaphoreType.DMA((groups, MESSAGES)),
                pltpu.SemaphoreType.DMA((groups,)),
            ]
        ),
        compiler_params=pltpu.CompilerParams(
            vmem_limit_bytes=62 * MIB,
            collective_id=0 if fast else None,
            has_side_effects=fast,
        ),
        name="layer_forward",
    )(cameras, tokens, features, cotangent, *weights, *biases)


TAIL = 1280


def reduce_plan(width, hidden):
    cuts = ((0, TAIL), (TAIL, TAIL), (2 * TAIL, hidden - 2 * TAIL))
    plan = [(which, cols, False) for which in (0, 1) for cols in cuts]
    plan += [(2, (0, width), False)]
    pairs = width // 128
    plan += [(3, (pair * 384, 384), pair == pairs - 1) for pair in range(pairs)]
    return plan + [(4, (0, width), True)]


REDUCE_HOOKS = {
    "start": ((0, 12),),
    "out": ((0, 6),),
    "tails": ((0, 5), (0, 2), (1, 6)),
    "up0": ((0, 3), (1, 5), (1, 12)),
    "up1": ((0, 4), (1, 2)),
    "down0": ((0, 0), (1, 3), (2, 6)),
    "down1": ((0, 1), (1, 4), (2, 5)),
    (0, 0): ((2, 2), (2, 12)),
    (0, 1): ((1, 0),),
    (0, 2): ((2, 3), (1, 1), (3, 12)),
    (1, 0): ((2, 4), (0, 7), (3, 6)),
    (1, 1): ((1, 7), (3, 5)),
    (1, 2): ((2, 0), (3, 2)),
    (2, 0): ((0, 8), (2, 1)),
    (2, 1): ((1, 8), (2, 7), (3, 3)),
    (2, 2): ((3, 4),),
    (3, 0): ((0, 9), (2, 8)),
    (3, 1): ((1, 9), (3, 0)),
    (3, 2): ((3, 1),),
    "pairs": ((0, 10), (2, 9), (3, 7)),
    "rows0": ((1, 10),),
    "rows1": ((3, 8),),
    "rows2": ((4, 6), (4, 5), (4, 2), (3, 9), (5, 6), (5, 5), (5, 2), (5, 12)),
    "feat": ((0, 11), (0, 13), (4, 3), (5, 3)),
    "half": ((1, 11), (1, 13), (3, 10), (4, 4), (4, 0), (4, 1), (5, 4), (5, 0), (5, 1)),
    "end": ((2, 13), (4, 7), (4, 8), (4, 9), (5, 7), (5, 8), (5, 9), (3, 11), (4, 10), (5, 10))
    + ((3, 13), (5, 13), (4, 11), (5, 11)),
}


def put(target, cols, value):
    if len(target.shape) == 2:
        target[:, cols] = value
    else:
        target[:, :, :, :, cols] = value.reshape(target.shape[:4] + value.shape[1:])


def backward_kernel(fast, *refs):
    refs = list(refs)
    take = lambda count: [refs.pop(0) for _ in range(count)]
    cameras, features, probs, dots, act, gin, *wgrad_in = take(10)
    inputs = take(9)
    small = take(1)[0] if fast else None
    grad_tokens, grad_features = take(2)
    if fast:
        summed, (total, total_late) = take(5), take(2)
        parts_of = take(5)
        small_late = take(1)[0]
    else:
        parts_of = take(5)
        small_late = take(1)[0]
    loaded = take(9)
    q_rows, k_rows, v_rows, dmix_high, dmix_low, start_low, grad_first, w_qkv, w_feat = loaded
    weights, grad_scores, joined, d_cat, d_rows, v_cat, k_turned, blank, sums = take(9)
    prob_sem, load_sem, wgrad_sem, out_sem = take(4)
    width = q_rows.shape[1]
    hidden = act.shape[1]
    heads = width // HEAD
    pairs = heads // 2
    limit = 2 + CAM_LEN * cameras[0]
    if fast:
        send, recv, local = refs[-3:]
        plan = reduce_plan(width, hidden)

        def writer(which, cols):
            def write(value):
                if which == 3:
                    pair = cols[0] // 384
                    for i in range(3):
                        at = i * width + pair * 128
                        summed[3][:, at : at + 128] = value[:, i * 128 : i * 128 + 128]
                else:
                    summed[which][:, cols[0] : cols[0] + cols[1]] = value

            return write

        groups = [
            Reduce(parts_of[which], cols, writer(which, cols), take(4), direct, send, recv, i)
            for i, (which, cols, direct) in enumerate(plan)
        ]
        groups.append(Total(small, total, take(3), send, recv, len(plan)))
        groups.append(Total(small_late, total_late, take(3), send, recv, len(plan) + 1))

    def hook(where):
        if fast:
            turns(groups, *REDUCE_HOOKS[where])

    def pair_hook(pair, spot):
        if fast:
            for at_pair in range(pairs):

                @pl.when(pair == at_pair)
                def _():
                    hook((at_pair, spot))

    mixed_low, normed_low = d_cat, joined.at[:, pl.ds(0, width)]
    grad_branch, grad_att = joined.at[:, pl.ds(width, width)], joined.at[:, pl.ds(2 * width, width)]
    tail = pl.ds(2 * TAIL, hidden - 2 * TAIL)
    act_tail = weights.at[2, :, pl.ds(0, hidden - 2 * TAIL)]
    gin_tail = weights.at[2, :, pl.ds(hidden - 2 * TAIL, hidden - 2 * TAIL)]
    ends = [
        (wgrad_in[3], mixed_low),
        (wgrad_in[2], grad_att),
        (wgrad_in[0], normed_low),
        (gin.at[:, tail], gin_tail),
        (wgrad_in[1], grad_branch),
        (act.at[:, tail], act_tail),
        (gin.at[:, pl.ds(0, TAIL)], weights.at[3]),
        (gin.at[:, pl.ds(TAIL, TAIL)], grad_scores.at[0]),
        (act.at[:, pl.ds(0, TAIL)], weights.at[0]),
        (act.at[:, pl.ds(TAIL, TAIL)], weights.at[1]),
    ]
    fetch = [
        pltpu.make_async_copy(source, target, wgrad_sem.at[i])
        for i, (source, target) in enumerate(ends)
    ]
    loads = [
        pltpu.make_async_copy(source, target, load_sem.at[i])
        for i, (source, target) in enumerate(zip(inputs, loaded))
    ]
    for copy in fetch + loads:
        copy.start()
    if fast:
        greet()
    hook("start")

    def prob_copy(pair, side):
        slot = 2 * lax.rem(pair + 1, 2) + side
        return pltpu.make_async_copy(
            probs.at[2 * pair + side], weights.at[slot], prob_sem.at[slot]
        )

    def weight_grad(which, left, right, at, size):
        def part(turn, carry):
            cut = pl.multiple_of(turn * 512, 512)
            grad = dg(left[...], right[:, pl.ds(cut, 512)], 0, 0).astype(bf16)
            put(parts_of[which], pl.ds(at + cut, 512), grad)
            return carry

        lax.fori_loop(0, size // 512, part, 0)
        if size % 512:
            cut, wide = size // 512 * 512, size % 512
            grad = dg(left[...], right[:, cut : cut + wide], 0, 0).astype(bf16)
            put(parts_of[which], pl.ds(at + cut, wide), grad)

    fetch[0].wait()
    fetch[1].wait()
    grad = dg(mixed_low[...].reshape(width, ROWS), grad_att[...], 1, 0).astype(bf16)
    put(parts_of[2], pl.ds(0, width), grad)
    hook("out")
    fetch[2].wait()
    fetch[3].wait()
    weight_grad(1, normed_low, gin_tail, 2 * TAIL, hidden - 2 * TAIL)
    fetch[4].wait()
    fetch[5].wait()
    weight_grad(0, grad_branch, act_tail, 2 * TAIL, hidden - 2 * TAIL)
    hook("tails")
    fetch[6].wait()
    weight_grad(1, normed_low, weights.at[3], 0, TAIL)
    hook("up0")
    for side in range(2):
        prob_copy(0, side).start()
    fetch[7].wait()
    weight_grad(1, normed_low, grad_scores.at[0], TAIL, TAIL)
    hook("up1")
    fetch[8].wait()
    weight_grad(0, grad_branch, weights.at[0], 0, TAIL)
    hook("down0")
    fetch[9].wait()
    weight_grad(0, grad_branch, weights.at[1], TAIL, TAIL)
    hook("down1")
    for load in loads:
        load.wait()

    sums[...] = jnp.zeros_like(sums)
    lane_valid = lax.broadcasted_iota(jnp.int32, (1, ROWS), 1) < limit
    row_valid = lax.broadcasted_iota(jnp.int32, (ROWS, 1), 0) < limit
    none = jnp.zeros((HEAD, ROWS), bf16)

    def attend_back(pair, carry):
        lanes = pl.ds(pl.multiple_of(pair * 128, 128), 128)

        @pl.when(pair + 1 < pairs)
        def _():
            prob_copy(pair + 1, 0).start()
            prob_copy(pair + 1, 1).start()

        pair_hook(pair, 0)
        high = dmix_high[lanes, :]
        low = dmix_low[lanes, :]
        for side in range(2):
            own = slice(side * HEAD, side * HEAD + HEAD)
            mine, its = side * HEAD, (1 - side) * HEAD
            d_cat[side, mine : mine + HEAD, :] = high[own]
            d_cat[side, its : its + HEAD, :] = none
            d_cat[side, 128 + mine : 128 + mine + HEAD, :] = low[own]
            d_cat[side, 128 + its : 128 + its + HEAD, :] = none
        d_rows[:, :128] = high.astype(f32).T.astype(bf16)
        d_rows[:, 128:] = low.astype(f32).T.astype(bf16)
        values = v_rows[:, lanes]
        v_cat[:, :128] = values
        v_cat[:, 128:] = values
        k_turned[...] = jnp.where(lane_valid, k_rows[:, lanes].astype(f32).T, 0.0).astype(bf16)
        base = 2 * lax.rem(pair + 1, 2)
        jobs = [(side, at, size) for side in range(2) for at, size in QBLOCKS]
        parts = chunks(ROWS, STEP)
        turned = {0: [], 1: []}
        wide = {}

        def slope(job):
            side, at, size = jobs[job]
            offset = dots[2 * pair + side, :, at : at + size]
            for at_key, keys_here in parts:
                here = slice(at_key, at_key + keys_here)
                grad = dg(v_cat[here, :], d_cat[side, :, at : at + size], 1, 0) - offset
                weight = weights[base + side, here, at : at + size].astype(f32)
                grad_scores[side, here, at : at + size] = (weight * grad).astype(bf16)

        def queries(job):
            side, at, size = jobs[job]
            turned[side].append(
                dg(k_turned[...], grad_scores[side, :, at : at + size], 1, 0)[
                    side * HEAD : side * HEAD + HEAD
                ]
            )

        def spread(side, part):
            here = slice(part[0], part[0] + part[1])
            value = dg(weights[base + side, here, :ROWS], d_rows[...], 1, 0)
            value = value[:, :128] + value[:, 128:]
            key = dg(grad_scores[side, here, :ROWS], q_rows[:, lanes], 1, 0)
            wide[side, part] = (value, key)

        for side in range(2):
            prob_copy(pair, side).wait()
        for job in range(len(jobs)):
            if job == len(QBLOCKS):
                pair_hook(pair, 1)
            slope(job)
            if job >= 1:
                queries(job - 1)
            if job > len(QBLOCKS):
                side_job = job - len(QBLOCKS) - 1
                if side_job < len(parts):
                    spread(0, parts[side_job])
        queries(len(jobs) - 1)
        pair_hook(pair, 2)
        first_lane = lax.broadcasted_iota(jnp.int32, (STEP, 128), 1) < HEAD
        spot = lambda i: pl.ds(pl.multiple_of(pair * 384 + i * 128, 128), 128)
        for part in parts:
            spread(1, part)
            here = slice(part[0], part[0] + part[1])
            keep = row_valid[here]
            for which, i in ((0, 2), (1, 1)):
                value = jnp.where(first_lane, wide[0, part][which], wide[1, part][which])
                joined[here, spot(i)] = jnp.where(keep, value, 0.0).astype(bf16)
        query = jnp.concatenate(
            [jnp.concatenate(turned[0], axis=1), jnp.concatenate(turned[1], axis=1)], axis=0
        )
        joined[:, spot(0)] = (query.astype(bf16).astype(f32).T * 0.125).astype(bf16)
        at = pl.ds(pl.multiple_of(pair * 384, 128), 384)
        put(parts_of[3], at, dg(start_low[...], joined[:, at], 0, 0).astype(bf16))
        return carry

    lax.fori_loop(0, pairs, attend_back, 0)
    feats = weights.at[2, :, pl.ds(0, width)]
    tokens_out = weights.at[2, :, pl.ds(width, width)]
    features_out = weights.at[3, :, pl.ds(0, width)]
    grad_memory = grad_scores.at[0, :, pl.ds(0, width)]
    load = pltpu.make_async_copy(features.at[pl.ds(0, ROWS), :], feats, out_sem.at[0])
    load.start()
    blank[...] = jnp.zeros_like(blank)
    body, rest = pl.ds(0, ROWS), pl.ds(ROWS, SLOTS - ROWS)
    stores = [
        pltpu.make_async_copy(source, target, out_sem.at[1 + i])
        for i, (source, target) in enumerate(
            (
                (blank, grad_tokens.at[rest, :]),
                (blank, grad_features.at[rest, :]),
                (tokens_out, grad_tokens.at[body, :]),
                (features_out, grad_features.at[body, :]),
            )
        )
    ]
    stores[0].start()
    stores[1].start()
    hook("pairs")

    def project_back(step, carry):
        rows = pl.ds(pl.multiple_of(step * STEP, 16), STEP)
        ids = step * STEP + lax.broadcasted_iota(jnp.int32, (STEP, 1), 0)
        camera = jnp.logical_and(ids >= 2, ids < limit)
        part = joined[rows, :]
        for pair in range(pairs):
            lanes = slice(pair * 128, pair * 128 + 128)
            sums[0, :, lanes] += fold(part[:, pair * 384 : pair * 384 + 128].astype(f32))
            sums[1, :, lanes] += fold(part[:, pair * 384 + 256 : pair * 384 + 384].astype(f32))
        grad_start = grad_first[rows, :] + dg(part, w_qkv[...], 1, 1)
        tokens_out[rows, :] = grad_start.astype(bf16)
        low = jnp.where(camera, grad_start, 0.0).astype(bf16)
        grad_memory[rows, :] = low
        sums[2] += fold(low.astype(f32))
        if fast:
            for at_step in (0, 1, 2):

                @pl.when(step == at_step)
                def _():
                    hook(f"rows{at_step}")

        return carry

    lax.fori_loop(0, 4, project_back, 0)
    stores[2].start()
    load.wait()
    put(parts_of[4], pl.ds(0, width), dg(feats[...], grad_memory[...], 0, 0).astype(bf16))
    small_late[...] = jnp.zeros_like(small_late)
    for i in range(3):
        small_late[i : i + 1, :] = jnp.sum(sums[i], axis=0, keepdims=True)
    hook("feat")
    hook("half")

    def spread_back(step, carry):
        rows = pl.ds(pl.multiple_of(step * STEP, 16), STEP)
        features_out[rows, :] = dg(grad_memory[rows, :], w_feat[...], 1, 1).astype(bf16)
        return carry

    lax.fori_loop(0, 4, spread_back, 0)
    stores[3].start()
    hook("end")
    for copy in stores:
        copy.wait()


def backward_call(fast, cameras, features, saved, small):
    probs, dots, act, gin, normed_low, grad_branch, grad_att, mixed_low, *inputs = saved
    width, hidden = features.shape[1], act.shape[1]
    vmem = pl.BlockSpec(memory_space=pltpu.VMEM)
    hbm = pl.BlockSpec(memory_space=pl.ANY)
    rows = width // 32
    columns = (hidden, hidden, width, 3 * width, width)
    late = (8, width)
    outs = (shaped((SLOTS, width), bf16),) * 2
    scratch = []
    reduce_scratch = []
    args = [cameras, features, probs, dots, act, gin, normed_low, grad_branch, grad_att]
    args += [mixed_low.reshape(2, width // 2, ROWS), *inputs]
    specs = [pl.BlockSpec(memory_space=pltpu.SMEM), hbm, hbm, vmem] + [hbm] * 15
    if fast:
        outs += tuple(shaped((rows, n), f32) for n in columns)
        outs += (shaped(small.shape, f32), shaped(late, f32))
        args += [small]
        specs += [vmem]
        scratch += [pltpu.VMEM((4, 4, 2, rows, n), bf16) for n in columns] + [pltpu.VMEM(late, f32)]
        plan = reduce_plan(width, hidden)
        for which, (_, size), direct in plan:
            reduce_scratch += [
                pltpu.VMEM((4, 4, rows, size), bf16),
                pltpu.VMEM((4, rows, size) if direct else (2, 2, rows, size), bf16),
                pltpu.VMEM((2, 4, rows, size), bf16),
                pltpu.VMEM((3, rows, size), bf16),
            ]
        for shape in (small.shape, late):
            reduce_scratch += [pltpu.VMEM((count,) + shape, f32) for count in (4, 4, 2)]
        reduce_scratch += [
            pltpu.SemaphoreType.DMA((len(plan) + 2, MESSAGES)),
            pltpu.SemaphoreType.DMA((len(plan) + 2, MESSAGES)),
            pltpu.SemaphoreType.DMA((len(plan),)),
        ]
    else:
        outs += tuple(shaped((width, n), bf16) for n in columns) + (shaped(late, f32),)
    scratch += [pltpu.VMEM(a.shape, a.dtype) for a in inputs]
    scratch += [
        pltpu.VMEM((4, ROWS, 1280), bf16),
        pltpu.VMEM((2, ROWS, 1280), bf16),
        pltpu.VMEM((ROWS, 3 * width), bf16),
        pltpu.VMEM((2, 256, ROWS), bf16),
        pltpu.VMEM((ROWS, 256), bf16),
        pltpu.VMEM((ROWS, 256), bf16),
        pltpu.VMEM((128, ROWS), bf16),
        pltpu.VMEM((SLOTS - ROWS, width), bf16),
        pltpu.VMEM((3, 8, width), f32),
        pltpu.SemaphoreType.DMA((4,)),
        pltpu.SemaphoreType.DMA((9,)),
        pltpu.SemaphoreType.DMA((10,)),
        pltpu.SemaphoreType.DMA((5,)),
    ]
    return pl.pallas_call(
        functools.partial(backward_kernel, fast),
        out_shape=outs,
        in_specs=specs,
        out_specs=(hbm,) * 2 + (vmem,) * (len(outs) - 2),
        scratch_shapes=scratch + reduce_scratch,
        compiler_params=pltpu.CompilerParams(
            vmem_limit_bytes=62 * MIB,
            collective_id=1 if fast else None,
            has_side_effects=fast,
        ),
        name="layer_backward",
    )(*args)


def finish_kernel(*refs):
    refs = list(refs)
    take = lambda count: [refs.pop(0) for _ in range(count)]
    sources, (small, late), targets = take(8), take(2), take(8)
    vectors, sem = take(10), refs[0]
    copies = [
        pltpu.make_async_copy(source, target, sem.at[i])
        for i, (source, target) in enumerate(zip(sources, targets))
    ]
    for copy in copies:
        copy.start()
    places = ((late, 0), (late, 1), (small, 5), (small, 3), (small, 4), None)
    places += ((small, 2), (small, 0), (small, 1), (late, 2))
    for vector, spot in zip(vectors, places):
        if spot is None:
            for i, (at, size) in enumerate(chunks(vector.shape[0], small.shape[1])):
                vector[at : at + size] = small[6 + i, :size]
        else:
            vector[...] = spot[0][spot[1]]
    for copy in copies:
        copy.wait()


def finish_call(large, small, late, hidden):
    width = small.shape[1]
    vmem = pl.BlockSpec(memory_space=pltpu.VMEM)
    hbm = pl.BlockSpec(memory_space=pl.ANY)
    return pl.pallas_call(
        finish_kernel,
        out_shape=tuple(shaped(a.shape, a.dtype) for a in large)
        + tuple(shaped((hidden if i == 5 else width,), f32) for i in range(10)),
        in_specs=[vmem] * 10,
        out_specs=(hbm,) * 8 + (vmem,) * 10,
        scratch_shapes=[pltpu.SemaphoreType.DMA((8,))],
        name="place_outputs",
    )(*large, small, late)


AXES = ("dp", "fsdp")


def on_device(
    fast,
    tokens,
    features,
    cameras,
    cotangent,
    w_qkv,
    w_out,
    w_up,
    w_down,
    w_feat,
    *biases,
):
    width = tokens.shape[1]
    hidden = w_up.shape[1]
    pairs = width // 128
    weights = (w_feat, w_qkv, w_out, w_up, w_down)
    if not fast:
        weights = [lax.all_gather(w, AXES, axis=0, tiled=True) for w in weights]
        by_pair = weights[1].reshape(width, 3, pairs, 128).transpose(0, 2, 1, 3)
        weights[1] = by_pair.reshape(width, 3 * width)
    output, *kept = forward_call(fast, cameras, tokens, features, cotangent, weights, biases)
    start_low, q_rows, k_rows, v_rows, dmix_high, dmix_low, grad_first, *kept = kept
    act, gin, normed_low, grad_branch, grad_att, mixed_low, probs, dots, small, *wholes = kept
    if fast:
        weights = [whole.reshape(width, -1) for whole in wholes]
    saved = (probs, dots, act, gin, normed_low, grad_branch, grad_att, mixed_low)
    saved += (q_rows, k_rows, v_rows, dmix_high, dmix_low, start_low, grad_first)
    saved += (weights[1], weights[0])
    grad_tokens, grad_features, *grads = backward_call(fast, cameras, features, saved, small)
    if fast:
        *grads, small, late = grads
    else:
        *grads, late = grads
        by_pair = grads[3].reshape(width, pairs, 3, 128).transpose(0, 2, 1, 3)
        grads[3] = by_pair.reshape(width, 3 * width)
        grads = [
            lax.psum_scatter(
                lax.optimization_barrier(grad.astype(f32)), AXES, scatter_dimension=0, tiled=True
            )
            for grad in grads
        ]
        small, late = lax.psum((small, late), AXES)
    grad_down, grad_up, grad_out, grad_qkv, grad_feat = grads
    large = (output, grad_tokens, grad_features, grad_qkv, grad_out, grad_up, grad_down, grad_feat)
    return finish_call(large, small, late, hidden)


def solution(mesh):
    split = P(AXES, None)
    fast = mesh.shape["dp"] == 4 and mesh.shape["fsdp"] == 8
    return jax.shard_map(
        functools.partial(on_device, fast),
        mesh=mesh,
        in_specs=(split, split, P(AXES), split) + (split,) * 5 + (P(),) * 10,
        out_specs=(split,) * 8 + (P(),) * 10,
        check_vma=False,
    )
```

```python
import functools

import jax
import jax.numpy as jnp
from jax import lax
from jax.experimental import pallas as pl
from jax.experimental.pallas import tpu as pltpu
from jax.sharding import PartitionSpec as P

HEAD = 64
SLOTS = 1280
CAM_LEN = 300
CAMS_MAX = 4
NORM_EPS = 1e-05
LOG2E = 1.4426950408889634
GELU_C = 0.7978845608028654
GELU_A = 0.044715

ROWS = -(-(2 + CAM_LEN * CAMS_MAX) // 64) * 64
STEP = ROWS // 4
QBLOCKS = [(at, min(256, ROWS - at)) for at in range(0, ROWS, 256)]
MIB = 2**20

bf16 = jnp.bfloat16
f32 = jnp.float32


def dg(left, right, over_left, over_right):
    return lax.dot_general(
        left, right, (((over_left,), (over_right,)), ((), ())), preferred_element_type=f32
    )


def chunks(total, width):
    return [(at, min(width, total - at)) for at in range(0, total, width)]


def norm_parts(value):
    average = jnp.mean(value, axis=-1, keepdims=True)
    centered = value - average
    variance = jnp.mean(centered * centered, axis=-1, keepdims=True)
    scale = lax.rsqrt(variance + NORM_EPS)
    return centered * scale, scale


def norm_back(grad, unit, scale, gain):
    inside = grad * gain
    one = jnp.mean(inside, axis=-1, keepdims=True)
    two = jnp.mean(inside * unit, axis=-1, keepdims=True)
    return scale * (inside - one - unit * two)


def line_of(ref, cols=slice(None)):
    return ref[cols].reshape(1, -1)


def fold(value):
    rows, width = value.shape
    return jnp.sum(value.reshape(rows // 8, 8, width), axis=0)


def split_low(value):
    high = value.astype(bf16)
    return high, (value - high.astype(f32)).astype(bf16)


MESH = pl.DeviceIdType.MESH
MESSAGES = 11


def place():
    dp = lax.axis_index("dp")
    fs = lax.axis_index("fsdp")
    return dp // 2, dp % 2, fs // 2, fs % 2


def device(y, x, z, c):
    return (y * 2 + x, z * 2 + c)


def neighbours():
    y, x, z, c = place()
    around = [device(y, x, (z + k) % 4, c) for k in (1, 2, 3)]
    return around + [
        device(y, 1 - x, z, c),
        device(1 - y, x, z, c),
        device(1 - y, 1 - x, z, c),
        device(y, x, z, 1 - c),
    ]


def greet():
    barrier = pltpu.get_barrier_semaphore()
    peers = neighbours()
    for peer in peers:
        pl.semaphore_signal(barrier, inc=1, device_id=peer, device_id_type=MESH)
    pl.semaphore_wait(barrier, len(peers))


class Gather:
    def __init__(self, shard, whole, cols, send, recv, local, group):
        self.shard, self.whole, self.cols, self.send, self.recv = shard, whole, cols, send, recv
        self.local, self.group = local, group

    def copy(self, msg, source, target, peer):
        return pltpu.make_async_remote_copy(
            src_ref=source,
            dst_ref=target,
            send_sem=self.send.at[self.group, msg],
            recv_sem=self.recv.at[self.group, msg],
            device_id=peer,
            device_id_type=MESH,
        )

    def stage(self, number):
        y, x, z, c = place()
        at_x, at_y, at_d, at = y * 2 + 1 - x, (1 - y) * 2 + x, (1 - y) * 2 + 1 - x, y * 2 + x
        to_x, to_y, to_c = device(y, 1 - x, z, c), device(1 - y, x, z, c), device(y, x, z, 1 - c)
        cols = pl.ds(*self.cols)
        whole = lambda dp, line, core: self.whole.at[dp, line, core, :, cols]
        own = whole(at, z, c)
        shard = self.shard.at[:, cols]
        every, low, high = slice(None), pl.ds(0, 2), pl.ds(2, 2)
        out = [(shard, own, device(y, x, (z + k) % 4, c)) for k in (1, 2, 3)] + [
            (part, part, peer)
            for part, peer in (
                (whole(at, every, c), to_x),
                (whole(at, every, c), to_y),
                (whole(at_x, low, c), to_y),
                (whole(at_y, high, c), to_x),
                (whole(at, every, c), to_c),
                (whole(at_x, every, c), to_c),
                (whole(at_y, every, c), to_c),
                (whole(at_d, every, c), to_c),
            )
        ]
        arrived = lambda msg, part: self.copy(msg, part, part, to_c).wait_recv()
        start = lambda msg: self.copy(msg, *out[msg]).start()
        if number == 0:
            keep = pltpu.make_async_copy(shard, own, self.local.at[self.group])
            keep.start()
            for msg in (0, 1, 2):
                start(msg)
            keep.wait()
        elif number == 1:
            for k in (1, 2, 3):
                arrived(k - 1, whole(at, (z + 4 - k) % 4, c))
            for msg in (3, 4, 7):
                start(msg)
        elif number == 2:
            arrived(3, whole(at_x, every, c))
            start(5)
            arrived(4, whole(at_y, every, c))
            for msg in (6, 8, 9):
                start(msg)
        elif number == 3:
            arrived(5, whole(at_d, low, c))
            arrived(6, whole(at_d, high, c))
            start(10)
        elif number == 4:
            for msg, dp in ((7, at), (8, at_x), (9, at_y), (10, at_d)):
                arrived(msg, whole(dp, every, 1 - c))
        elif number == 5:
            for msg, ends in enumerate(out):
                self.copy(msg, *ends).wait_send()


def turns(groups, *list_of):
    for stage, group in list_of:
        groups[group].stage(stage)


def matrix(ref, cols=slice(None)):
    value = ref[(slice(None),) * (len(ref.shape) - 1) + (cols,)]
    return value.reshape(-1, value.shape[-1])


class Reduce:
    def __init__(self, part, cols, write, bufs, direct, send, recv, group):
        self.part, self.cols, self.write, self.direct = part, cols, write, direct
        self.send, self.recv, self.group = send, recv, group
        self.half, self.diag, self.side, self.line = bufs

    copy = Gather.copy

    def add(self, target, *sources):
        if len(sources) == 2:
            target[...] = sources[0][...] + sources[1][...]
            return
        total = sources[0][...].astype(f32)
        for source in sources[1:]:
            total = total + source[...].astype(f32)
        target[...] = total.astype(target.dtype)

    def stage(self, number):
        y, x, z, c = place()
        at_x, at_y, at_d, at = y * 2 + 1 - x, (1 - y) * 2 + x, (1 - y) * 2 + 1 - x, y * 2 + x
        to_x, to_y, to_c = device(y, 1 - x, z, c), device(1 - y, x, z, c), device(y, x, z, 1 - c)
        to_d = device(1 - y, 1 - x, z, c)
        cols = pl.ds(*self.cols)
        half, diag, side, line = self.half, self.diag, self.side, self.line
        mine = lambda dp: self.part.at[dp, :, c, :, cols]
        low, high = pl.ds(0, 2), pl.ds(2, 2)
        blocks = (at_d, at_x, at_y, at)
        out = [(self.part.at[dp, :, 1 - c, :, cols], half.at[dp], to_c) for dp in blocks]
        if self.direct:
            out += [
                (half.at[at_d], diag, to_d),
                None,
                (half.at[at_x], side.at[0], to_x),
                (half.at[at_y], side.at[1], to_y),
            ]
        else:
            out += [
                (half.at[at_d, low], diag.at[0], to_x),
                (half.at[at_d, high], diag.at[1], to_y),
                (half.at[at_x], side.at[0], to_x),
                (half.at[at_y], side.at[1], to_y),
            ]
        out += [
            (half.at[at, (z + k) % 4], line.at[k - 1], device(y, x, (z + k) % 4, c))
            for k in (1, 2, 3)
        ]
        arrived = lambda msg: self.copy(msg, *out[msg][1:2] * 2, to_c).wait_recv()
        start = lambda msg: self.copy(msg, *out[msg]).start()

        def halve(msg):
            self.copy(msg, half.at[blocks[msg]], half.at[blocks[msg]], to_c).wait_recv()
            self.add(half.at[blocks[msg]], half.at[blocks[msg]], mine(blocks[msg]))

        if number == 0:
            for msg in range(4):
                start(msg)
        elif number == 1:
            halve(0)
            start(4)
            if not self.direct:
                start(5)
            halve(1)
            if self.direct:
                start(6)
            halve(2)
            if self.direct:
                start(7)
            halve(3)
        elif number == 2 and not self.direct:
            arrived(5)
            late = half.at[at_x, high]
            self.add(late, late, diag.at[1])
            start(6)
            arrived(4)
            late = half.at[at_y, low]
            self.add(late, late, diag.at[0])
            start(7)
        elif number == 3:
            own = half.at[at]
            if self.direct:
                arrived(4)
            arrived(6)
            arrived(7)
            self.add(own, own, side.at[0], side.at[1], *((diag,) if self.direct else ()))
            for k in (1, 2, 3):
                start(7 + k)
        elif number == 4:
            for k in (1, 2, 3):
                arrived(7 + k)
            total = half[at, z].astype(f32) + line[0].astype(f32)
            self.write(total + line[1].astype(f32) + line[2].astype(f32))
        elif number == 5:
            for msg, ends in enumerate(out):
                if ends is not None:
                    self.copy(msg, *ends).wait_send()


class Total:
    def __init__(self, value, out, bufs, send, recv, group):
        self.value, self.out, self.send, self.recv, self.group = value, out, send, recv, group
        self.line, self.plane, self.pair = bufs

    copy = Gather.copy

    def stage(self, number):
        y, x, z, c = place()
        at_x, at_y, at_d, at = y * 2 + 1 - x, (1 - y) * 2 + x, (1 - y) * 2 + 1 - x, y * 2 + x
        to_c = device(y, x, z, 1 - c)
        line, plane, pair = self.line, self.plane, self.pair
        out = [(line.at[z], device(y, x, (z + k) % 4, c)) for k in (1, 2, 3)] + [
            (plane.at[at], device(y, 1 - x, z, c)),
            (plane.at[at], device(1 - y, x, z, c)),
            (plane.at[at], device(1 - y, 1 - x, z, c)),
            (pair.at[c], to_c),
        ]
        came = [line.at[(z + 4 - k) % 4] for k in (1, 2, 3)]
        came += [plane.at[dp] for dp in (at_x, at_y, at_d)] + [pair.at[1 - c]]

        def start(msg):
            self.copy(msg, out[msg][0], out[msg][0], out[msg][1]).start()

        def arrived(msg):
            self.copy(msg, came[msg], came[msg], to_c).wait_recv()

        if number == 0:
            line[z] = self.value[...]
            for msg in (0, 1, 2):
                start(msg)
        elif number == 1:
            for msg in (0, 1, 2):
                arrived(msg)
            plane[at] = line[0] + line[1] + line[2] + line[3]
            for msg in (3, 4, 5):
                start(msg)
        elif number == 2:
            for msg in (3, 4, 5):
                arrived(msg)
            pair[c] = plane[0] + plane[1] + plane[2] + plane[3]
            start(6)
        elif number == 3:
            arrived(6)
            self.out[...] = pair[0] + pair[1]
        elif number == 5:
            for msg in range(7):
                self.copy(msg, out[msg][0], out[msg][0], out[msg][1]).wait_send()


GATHER_HOOKS = {
    "start": tuple((0, i) for i in range(8)),
    "first": ((1, 0), (1, 1), (1, 2), (2, 0), (2, 1), (3, 0), (3, 1), (4, 0)),
    0: ((2, 2), (1, 3), (1, 4), (4, 1)),
    1: ((3, 2), (1, 5), (2, 3), (4, 2)),
    2: ((2, 4), (3, 3), (1, 6)),
    3: ((2, 5), (3, 4), (1, 7)),
    "out": ((2, 6), (3, 5), (4, 3)),
    "up": ((4, 4), (4, 5)),
    "up1": ((2, 7), (3, 6)),
    "up2": (),
    "down": ((3, 7), (4, 6), (4, 7)) + tuple((5, i) for i in range(8)),
}


def gather_plan(width, hidden):
    half = hidden // 256 * 128
    plan = [(0, (0, width)), (1, (0, 384)), (1, (384, 3 * width - 384)), (2, (0, width))]
    return plan + [(which, cols) for which in (3, 4) for cols in ((0, half), (half, hidden - half))]


def forward_kernel(fast, *refs):
    refs = list(refs)
    take = lambda count: [refs.pop(0) for _ in range(count)]
    cameras, tokens, features, cotangent_in = take(4)
    shards = take(5)
    b_query, b_value, b_out, gain_first, shift_first = take(5)
    b_up, b_down, gain_second, shift_second, b_feat = take(5)
    stored = take(14)
    probs, dots, small = take(3)
    wholes_out = take(2) if fast else []
    kept = take(14)
    output, start_low, q_rows, k_rows, v_rows, dmix_high, dmix_low = kept[:7]
    grad_first, act, gin, normed_low, grad_branch, grad_att, mixed_low = kept[7:]
    first, work, mixed, inverse, q_cat, v_cat, k_cat, cotangent, sums, sums_up = take(10)
    prob_sem, load_sem, store_sem, step_sem = take(4)
    w_feat, w_qkv, w_out, w_up, w_down = take(5) if fast else shards
    width = tokens.shape[1]
    hidden = w_up.shape[-1]
    heads = width // HEAD
    pairs = heads // 2
    limit = 2 + CAM_LEN * cameras[0]
    if fast:
        turned_shard, send, recv, local = take(4)
        for pair in range(pairs):
            for i in range(3):
                at = i * width + pair * 128
                turned_shard[:, pair * 384 + i * 128 : pair * 384 + i * 128 + 128] = shards[1][
                    :, at : at + 128
                ]
        shards[1] = turned_shard
        wholes = (w_feat, w_qkv, w_out, w_up, w_down)
        gather = [
            Gather(shards[which], wholes[which], cols, send, recv, local, i)
            for i, (which, cols) in enumerate(gather_plan(width, hidden))
        ]
        greet()

    def hook(where):
        if fast:
            turns(gather, *GATHER_HOOKS[where])

    def hooks(step, where):
        if fast:
            for at_step, name in where:

                @pl.when(step == at_step)
                def _():
                    hook(name)

    def rows_of(step):
        return pl.ds(pl.multiple_of(step * STEP, 16), STEP)

    def row_ids(step):
        return step * STEP + lax.broadcasted_iota(jnp.int32, (STEP, 1), 0)

    def store(i, source=None, target=None):
        return pltpu.make_async_copy(
            kept[i] if source is None else source,
            stored[i] if target is None else target,
            store_sem.at[i],
        )

    def store_step(i, step):
        which = 0 if i == 8 else 1
        rows = rows_of(step)
        return pltpu.make_async_copy(
            kept[i].at[rows, :], stored[i].at[rows, :], step_sem.at[4 * which + step]
        )

    hook("start")
    loads = [
        pltpu.make_async_copy(
            source.at[pl.ds(0, ROWS), :], act.at[:, pl.ds(i * width, width)], load_sem.at[i]
        )
        for i, source in enumerate((features, tokens))
    ]
    loads.append(
        pltpu.make_async_copy(cotangent_in.at[pl.ds(0, ROWS), :], cotangent, load_sem.at[2])
    )
    for load in loads:
        load.start()
    hook("first")
    for load in loads:
        load.wait()

    def project(step, carry):
        rows = rows_of(step)
        ids = row_ids(step)
        camera = jnp.logical_and(ids >= 2, ids < limit)
        memory = dg(act[rows, :width], matrix(w_feat), 1, 0) + line_of(b_feat)
        start = act[rows, width : 2 * width].astype(f32) + jnp.where(camera, memory, 0.0)
        first[rows, :] = start
        start_low[rows, :] = start.astype(bf16)
        return carry

    lax.fori_loop(0, 4, project, 0)
    store(1).start()

    lane_valid = lax.broadcasted_iota(jnp.int32, (1, ROWS), 1) < limit

    def prob_copy(pair, side):
        source = act if side == 0 else gin
        at = pl.ds(pl.multiple_of(lax.rem(pair, 2) * 1280, 128), 1280)
        return pltpu.make_async_copy(
            source.at[:, at], probs.at[2 * pair + side], prob_sem.at[2 * lax.rem(pair, 2) + side]
        )

    def attend(pair, carry):
        lanes = pl.ds(pl.multiple_of(pair * 128, 128), 128)
        hooks(pair, [(i, i) for i in range(pairs)])

        @pl.when(pair >= 2)
        def _():
            prob_copy(pair - 2, 0).wait()
            prob_copy(pair - 2, 1).wait()

        w_pair = matrix(w_qkv, pl.ds(pl.multiple_of(pair * 384, 128), 384))
        for step in range(4):
            rows = slice(step * STEP, step * STEP + STEP)
            part = dg(start_low[rows, :], w_pair, 1, 0)
            q_rows[rows, lanes] = ((part[:, :128] + line_of(b_query, lanes)) * 0.125).astype(bf16)
            keys = part[:, 128:256]
            if step == 0:
                lead = keys[0:1]
            keys = jnp.where(row_ids(step) < limit, keys, lead).astype(bf16)
            k_rows[rows, lanes] = keys
            k_cat[rows, :128] = keys
            k_cat[rows, 128:] = keys
            v_rows[rows, lanes] = (part[:, 256:] + line_of(b_value, lanes)).astype(bf16)
        queries = q_rows[:, lanes].astype(f32).T * LOG2E
        high, low = split_low(queries)
        none = jnp.zeros((HEAD, ROWS), bf16)
        values = jnp.where(lane_valid, v_rows[:, lanes].astype(f32).T, 0.0).astype(bf16)
        ones = jnp.broadcast_to(jnp.where(lane_valid, 1.0, 0.0), (HEAD, ROWS)).astype(bf16)
        for side in range(2):
            own = slice(side * HEAD, side * HEAD + HEAD)
            other = slice((1 - side) * HEAD, (1 - side) * HEAD + HEAD)
            q_cat[side, own, :] = high[own]
            q_cat[side, other, :] = none
            q_cat[side, 128 + side * HEAD : 128 + side * HEAD + HEAD, :] = low[own]
            q_cat[side, 128 + (1 - side) * HEAD : 128 + (1 - side) * HEAD + HEAD, :] = none
            v_cat[side, :HEAD, :] = values[own]
            v_cat[side, HEAD:, :] = ones
        base = lax.rem(pair, 2) * 1280
        jobs = [(side, at, size) for side in range(2) for at, size in QBLOCKS]
        peak = {}

        def score(job, at_key, keys_here):
            side, at, size = jobs[job]
            here = slice(at_key, at_key + keys_here)
            scores = dg(k_cat[here, :], q_cat[side, :, at : at + size], 1, 0)
            work[job % 3 * 4 + at_key // STEP, :, :size] = scores
            high_here = jnp.max(scores, axis=0, keepdims=True)
            peak[job] = jnp.maximum(peak[job], high_here) if job in peak else high_here

        def weigh(job, at_key, keys_here):
            side, at, size = jobs[job]
            slot = act if side == 0 else gin
            here = slice(at_key, at_key + keys_here)
            slot[here, pl.ds(pl.multiple_of(base + at, 128), size)] = jnp.exp2(
                work[job % 3 * 4 + at_key // STEP, :, :size] - peak[job]
            ).astype(bf16)

        def mix(job):
            side, at, size = jobs[job]
            slot = act if side == 0 else gin
            weight = slot[:, pl.ds(pl.multiple_of(base + at, 128), size)]
            summed = dg(v_cat[side], weight, 1, 0)
            inv = 1.0 / summed[HEAD : HEAD + 1]
            mixed[pl.ds(pl.multiple_of(pair * 128 + side * HEAD, 8), HEAD), at : at + size] = (
                summed[:HEAD] * inv
            )
            inverse[2 * pair + side, :, at : at + size] = inv

        parts = chunks(ROWS, STEP)
        for job in (0, 1):
            for part in parts:
                score(job, *part)
        for job in range(len(jobs)):
            for part in parts:
                if job + 2 < len(jobs):
                    score(job + 2, *part)
                weigh(job, *part)
            if job >= 2:
                mix(job - 2)
            if job == len(QBLOCKS) - 1:
                prob_copy(pair, 0).start()
        mix(len(jobs) - 2)
        mix(len(jobs) - 1)
        prob_copy(pair, 1).start()
        return carry

    lax.fori_loop(0, pairs, attend, 0)
    for pair in (pairs - 2, pairs - 1):
        for side in range(2):
            prob_copy(pair, side).wait()

    for i in (2, 3, 4):
        store(i).start()
    hook("out")
    mixed_low[...] = mixed[...].astype(bf16)
    store(13).start()
    for at, size in chunks(width, 256):
        cols = slice(at, at + size)
        first[:, cols] += dg(mixed_low[...], matrix(w_out, cols), 0, 0) + line_of(b_out, cols)
    sums[...] = jnp.zeros_like(sums)
    sums_up[...] = jnp.zeros_like(sums_up)
    cuts = chunks(hidden, 512)
    hook("up")

    def widen(step, carry):
        hooks(step, [(1, "up1"), (2, "up2")])
        rows = rows_of(step)
        unit_first, scale_first = norm_parts(first[rows, :])
        low = (unit_first * line_of(gain_first) + line_of(shift_first)).astype(bf16)
        normed_low[rows, :] = low
        for at, size in cuts:
            cols = slice(at, at + size)
            inner = dg(low, matrix(w_up, cols), 1, 0) + line_of(b_up, cols)
            square = inner * inner
            half = 0.5 + 0.5 * jnp.tanh(inner * (GELU_C + (GELU_C * GELU_A) * square))
            value = inner * half
            act[rows, cols] = value.astype(bf16)
            slope = half + value * (1.0 - half) * (2 * GELU_C + (6 * GELU_C * GELU_A) * square)
            gin[rows, cols] = slope.astype(bf16)
        store_step(8, step).start()
        return carry

    lax.fori_loop(0, 4, widen, 0)
    store(10).start()
    hook("down")

    def feed(step, carry):
        rows = rows_of(step)
        valid = row_ids(step) < limit
        unit_first, scale_first = norm_parts(first[rows, :])
        normed = unit_first * line_of(gain_first) + line_of(shift_first)
        branch = dg(act[rows, :], matrix(w_down), 1, 1) + line_of(b_down)
        unit_second, scale_second = norm_parts(normed + branch)
        final = unit_second * line_of(gain_second) + line_of(shift_second)
        output[rows, :] = jnp.where(valid, final, 0.0).astype(bf16)
        grad = jnp.where(valid, cotangent[rows, :].astype(f32), 0.0)
        sums[0] += fold(grad * unit_second)
        sums[1] += fold(grad)
        grad_second = norm_back(grad, unit_second, scale_second, line_of(gain_second))
        low_branch = grad_second.astype(bf16)
        grad_branch[rows, :] = low_branch
        sums[2] += fold(low_branch.astype(f32))
        for at, size in cuts:
            cols = slice(at, at + size)
            low_inner = (
                dg(low_branch, matrix(w_down, cols), 1, 0) * gin[rows, cols].astype(f32)
            ).astype(bf16)
            gin[rows, cols] = low_inner
            sums_up[:, cols] += fold(low_inner.astype(f32))
        store_step(9, step).start()
        grad_normed = grad_second + dg(gin[rows, :], matrix(w_up), 1, 1)
        sums[3] += fold(grad_normed * unit_first)
        sums[4] += fold(grad_normed)
        back = norm_back(grad_normed, unit_first, scale_first, line_of(gain_first))
        grad_first[rows, :] = back
        low_att = back.astype(bf16)
        grad_att[rows, :] = low_att
        sums[5] += fold(low_att.astype(f32))
        return carry

    lax.fori_loop(0, 4, feed, 0)
    output[ROWS:, :] = jnp.zeros((SLOTS - ROWS, width), bf16)
    for i in (0, 7, 11, 12):
        store(i).start()
    small[...] = jnp.zeros_like(small)
    for i in range(6):
        small[i : i + 1, :] = jnp.sum(sums[i], axis=0, keepdims=True)
    for i, (at, size) in enumerate(chunks(hidden, width)):
        small[6 + i : 7 + i, :size] = jnp.sum(sums_up[:, at : at + size], axis=0, keepdims=True)
    if fast:
        whole_copies = [
            store(14 + i, source, target)
            for i, (source, target) in enumerate(zip((w_feat, w_qkv), wholes_out))
        ]
        for copy in whole_copies:
            copy.start()

    for at, size in QBLOCKS:
        cols = slice(at, at + size)
        grad_mixed = dg(matrix(w_out), grad_att[cols, :], 1, 1).astype(bf16).astype(f32)
        scaled = grad_mixed.reshape(heads, HEAD, size) * inverse[:, :, cols]
        dots[:, :, cols] = jnp.sum(
            scaled * mixed[:, cols].reshape(heads, HEAD, size), axis=1, keepdims=True
        )
        high, low = split_low(scaled.reshape(width, size))
        dmix_high[:, cols] = high
        dmix_low[:, cols] = low
    for i in (5, 6):
        store(i).start()
    for step in range(4):
        store_step(8, step).wait()
        store_step(9, step).wait()
    for i in (0, 1, 2, 3, 4, 5, 6, 7, 10, 11, 12, 13):
        store(i).wait()
    if fast:
        for copy in whole_copies:
            copy.wait()


def shaped(shape, dtype):
    return jax.ShapeDtypeStruct(shape, dtype)


def forward_call(fast, cameras, tokens, features, cotangent, weights, biases):
    width = tokens.shape[1]
    hidden = weights[3].shape[1]
    heads = width // HEAD
    token_rows = shaped((ROWS, width), bf16)
    kept = (shaped((SLOTS, width), bf16),) + (token_rows,) * 4 + (shaped((width, ROWS), bf16),) * 2
    kept += (shaped((ROWS, width), f32),) + (shaped((ROWS, hidden), bf16),) * 2
    kept += (token_rows,) * 3 + (shaped((width, ROWS), bf16),)
    wholes = [(4, 4, 2) + w.shape for w in weights]
    outs = kept + (
        shaped((heads, ROWS, 1280), bf16),
        shaped((heads, 1, ROWS), f32),
        shaped((-(-(6 + -(-hidden // width)) // 8) * 8, width), f32),
    )
    if fast:
        outs += tuple(shaped(whole, bf16) for whole in wholes[:2])
    vmem = pl.BlockSpec(memory_space=pltpu.VMEM)
    hbm = pl.BlockSpec(memory_space=pl.ANY)
    groups = len(gather_plan(width, hidden))
    return pl.pallas_call(
        functools.partial(forward_kernel, fast),
        out_shape=outs,
        in_specs=[pl.BlockSpec(memory_space=pltpu.SMEM)] + [hbm] * 3 + [vmem] * 15,
        out_specs=tuple(vmem if i in (15, 16) else hbm for i in range(len(outs))),
        scratch_shapes=[pltpu.VMEM(k.shape, k.dtype) for k in kept]
        + [
            pltpu.VMEM((ROWS, width), f32),
            pltpu.VMEM((12, STEP, 256), f32),
            pltpu.VMEM((width, ROWS), f32),
            pltpu.VMEM((heads, 1, ROWS), f32),
            pltpu.VMEM((2, 256, ROWS), bf16),
            pltpu.VMEM((2, 128, ROWS), bf16),
            pltpu.VMEM((ROWS, 256), bf16),
            pltpu.VMEM((ROWS, width), bf16),
            pltpu.VMEM((6, 8, width), f32),
            pltpu.VMEM((8, hidden), f32),
            pltpu.SemaphoreType.DMA((4,)),
            pltpu.SemaphoreType.DMA((3,)),
            pltpu.SemaphoreType.DMA((16,)),
            pltpu.SemaphoreType.DMA((8,)),
        ]
        + fast
        * (
            [pltpu.VMEM(whole, bf16) for whole in wholes]
            + [
                pltpu.VMEM(weights[1].shape, bf16),
                pltpu.SemaphoreType.DMA((groups, MESSAGES)),
                pltpu.SemaphoreType.DMA((groups, MESSAGES)),
                pltpu.SemaphoreType.DMA((groups,)),
            ]
        ),
        compiler_params=pltpu.CompilerParams(
            vmem_limit_bytes=62 * MIB,
            collective_id=0 if fast else None,
            has_side_effects=fast,
        ),
        name="layer_forward",
    )(cameras, tokens, features, cotangent, *weights, *biases)


TAIL = 1280


def reduce_plan(width, hidden):
    cuts = ((0, TAIL), (TAIL, TAIL), (2 * TAIL, hidden - 2 * TAIL))
    plan = [(which, cols, False) for which in (0, 1) for cols in cuts]
    plan += [(2, (0, width), False)]
    last = 3 * width - 384
    plan += [(3, (0, last - 384), False), (3, (last - 384, 384), False), (3, (last, 384), True)]
    return plan + [(4, (0, width), True)]


REDUCE_HOOKS = {
    "start": ((0, 11),),
    "out": ((0, 6),),
    "tails": ((0, 5), (0, 2), (1, 6)),
    "up0": ((0, 3), (1, 5), (1, 11)),
    "up1": ((0, 4), (1, 2)),
    "down0": ((0, 0), (1, 3), (2, 6)),
    "down1": ((0, 1), (1, 4), (2, 5)),
    (0, 0): ((2, 2), (2, 11)),
    (0, 1): ((1, 0),),
    (0, 2): ((2, 3), (1, 1), (3, 11)),
    (1, 0): ((2, 4), (3, 6)),
    (1, 1): ((3, 5),),
    (1, 2): ((2, 0), (3, 2)),
    (2, 0): ((0, 7), (2, 1)),
    (2, 1): ((1, 7), (3, 3)),
    (2, 2): ((3, 4),),
    (3, 0): ((0, 8), (2, 7)),
    (3, 1): ((1, 8), (3, 0)),
    (3, 2): ((3, 1),),
    "pairs": ((0, 9), (2, 8), (3, 7)),
    "rows0": ((1, 9),),
    "rows1": (),
    "rows2": ((4, 6), (4, 5), (4, 2), (3, 8), (5, 6), (5, 5), (5, 2), (5, 11)),
    "feat": ((0, 10), (0, 12), (4, 3), (5, 3)),
    "half": ((1, 10), (1, 12), (3, 9), (4, 4), (4, 0), (4, 1), (5, 4), (5, 0), (5, 1)),
    "end": ((2, 12), (4, 7), (4, 8), (5, 7), (5, 8), (3, 10), (4, 9), (5, 9))
    + ((3, 12), (5, 12), (4, 10), (5, 10)),
}


def put(target, cols, value):
    if len(target.shape) == 2:
        target[:, cols] = value
    else:
        target[:, :, :, :, cols] = value.reshape(target.shape[:4] + value.shape[1:])


def backward_kernel(fast, *refs):
    refs = list(refs)
    take = lambda count: [refs.pop(0) for _ in range(count)]
    cameras, features, probs, dots, act, gin, *wgrad_in = take(10)
    inputs = take(9)
    small = take(1)[0] if fast else None
    grad_tokens, grad_features = take(2)
    if fast:
        summed, (total, total_late) = take(5), take(2)
        parts_of = take(5)
        small_late = take(1)[0]
    else:
        parts_of = take(5)
        small_late = take(1)[0]
    loaded = take(9)
    q_rows, k_rows, v_rows, dmix_high, dmix_low, start_low, grad_first, w_qkv, w_feat = loaded
    weights, grad_scores, joined, d_cat, d_rows, v_cat, k_turned, blank, sums = take(9)
    prob_sem, load_sem, wgrad_sem, out_sem = take(4)
    width = q_rows.shape[1]
    hidden = act.shape[1]
    heads = width // HEAD
    pairs = heads // 2
    limit = 2 + CAM_LEN * cameras[0]
    if fast:
        send, recv, local = refs[-3:]
        plan = reduce_plan(width, hidden)

        def writer(which, cols):
            def write(value):
                if which == 3:
                    for here in range(0, cols[1], 128):
                        pair, i = (cols[0] + here) // 384, (cols[0] + here) // 128 % 3
                        at = i * width + pair * 128
                        summed[3][:, at : at + 128] = value[:, here : here + 128]
                else:
                    summed[which][:, cols[0] : cols[0] + cols[1]] = value

            return write

        groups = [
            Reduce(parts_of[which], cols, writer(which, cols), take(4), direct, send, recv, i)
            for i, (which, cols, direct) in enumerate(plan)
        ]
        groups.append(Total(small, total, take(3), send, recv, len(plan)))
        groups.append(Total(small_late, total_late, take(3), send, recv, len(plan) + 1))

    def hook(where):
        if fast:
            turns(groups, *REDUCE_HOOKS[where])

    def pair_hook(pair, spot):
        if fast:
            for at_pair in range(pairs):

                @pl.when(pair == at_pair)
                def _():
                    hook((at_pair, spot))

    mixed_low, normed_low = d_cat, joined.at[:, pl.ds(0, width)]
    grad_branch, grad_att = joined.at[:, pl.ds(width, width)], joined.at[:, pl.ds(2 * width, width)]
    tail = pl.ds(2 * TAIL, hidden - 2 * TAIL)
    act_tail = weights.at[2, :, pl.ds(0, hidden - 2 * TAIL)]
    gin_tail = weights.at[2, :, pl.ds(hidden - 2 * TAIL, hidden - 2 * TAIL)]
    ends = [
        (wgrad_in[3], mixed_low),
        (wgrad_in[2], grad_att),
        (wgrad_in[0], normed_low),
        (gin.at[:, tail], gin_tail),
        (wgrad_in[1], grad_branch),
        (act.at[:, tail], act_tail),
        (gin.at[:, pl.ds(0, TAIL)], weights.at[3]),
        (gin.at[:, pl.ds(TAIL, TAIL)], grad_scores.at[0]),
        (act.at[:, pl.ds(0, TAIL)], weights.at[0]),
        (act.at[:, pl.ds(TAIL, TAIL)], weights.at[1]),
    ]
    fetch = [
        pltpu.make_async_copy(source, target, wgrad_sem.at[i])
        for i, (source, target) in enumerate(ends)
    ]
    loads = [
        pltpu.make_async_copy(source, target, load_sem.at[i])
        for i, (source, target) in enumerate(zip(inputs, loaded))
    ]
    for copy in fetch + loads:
        copy.start()
    if fast:
        greet()
    hook("start")

    def prob_copy(pair, side):
        slot = 2 * lax.rem(pair + 1, 2) + side
        return pltpu.make_async_copy(
            probs.at[2 * pair + side], weights.at[slot], prob_sem.at[slot]
        )

    def weight_grad(which, left, right, at, size):
        def part(turn, carry):
            cut = pl.multiple_of(turn * 512, 512)
            grad = dg(left[...], right[:, pl.ds(cut, 512)], 0, 0).astype(bf16)
            put(parts_of[which], pl.ds(at + cut, 512), grad)
            return carry

        lax.fori_loop(0, size // 512, part, 0)
        if size % 512:
            cut, wide = size // 512 * 512, size % 512
            grad = dg(left[...], right[:, cut : cut + wide], 0, 0).astype(bf16)
            put(parts_of[which], pl.ds(at + cut, wide), grad)

    fetch[0].wait()
    fetch[1].wait()
    grad = dg(mixed_low[...].reshape(width, ROWS), grad_att[...], 1, 0).astype(bf16)
    put(parts_of[2], pl.ds(0, width), grad)
    hook("out")
    fetch[2].wait()
    fetch[3].wait()
    weight_grad(1, normed_low, gin_tail, 2 * TAIL, hidden - 2 * TAIL)
    fetch[4].wait()
    fetch[5].wait()
    weight_grad(0, grad_branch, act_tail, 2 * TAIL, hidden - 2 * TAIL)
    hook("tails")
    fetch[6].wait()
    weight_grad(1, normed_low, weights.at[3], 0, TAIL)
    hook("up0")
    for side in range(2):
        prob_copy(0, side).start()
    fetch[7].wait()
    weight_grad(1, normed_low, grad_scores.at[0], TAIL, TAIL)
    hook("up1")
    fetch[8].wait()
    weight_grad(0, grad_branch, weights.at[0], 0, TAIL)
    hook("down0")
    fetch[9].wait()
    weight_grad(0, grad_branch, weights.at[1], TAIL, TAIL)
    hook("down1")
    for load in loads:
        load.wait()

    sums[...] = jnp.zeros_like(sums)
    lane_valid = lax.broadcasted_iota(jnp.int32, (1, ROWS), 1) < limit
    row_valid = lax.broadcasted_iota(jnp.int32, (ROWS, 1), 0) < limit
    none = jnp.zeros((HEAD, ROWS), bf16)

    def attend_back(pair, carry):
        lanes = pl.ds(pl.multiple_of(pair * 128, 128), 128)

        @pl.when(pair + 1 < pairs)
        def _():
            prob_copy(pair + 1, 0).start()
            prob_copy(pair + 1, 1).start()

        pair_hook(pair, 0)
        high = dmix_high[lanes, :]
        low = dmix_low[lanes, :]
        for side in range(2):
            own = slice(side * HEAD, side * HEAD + HEAD)
            mine, its = side * HEAD, (1 - side) * HEAD
            d_cat[side, mine : mine + HEAD, :] = high[own]
            d_cat[side, its : its + HEAD, :] = none
            d_cat[side, 128 + mine : 128 + mine + HEAD, :] = low[own]
            d_cat[side, 128 + its : 128 + its + HEAD, :] = none
        d_rows[:, :128] = high.astype(f32).T.astype(bf16)
        d_rows[:, 128:] = low.astype(f32).T.astype(bf16)
        values = v_rows[:, lanes]
        v_cat[:, :128] = values
        v_cat[:, 128:] = values
        k_turned[...] = jnp.where(lane_valid, k_rows[:, lanes].astype(f32).T, 0.0).astype(bf16)
        base = 2 * lax.rem(pair + 1, 2)
        jobs = [(side, at, size) for side in range(2) for at, size in QBLOCKS]
        parts = chunks(ROWS, STEP)
        turned = {0: [], 1: []}
        wide = {}

        def slope(job):
            side, at, size = jobs[job]
            offset = dots[2 * pair + side, :, at : at + size]
            for at_key, keys_here in parts:
                here = slice(at_key, at_key + keys_here)
                grad = dg(v_cat[here, :], d_cat[side, :, at : at + size], 1, 0) - offset
                weight = weights[base + side, here, at : at + size].astype(f32)
                grad_scores[side, here, at : at + size] = (weight * grad).astype(bf16)

        def queries(job):
            side, at, size = jobs[job]
            turned[side].append(
                dg(k_turned[...], grad_scores[side, :, at : at + size], 1, 0)[
                    side * HEAD : side * HEAD + HEAD
                ]
            )

        def spread(side, part):
            here = slice(part[0], part[0] + part[1])
            value = dg(weights[base + side, here, :ROWS], d_rows[...], 1, 0)
            value = value[:, :128] + value[:, 128:]
            key = dg(grad_scores[side, here, :ROWS], q_rows[:, lanes], 1, 0)
            wide[side, part] = (value, key)

        for side in range(2):
            prob_copy(pair, side).wait()
        for job in range(len(jobs)):
            if job == len(QBLOCKS):
                pair_hook(pair, 1)
            slope(job)
            if job >= 1:
                queries(job - 1)
            if job > len(QBLOCKS):
                side_job = job - len(QBLOCKS) - 1
                if side_job < len(parts):
                    spread(0, parts[side_job])
        queries(len(jobs) - 1)
        pair_hook(pair, 2)
        first_lane = lax.broadcasted_iota(jnp.int32, (STEP, 128), 1) < HEAD
        spot = lambda i: pl.ds(pl.multiple_of(pair * 384 + i * 128, 128), 128)
        for part in parts:
            spread(1, part)
            here = slice(part[0], part[0] + part[1])
            keep = row_valid[here]
            for which, i in ((0, 2), (1, 1)):
                value = jnp.where(first_lane, wide[0, part][which], wide[1, part][which])
                joined[here, spot(i)] = jnp.where(keep, value, 0.0).astype(bf16)
        query = jnp.concatenate(
            [jnp.concatenate(turned[0], axis=1), jnp.concatenate(turned[1], axis=1)], axis=0
        )
        joined[:, spot(0)] = (query.astype(bf16).astype(f32).T * 0.125).astype(bf16)
        at = pl.ds(pl.multiple_of(pair * 384, 128), 384)
        put(parts_of[3], at, dg(start_low[...], joined[:, at], 0, 0).astype(bf16))
        return carry

    lax.fori_loop(0, pairs, attend_back, 0)
    feats = weights.at[2, :, pl.ds(0, width)]
    tokens_out = weights.at[2, :, pl.ds(width, width)]
    features_out = weights.at[3, :, pl.ds(0, width)]
    grad_memory = grad_scores.at[0, :, pl.ds(0, width)]
    load = pltpu.make_async_copy(features.at[pl.ds(0, ROWS), :], feats, out_sem.at[0])
    load.start()
    blank[...] = jnp.zeros_like(blank)
    body, rest = pl.ds(0, ROWS), pl.ds(ROWS, SLOTS - ROWS)
    stores = [
        pltpu.make_async_copy(source, target, out_sem.at[1 + i])
        for i, (source, target) in enumerate(
            (
                (blank, grad_tokens.at[rest, :]),
                (blank, grad_features.at[rest, :]),
                (tokens_out, grad_tokens.at[body, :]),
                (features_out, grad_features.at[body, :]),
            )
        )
    ]
    stores[0].start()
    stores[1].start()
    hook("pairs")

    def project_back(step, carry):
        rows = pl.ds(pl.multiple_of(step * STEP, 16), STEP)
        ids = step * STEP + lax.broadcasted_iota(jnp.int32, (STEP, 1), 0)
        camera = jnp.logical_and(ids >= 2, ids < limit)
        part = joined[rows, :]
        for pair in range(pairs):
            lanes = slice(pair * 128, pair * 128 + 128)
            sums[0, :, lanes] += fold(part[:, pair * 384 : pair * 384 + 128].astype(f32))
            sums[1, :, lanes] += fold(part[:, pair * 384 + 256 : pair * 384 + 384].astype(f32))
        grad_start = grad_first[rows, :] + dg(part, w_qkv[...], 1, 1)
        tokens_out[rows, :] = grad_start.astype(bf16)
        low = jnp.where(camera, grad_start, 0.0).astype(bf16)
        grad_memory[rows, :] = low
        sums[2] += fold(low.astype(f32))
        if fast:
            for at_step in (0, 1, 2):

                @pl.when(step == at_step)
                def _():
                    hook(f"rows{at_step}")

        return carry

    lax.fori_loop(0, 4, project_back, 0)
    stores[2].start()
    load.wait()
    put(parts_of[4], pl.ds(0, width), dg(feats[...], grad_memory[...], 0, 0).astype(bf16))
    small_late[...] = jnp.zeros_like(small_late)
    for i in range(3):
        small_late[i : i + 1, :] = jnp.sum(sums[i], axis=0, keepdims=True)
    hook("feat")
    hook("half")

    def spread_back(step, carry):
        rows = pl.ds(pl.multiple_of(step * STEP, 16), STEP)
        features_out[rows, :] = dg(grad_memory[rows, :], w_feat[...], 1, 1).astype(bf16)
        return carry

    lax.fori_loop(0, 4, spread_back, 0)
    stores[3].start()
    hook("end")
    for copy in stores:
        copy.wait()


def backward_call(fast, cameras, features, saved, small):
    probs, dots, act, gin, normed_low, grad_branch, grad_att, mixed_low, *inputs = saved
    width, hidden = features.shape[1], act.shape[1]
    vmem = pl.BlockSpec(memory_space=pltpu.VMEM)
    hbm = pl.BlockSpec(memory_space=pl.ANY)
    rows = width // 32
    columns = (hidden, hidden, width, 3 * width, width)
    late = (8, width)
    outs = (shaped((SLOTS, width), bf16),) * 2
    scratch = []
    reduce_scratch = []
    args = [cameras, features, probs, dots, act, gin, normed_low, grad_branch, grad_att]
    args += [mixed_low.reshape(2, width // 2, ROWS), *inputs]
    specs = [pl.BlockSpec(memory_space=pltpu.SMEM), hbm, hbm, vmem] + [hbm] * 15
    if fast:
        outs += tuple(shaped((rows, n), f32) for n in columns)
        outs += (shaped(small.shape, f32), shaped(late, f32))
        args += [small]
        specs += [vmem]
        scratch += [pltpu.VMEM((4, 4, 2, rows, n), bf16) for n in columns] + [pltpu.VMEM(late, f32)]
        plan = reduce_plan(width, hidden)
        for which, (_, size), direct in plan:
            reduce_scratch += [
                pltpu.VMEM((4, 4, rows, size), bf16),
                pltpu.VMEM((4, rows, size) if direct else (2, 2, rows, size), bf16),
                pltpu.VMEM((2, 4, rows, size), bf16),
                pltpu.VMEM((3, rows, size), bf16),
            ]
        for shape in (small.shape, late):
            reduce_scratch += [pltpu.VMEM((count,) + shape, f32) for count in (4, 4, 2)]
        reduce_scratch += [
            pltpu.SemaphoreType.DMA((len(plan) + 2, MESSAGES)),
            pltpu.SemaphoreType.DMA((len(plan) + 2, MESSAGES)),
            pltpu.SemaphoreType.DMA((len(plan),)),
        ]
    else:
        outs += tuple(shaped((width, n), bf16) for n in columns) + (shaped(late, f32),)
    scratch += [pltpu.VMEM(a.shape, a.dtype) for a in inputs]
    scratch += [
        pltpu.VMEM((4, ROWS, 1280), bf16),
        pltpu.VMEM((2, ROWS, 1280), bf16),
        pltpu.VMEM((ROWS, 3 * width), bf16),
        pltpu.VMEM((2, 256, ROWS), bf16),
        pltpu.VMEM((ROWS, 256), bf16),
        pltpu.VMEM((ROWS, 256), bf16),
        pltpu.VMEM((128, ROWS), bf16),
        pltpu.VMEM((SLOTS - ROWS, width), bf16),
        pltpu.VMEM((3, 8, width), f32),
        pltpu.SemaphoreType.DMA((4,)),
        pltpu.SemaphoreType.DMA((9,)),
        pltpu.SemaphoreType.DMA((10,)),
        pltpu.SemaphoreType.DMA((5,)),
    ]
    return pl.pallas_call(
        functools.partial(backward_kernel, fast),
        out_shape=outs,
        in_specs=specs,
        out_specs=(hbm,) * 2 + (vmem,) * (len(outs) - 2),
        scratch_shapes=scratch + reduce_scratch,
        compiler_params=pltpu.CompilerParams(
            vmem_limit_bytes=62 * MIB,
            collective_id=1 if fast else None,
            has_side_effects=fast,
        ),
        name="layer_backward",
    )(*args)


def finish_kernel(*refs):
    refs = list(refs)
    take = lambda count: [refs.pop(0) for _ in range(count)]
    sources, (small, late), targets = take(8), take(2), take(8)
    vectors, held, (sem_in, sem_out, sem_row) = take(10), take(8), refs
    loads = [
        pltpu.make_async_copy(source, hold, sem_in.at[i])
        for i, (source, hold) in enumerate(zip(sources, held))
    ]
    copies = [
        pltpu.make_async_copy(hold, target, sem_out.at[i])
        for i, (hold, target) in enumerate(zip(held, targets))
    ]
    for load in loads:
        load.start()
    places = ((late, 0), (late, 1), (small, 5), (small, 3), (small, 4), None)
    places += ((small, 2), (small, 0), (small, 1), (late, 2))
    rows = [(*spot, vector) for vector, spot in zip(vectors, places) if spot is not None]
    pieces = [(ref.at[row], vector) for ref, row, vector in rows]
    pieces += [
        (small.at[6 + i, pl.ds(0, size)], vectors[5].at[pl.ds(at, size)])
        for i, (at, size) in enumerate(chunks(vectors[5].shape[0], small.shape[1]))
    ]
    moves = [
        pltpu.make_async_copy(source, target, sem_row.at[i])
        for i, (source, target) in enumerate(pieces)
    ]
    for move in moves:
        move.start()
    for load, copy in zip(loads, copies):
        load.wait()
        copy.start()
    for copy in moves + copies:
        copy.wait()


def finish_call(large, small, late, hidden):
    width = small.shape[1]
    vmem = pl.BlockSpec(memory_space=pltpu.VMEM)
    hbm = pl.BlockSpec(memory_space=pl.ANY)
    return pl.pallas_call(
        finish_kernel,
        out_shape=tuple(shaped(a.shape, a.dtype) for a in large)
        + tuple(shaped((hidden if i == 5 else width,), f32) for i in range(10)),
        in_specs=[hbm] * 8 + [vmem] * 2,
        out_specs=(hbm,) * 18,
        scratch_shapes=[pltpu.VMEM(a.shape, a.dtype) for a in large]
        + [pltpu.SemaphoreType.DMA((count,)) for count in (8, 8, 9 - (-hidden // width))],
        name="place_outputs",
    )(*large, small, late)


AXES = ("dp", "fsdp")


def on_device(
    fast,
    tokens,
    features,
    cameras,
    cotangent,
    w_qkv,
    w_out,
    w_up,
    w_down,
    w_feat,
    *biases,
):
    width = tokens.shape[1]
    hidden = w_up.shape[1]
    pairs = width // 128
    weights = (w_feat, w_qkv, w_out, w_up, w_down)
    if not fast:
        weights = [lax.all_gather(w, AXES, axis=0, tiled=True) for w in weights]
        by_pair = weights[1].reshape(width, 3, pairs, 128).transpose(0, 2, 1, 3)
        weights[1] = by_pair.reshape(width, 3 * width)
    output, *kept = forward_call(fast, cameras, tokens, features, cotangent, weights, biases)
    start_low, q_rows, k_rows, v_rows, dmix_high, dmix_low, grad_first, *kept = kept
    act, gin, normed_low, grad_branch, grad_att, mixed_low, probs, dots, small, *wholes = kept
    if fast:
        weights = [whole.reshape(width, -1) for whole in wholes]
    saved = (probs, dots, act, gin, normed_low, grad_branch, grad_att, mixed_low)
    saved += (q_rows, k_rows, v_rows, dmix_high, dmix_low, start_low, grad_first)
    saved += (weights[1], weights[0])
    grad_tokens, grad_features, *grads = backward_call(fast, cameras, features, saved, small)
    if fast:
        *grads, small, late = grads
    else:
        *grads, late = grads
        by_pair = grads[3].reshape(width, pairs, 3, 128).transpose(0, 2, 1, 3)
        grads[3] = by_pair.reshape(width, 3 * width)
        grads = [
            lax.psum_scatter(
                lax.optimization_barrier(grad.astype(f32)), AXES, scatter_dimension=0, tiled=True
            )
            for grad in grads
        ]
        small, late = lax.psum((small, late), AXES)
    grad_down, grad_up, grad_out, grad_qkv, grad_feat = grads
    large = (output, grad_tokens, grad_features, grad_qkv, grad_out, grad_up, grad_down, grad_feat)
    return finish_call(large, small, late, hidden)


def solution(mesh):
    split = P(AXES, None)
    fast = mesh.shape["dp"] == 4 and mesh.shape["fsdp"] == 8
    return jax.shard_map(
        functools.partial(on_device, fast),
        mesh=mesh,
        in_specs=(split, split, P(AXES), split) + (split,) * 5 + (P(),) * 10,
        out_specs=(split,) * 8 + (P(),) * 10,
        check_vma=False,
    )
```
